32 devices in a mesh: dp: 4 (over y, x), row: 4 (over z), col: 2 (over core).
Axes of the slice: x: 2, y: 2, z: 4, core: 2. Of those that a mesh axis runs over, the one named last changes fastest.
Arguments:
- tokens_in: bfloat16 [16384, 1024], P(('dp', 'col'), 'row'), may hold values from -6 to 6
- prefix_len: int32 [16], P(('dp', 'row')), may hold values from 102 to 512
- first_gain: float32 [1024], P('row'), may hold values from 0.5 to 1.5
- first_shift: float32 [1024], P('row'), may hold values from -1.75 to 1.75
- second_gain: float32 [1024], P('row'), may hold values from 0.5 to 1.5
- second_shift: float32 [1024], P('row'), may hold values from -1.75 to 1.75
- qkv_weight: float32 [1024, 3072], P(('row', 'dp'), 'col'), may hold values from -0.1875 to 0.1875
- qkv_bias: float32 [3072], P(('col', 'dp')), may hold values from -1.75 to 1.75
- up_weight: float32 [1024, 4096], P(('row', 'dp'), 'col'), may hold values from -0.1875 to 0.1875
- up_bias: float32 [4096], P(('col', 'dp')), may hold values from -1.75 to 1.75
- dense_weight: float32 [1024, 1024], P(('col', 'dp'), 'row'), may hold values from -3 to 3
- dense_bias: float32 [1024], P(('row', 'dp')), may hold values from -1.75 to 1.75
- down_weight: float32 [4096, 1024], P(('col', 'dp'), 'row'), may hold values from -0.09375 to 0.09375
- down_bias: float32 [1024], P(('row', 'dp')), may hold values from -1.75 to 1.75
- cotangent: bfloat16 [16384, 1024], P(('dp', 'col'), 'row'), may hold values from -6 to 6
Outputs:
- layer_out: bfloat16 [16384, 1024], P(('dp', 'col'), 'row')
- grad_tokens: bfloat16 [16384, 1024], P(('dp', 'col'), 'row')
- grad_qkv_weight: float32 [1024, 3072], P(('row', 'dp'), 'col')
- grad_qkv_bias: float32 [3072], P(('col', 'dp'))
- grad_up_weight: float32 [1024, 4096], P(('row', 'dp'), 'col')
- grad_up_bias: float32 [4096], P(('col', 'dp'))
- grad_dense_weight: float32 [1024, 1024], P(('col', 'dp'), 'row')
- grad_dense_bias: float32 [1024], P(('row', 'dp'))
- grad_down_weight: float32 [4096, 1024], P(('col', 'dp'), 'row')
- grad_down_bias: float32 [1024], P(('row', 'dp'))
- grad_first_gain: float32 [1024], P('row')
- grad_first_shift: float32 [1024], P('row')
- grad_second_gain: float32 [1024], P('row')
- grad_second_shift: float32 [1024], P('row')
The draws below stay inside these ranges and needn't reach their ends.
All inputs are finite; a program needn't handle non-finite values.
Results may differ from the reference program's by a relative error of at most 0.012.
The reference program's roundings to bfloat16 on the way count: a program that leaves them out, or rounds other values in their place, can miss the bound.
Values may be sent and summed in bfloat16 or wider, within the bound.
A program may use at most 320 MiB of HBM per device.

```python
import math
import jax
import jax.numpy as jnp
from jax import lax

D = 1024
HEADS = 16
HD = 64
ROT = 16
FF = 4096
SEQ_LEN = 1024
SEQ_GROUP = 1
SEQS = 16
TOKENS = 16384


def touch_ends(drawn, own_key, low, high):
    longest = drawn.shape.index(max(drawn.shape))
    spots = []
    for shift in (0, 1):
        where = [jax.random.randint(jax.random.fold_in(own_key, axis), (), 0, length) for axis, length in enumerate(drawn.shape)]
        where[longest] = (where[longest] + shift) % drawn.shape[longest]
        spots.append(tuple(where))
    return drawn.at[spots[0]].set(low).at[spots[1]].set(high)


def block_scale(key, extent, split, smallest, largest):
    gain = 1.0
    for dim, parts in split:
        heights = jax.random.uniform(jax.random.fold_in(jax.random.fold_in(key, 6), dim), (parts,), jnp.float32, smallest / len(split), largest / len(split))
        gain = gain * jnp.repeat(jnp.exp(heights), extent[dim] // parts).reshape((-1,) + (1,) * (len(extent) - 1 - dim))
    return gain


def noise(rng, dims, width, limit, split=(), kind=jnp.bfloat16):
    drawn = width * jax.random.normal(rng, dims, jnp.float32)
    if split:
        drawn = drawn * block_scale(rng, dims, split, -0.22, 0.18)
    return jnp.clip(drawn, -limit, limit).astype(kind)


def setup_inputs(seed: int = 0) -> dict:
    arg_keys = jax.random.split(jax.random.key(seed), 16)
    tokens_in = noise(arg_keys[0], (TOKENS, D), 1.0, 6.0, ((0, 8), (1, 4)))
    prefix_len = touch_ends(jax.random.randint(arg_keys[1], (SEQS,), SEQ_LEN // 10, SEQ_LEN // 2 + 1), jax.random.fold_in(arg_keys[1], 1), SEQ_LEN // 10, (SEQ_LEN // 2 + 1) - 1).astype(jnp.int32)
    first_gain = jnp.clip(1.0 + 0.1 * jax.random.normal(arg_keys[2], (D,), jnp.float32), 0.5, 1.5)
    first_shift = noise(arg_keys[3], (D,), 0.3, 1.75, ((0, 4),), jnp.float32)
    second_gain = jnp.clip(1.0 + 0.1 * jax.random.normal(arg_keys[4], (D,), jnp.float32), 0.5, 1.5)
    second_shift = noise(arg_keys[5], (D,), 0.3, 1.75, ((0, 4),), jnp.float32)
    qkv_weight = noise(arg_keys[6], (D, 3 * D), D ** -0.5, 0.1875, ((0, 16), (1, 2)), jnp.float32)
    qkv_bias = noise(arg_keys[7], (3 * D,), 0.3, 1.75, ((0, 8),), jnp.float32)
    up_weight = noise(arg_keys[8], (D, FF), D ** -0.5, 0.1875, ((0, 16), (1, 2)), jnp.float32)
    up_bias = noise(arg_keys[9], (FF,), 0.3, 1.75, ((0, 8),), jnp.float32)
    dense_weight = noise(arg_keys[10], (D, D), (max(D // 256, 1)) ** -0.5, 3.0, ((0, 8), (1, 4)), jnp.float32)
    dense_bias = noise(arg_keys[11], (D,), 0.3, 1.75, ((0, 16),), jnp.float32)
    down_weight = noise(arg_keys[12], (FF, D), FF ** -0.5, 0.09375, ((0, 8), (1, 4)), jnp.float32)
    down_bias = noise(arg_keys[13], (D,), 0.3, 1.75, ((0, 16),), jnp.float32)
    cotangent = noise(arg_keys[14], (TOKENS, D), 1.0, 6.0, ((0, 8), (1, 4)))
    return dict(tokens_in=tokens_in, prefix_len=prefix_len, first_gain=first_gain, first_shift=first_shift, second_gain=second_gain, second_shift=second_shift, qkv_weight=qkv_weight, qkv_bias=qkv_bias, up_weight=up_weight, up_bias=up_bias, dense_weight=dense_weight, dense_bias=dense_bias, down_weight=down_weight, down_bias=down_bias, cotangent=cotangent)


EPS = 1e-05
NEGATIVE = -1e+30
HIGH = lax.Precision.HIGHEST

@jax.custom_vjp
def low(v):
    return lax.optimization_barrier(v.astype(jnp.bfloat16)).astype(jnp.float32)

@jax.custom_vjp
def low_back(v):
    return v

def low_keep(v):
    return (low(v), None)

def low_pass(kept, grad):
    return (grad,)

def back_keep(v):
    return (v, None)

def back_low(kept, grad):
    return (low(grad),)
low.defvjp(low_keep, low_pass)
low_back.defvjp(back_keep, back_low)

def product(left_side, right_side):
    return jnp.dot(left_side, right_side, precision=HIGH, preferred_element_type=jnp.float32)

def angles_table():
    half_rot = ROT // 2
    places = jnp.arange(SEQ_LEN, dtype=jnp.float32)
    rates = jnp.exp(jnp.arange(half_rot, dtype=jnp.float32) * (-2.0 * math.log(10000.0) / ROT))
    turned = places[:, None] * rates[None, :]
    return (jnp.cos(turned), jnp.sin(turned))

def rotate(paired, cos_table, sin_table):
    half_rot = cos_table.shape[1]
    cos_wide = cos_table[None, :, None, None, :]
    sin_wide = sin_table[None, :, None, None, :]
    first_half = paired[..., :half_rot]
    second_half = paired[..., half_rot:2 * half_rot]
    return jnp.concatenate([first_half * cos_wide - second_half * sin_wide, second_half * cos_wide + first_half * sin_wide, paired[..., 2 * half_rot:]], axis=-1)

def attend(inputs):
    queries, key_rows, value_rows, prefix_end = inputs
    scores = jnp.einsum('qhd,khd->hqk', queries, key_rows, precision=HIGH) * HD ** (-0.5)
    scores = low_back(scores)
    places = jnp.arange(SEQ_LEN)
    visible = (places[None, :] <= places[:, None]) | (places[None, :] < prefix_end)
    masked = jnp.where(visible[None], scores, NEGATIVE)
    highest = lax.optimization_barrier(jnp.max(masked, axis=-1, keepdims=True))
    exponent = jnp.exp(masked - highest)
    weights = low(exponent / lax.optimization_barrier(jnp.sum(exponent, axis=-1, keepdims=True)))
    return jnp.einsum('hqk,khd->qhd', weights, value_rows, precision=HIGH)

def layer(tokens, prefixes, params):
    first_gain, first_shift, second_gain, second_shift, qkv_weight, qkv_bias, up_weight, up_bias, dense_weight, dense_bias, down_weight, down_bias = params
    center = lax.optimization_barrier(jnp.mean(tokens, axis=-1, keepdims=True))
    spread = lax.optimization_barrier(jnp.mean(tokens * tokens, axis=-1, keepdims=True)) - center * center
    normed = (tokens - center) * lax.rsqrt(spread + EPS)
    first_in = low(normed * first_gain + first_shift)
    second_in = low(normed * second_gain + second_shift)
    mixed = low_back(product(first_in, low(qkv_weight)) + low(qkv_bias))
    mixed = mixed.reshape(SEQ_GROUP, SEQ_LEN, HEADS, 3, HD)
    cos_table, sin_table = angles_table()
    turned = low(rotate(mixed[:, :, :, :2, :], cos_table, sin_table))
    value_rows = low(mixed[:, :, :, 2, :])
    outputs = lax.map(jax.checkpoint(attend), (turned[:, :, :, 0, :], turned[:, :, :, 1, :], value_rows, prefixes))
    attended = low_back(low(outputs.reshape(SEQ_GROUP * SEQ_LEN, D)))
    hidden_pre = low_back(product(second_in, low(up_weight)) + low(up_bias))
    hidden = low(jax.nn.gelu(hidden_pre, approximate=False))
    return tokens + product(attended, low(dense_weight)) + low(dense_bias) + product(hidden, low(down_weight)) + low(down_bias)

def reference(tokens_in, prefix_len, first_gain, first_shift, second_gain, second_shift, qkv_weight, qkv_bias, up_weight, up_bias, dense_weight, dense_bias, down_weight, down_bias, cotangent):
    params = tuple((entry.astype(jnp.float32) for entry in (first_gain, first_shift, second_gain, second_shift, qkv_weight, qkv_bias, up_weight, up_bias, dense_weight, dense_bias, down_weight, down_bias)))
    groups = SEQS // SEQ_GROUP
    token_blocks = tokens_in.astype(jnp.float32).reshape(groups, SEQ_GROUP * SEQ_LEN, D)
    grad_blocks = cotangent.astype(jnp.float32).reshape(groups, SEQ_GROUP * SEQ_LEN, D)
    prefix_blocks = prefix_len.reshape(groups, SEQ_GROUP)

    def step(totals, inputs):
        block, prefixes, upstream = inputs
        result, backward = jax.vjp(lambda tokens, weights: layer(tokens, prefixes, weights), block, params)
        grad_block, grad_params = backward(upstream)
        totals = jax.tree.map(lambda earlier, later: earlier + later, totals, grad_params)
        return (totals, (result.astype(jnp.bfloat16), grad_block.astype(jnp.bfloat16)))
    zeros = jax.tree.map(jnp.zeros_like, params)
    totals, (results, grad_parts) = lax.scan(step, zeros, (token_blocks, prefix_blocks, grad_blocks))
    return (results.reshape(TOKENS, D), grad_parts.reshape(TOKENS, D), totals[4], totals[5], totals[6], totals[7], totals[8], totals[9], totals[10], totals[11], totals[0], totals[1], totals[2], totals[3])
```

```python
import functools
import math

import jax
import jax.numpy as jnp
from jax import lax
from jax.experimental import pallas as pl
from jax.experimental.pallas import tpu as pltpu
from jax.sharding import PartitionSpec as P

D = 1024
HD = 64
ROT = 16
FF = 4096
SEQ_LEN = 1024
EPS = 1e-05
NEGATIVE = -1e30
ROWS = 4
DPS = 4
MESH = pl.DeviceIdType.MESH
BF = jnp.bfloat16
F32 = jnp.float32


def places():
    dp, row, col = lax.axis_index("dp"), lax.axis_index("row"), lax.axis_index("col")
    across = dp + 1 - 2 * lax.rem(dp, 2)
    along = lax.rem(dp + 2, 4)
    return dp, row, col, across, along


def line_order(row):
    far = row // 2
    side = row - 3 * far + 2 * far * (3 - row)
    side = lax.rem(jnp.abs(side), 2)
    at = lambda place: far * 3 + (1 - 2 * far) * place
    return side, at


def greet(targets):
    barrier = pltpu.get_barrier_semaphore()
    for target in targets:
        pl.semaphore_signal(barrier, inc=1, device_id=target, device_id_type=MESH)
    pl.semaphore_wait(barrier, len(targets))


def peers_of(dp, row, col, cols):
    group = []
    for step in range(1, ROWS * cols):
        flat = lax.rem(row * cols + col + step, ROWS * cols)
        group.append((dp, flat // cols, lax.rem(flat, cols)))
    for step in range(1, DPS):
        for other in range(ROWS):
            group.append((lax.rem(dp + step, DPS), lax.rem(row + other, ROWS), col))
    return group


def remote(src, dst, send, recv, target):
    return pltpu.make_async_remote_copy(
        src_ref=src, dst_ref=dst, send_sem=send, recv_sem=recv, device_id=target, device_id_type=MESH
    )


N_W = 4


def slot(name, ref, row, dp, half=None):
    if name < 2:
        return ref.at[row, dp] if half is None else ref.at[row, dp, half]
    columns = pl.ds(pl.multiple_of(row * 256, 256), 256)
    return ref.at[dp, :, :, columns] if half is None else ref.at[dp, half, :, columns]


def gather_kernel(cols, *refs):
    (tok_ref, cot_ref, small_ref, wq_ref, wu_ref, wd_ref, wp_ref) = refs[:7]
    (x_ref, c_ref, smalls_ref, gq_ref, gu_ref, gd_ref, gp_ref) = refs[7:14]
    (z_send, z_recv, s1_send, s1_recv, s2_send, s2_recv, t_send, t_recv, a_send, a_recv, m_send, m_recv, l_sem) = refs[14:]
    own = (wq_ref, wu_ref, wd_ref, wp_ref)
    full = (gq_ref, gu_ref, gd_ref, gp_ref)
    dp, row, col, across, along = places()
    side, at = line_order(row)
    order = [row, at(1 - side), at(2), at(3)]
    middle = side == 1
    tok_col = tok_ref.shape[0]
    part = SEQ_LEN // cols
    chunk = min(tok_col, SEQ_LEN)
    n_seq = tok_col // chunk
    n_part = chunk // part

    greet(peers_of(dp, row, col, cols))

    waits = []

    def token_copy(kind, j, i):
        src_ref, dst_ref = ((tok_ref, x_ref), (cot_ref, c_ref))[kind]
        start = col * tok_col + j * chunk
        to_row = start // SEQ_LEN
        piece = lax.rem(start, SEQ_LEN) // part + i
        src = src_ref.at[pl.ds(j * chunk + i * part, part), :]
        dst = dst_ref.at[pl.ds(pl.multiple_of(piece * part, part), part), pl.ds(pl.multiple_of(row * 256, 256), 256)]
        sends, recvs = t_send.at[kind, j * n_part + i], t_recv.at[kind, row]
        is_here = jnp.logical_and(to_row == row, piece == col)
        far = remote(src, dst, sends, recvs, (dp, to_row, piece))
        near = pltpu.make_async_copy(src, dst, recvs)
        return is_here, far, near

    def token_start(kind):
        for j in range(n_seq):
            for i in range(n_part):
                is_here, far, near = token_copy(kind, j, i)
                pl.when(jnp.logical_not(is_here))(far.start)
                pl.when(is_here)(near.start)

    def part_rows(piece):
        return pl.ds(pl.multiple_of(piece * part, part), part)

    def spread_copy(kind, step):
        dst_ref = (x_ref, c_ref)[kind]
        mine = dst_ref.at[part_rows(col), :]
        to_col = lax.rem(col + step, cols)
        return remote(mine, mine, a_send.at[kind, step - 1], a_recv.at[kind, step - 1], (dp, row, to_col))

    def token_spread(kind):
        dst_ref = (x_ref, c_ref)[kind]
        for other in range(ROWS):
            block = dst_ref.at[part_rows(col), pl.ds(other * 256, 256)]
            pltpu.make_async_copy(block, block, t_recv.at[kind, other]).wait()
        for step in range(1, cols):
            spread_copy(kind, step).start()

    def token_finish(kind):
        dst_ref = (x_ref, c_ref)[kind]
        for j in range(n_seq):
            for i in range(n_part):
                is_here, far, near = token_copy(kind, j, i)
                pl.when(jnp.logical_not(is_here))(far.wait_send)
        for step in range(1, cols):
            copy = spread_copy(kind, step)
            copy.wait_send()
            from_col = lax.rem(col + cols - step, cols)
            theirs = dst_ref.at[part_rows(from_col), :]
            pltpu.make_async_copy(theirs, theirs, a_recv.at[kind, step - 1]).wait()

    me = row * DPS + dp

    def small_copy(step):
        flat = lax.rem(me + step, ROWS * DPS)
        return remote(
            small_ref, smalls_ref.at[me], m_send.at[step - 1], m_recv.at[step - 1], (lax.rem(flat, DPS), flat // DPS, col)
        )

    def source(w, k, half=None):
        if k == 0:
            return own[w] if half is None else own[w].at[half]
        return slot(w, full[w], order[k], dp, half)

    def line_copies(w, k):
        src = source(w, k)
        dst = slot(w, full[w], order[k], dp)
        recv = z_recv.at[w, order[k]]
        if k == 0:
            return [
                (None, remote(src, dst, z_send.at[w, 0], recv, (dp, at(1 - side), col))),
                (middle, remote(src, dst, z_send.at[w, 1], recv, (dp, at(2), col))),
            ]
        onward = at(2) if k == 1 else at(0)
        return [(middle, remote(src, dst, z_send.at[w, k + 1], recv, (dp, onward, col)))]

    def first_copies(w, k):
        out = []
        for half, target in ((0, across), (1, along)):
            out.append(
                remote(source(w, k, half), slot(w, full[w], order[k], dp, half), s1_send.at[w, k, half],
                       s1_recv.at[w, k, half], (target, row, col))
            )
        return out

    def second_copies(w, k, which):
        out = []
        for half, target, other in ((0, along, across), (1, across, along)):
            if which == 0:
                src, owner = source(w, k, half), dp
            else:
                src, owner = slot(w, full[w], order[k], other, half), other
            out.append(
                remote(src, slot(w, full[w], order[k], owner, half), s2_send.at[w, k, which, half],
                       s2_recv.at[w, k, which, half], (target, row, col))
            )
        return out

    def arrived(w, k):
        if k > 0:
            block = slot(w, full[w], order[k], dp)
            pltpu.make_async_copy(block, block, z_recv.at[w, order[k]]).wait()
        for cond, copy in line_copies(w, k):
            if cond is None:
                copy.start()
            else:
                pl.when(cond)(copy.start)
        for copy in first_copies(w, k) + second_copies(w, k, 0):
            copy.start()

    def passed(w, k):
        for copy in first_copies(w, k):
            copy.wait_recv()
        for copy in second_copies(w, k, 1):
            copy.start()

    def finished(w, k):
        for which in range(2):
            for copy in second_copies(w, k, which):
                copy.wait_recv()

    def drained(w, k):
        for cond, copy in line_copies(w, k):
            if cond is None:
                copy.wait_send()
            else:
                pl.when(cond)(copy.wait_send)
        for copy in first_copies(w, k) + second_copies(w, k, 0) + second_copies(w, k, 1):
            copy.wait_send()

    def home(w):
        return pltpu.make_async_copy(own[w], slot(w, full[w], row, dp), l_sem.at[w])

    small_home = pltpu.make_async_copy(small_ref, smalls_ref.at[me], l_sem.at[N_W])
    small_home.start()
    for step in range(1, ROWS * DPS):
        small_copy(step).start()
    token_start(0)
    for w in range(N_W):
        arrived(w, 0)
        home(w).start()
    token_start(1)
    token_spread(0)
    for w in range(N_W):
        passed(w, 0)
        for k in range(1, 4):
            arrived(w, k)
        for k in range(1, 4):
            passed(w, k)
    token_spread(1)
    for w in range(N_W):
        for k in range(4):
            finished(w, k)
            drained(w, k)
        home(w).wait()
    small_home.wait()
    for step in range(1, ROWS * DPS):
        small_copy(step).wait()
    for kind in range(2):
        token_finish(kind)


def gather(tokens_in, cotangent, small, weights, cols):
    wq, wu, wd, wp = weights
    any_spec = pl.BlockSpec(memory_space=pl.ANY)
    shapes = [
        jax.ShapeDtypeStruct((SEQ_LEN, D), BF),
        jax.ShapeDtypeStruct((SEQ_LEN, D), BF),
        jax.ShapeDtypeStruct((ROWS * DPS,) + small.shape, F32),
        jax.ShapeDtypeStruct((ROWS, DPS) + wq.shape, BF),
        jax.ShapeDtypeStruct((ROWS, DPS) + wu.shape, BF),
        jax.ShapeDtypeStruct((DPS,) + wd.shape[:2] + (D,), BF),
        jax.ShapeDtypeStruct((DPS,) + wp.shape[:2] + (D,), BF),
    ]
    tok_col = tokens_in.shape[0]
    pieces = tok_col // (SEQ_LEN // cols)
    dma = pltpu.SemaphoreType.DMA
    return pl.pallas_call(
        functools.partial(gather_kernel, cols),
        out_shape=shapes,
        in_specs=[any_spec] * 7,
        out_specs=[any_spec] * 7,
        scratch_shapes=[
            dma((N_W, 5)), dma((N_W, 4)), dma((N_W, 4, 2)), dma((N_W, 4, 2)), dma((N_W, 4, 2, 2)), dma((N_W, 4, 2, 2)),
            dma((2, pieces)), dma((2, 4)), dma((2, cols - 1)), dma((2, cols - 1)),
            dma((ROWS * DPS - 1,)), dma((ROWS * DPS - 1,)), dma((N_W + 1,)),
        ],
        compiler_params=pltpu.CompilerParams(collective_id=0, has_side_effects=True),
    )(tokens_in, cotangent, small, wq, wu, wd, wp)


def lead(name, y, x, half):
    return (slice(None), y, x, half) if name < 2 else (y, x, half)


def add_into(dst, src):
    shape = dst.shape
    outer, height = shape[:-2], shape[-2]
    step = 32
    per = height // step
    total = math.prod(outer) * per

    def body(i, carry):
        index, rest = [], i // per
        for size in reversed(outer):
            index.append(lax.rem(rest, size))
            rest = rest // size
        where = tuple(reversed(index)) + (pl.ds(pl.multiple_of(lax.rem(i, per) * step, step), step),)
        dst[where] = (dst[where].astype(F32) + src[where].astype(F32)).astype(BF)
        return carry

    lax.fori_loop(0, total, body, 0)


def scatter_kernel(cols, heights, *refs):
    g_refs = refs[:4]
    out_refs = refs[4:8]
    mine = (refs[8:10], refs[10:12], refs[12:14], refs[14:16])
    got1 = (refs[16:18], refs[18:20], refs[20:22], refs[22:24])
    got2 = (refs[24:26], refs[26:28], refs[28:30], refs[30:32])
    got3 = (refs[32:34], refs[34:36], refs[36:38], refs[38:40])
    l_sem, s1_send, s1_recv, s2_send, s2_recv, s3_send, s3_recv = refs[40:]
    dp, row, col, across, along = places()
    x, y = lax.rem(dp, 2), dp // 2

    greet(peers_of(dp, row, col, cols))

    def first(w, half):
        if half == 0:
            src, target = g_refs[w].at[lead(w, 1 - y, slice(None), 0)], along
        else:
            src, target = g_refs[w].at[lead(w, slice(None), 1 - x, 1)], across
        return remote(src, got1[w][half], s1_send.at[w, half], s1_recv.at[w, half], (target, row, col))

    def fetch(w, half):
        src = g_refs[w].at[lead(w, y, slice(None), 0)] if half == 0 else g_refs[w].at[lead(w, slice(None), x, 1)]
        return pltpu.make_async_copy(src, mine[w][half], l_sem.at[w, half])

    def keep(w, half, other):
        which = (x if half == 0 else y)
        which = 1 - which if other else which
        return mine[w][half].at[:, which] if w < 2 else mine[w][half].at[which]

    def second(w, half):
        target = across if half == 0 else along
        return remote(keep(w, half, True), got2[w][half], s2_send.at[w, half], s2_recv.at[w, half], (target, row, col))

    def block(w, half, r):
        kept = keep(w, half, False)
        if w < 2:
            return kept.at[r]
        return kept.at[:, pl.ds(pl.multiple_of(r * 256, 256), 256)]

    def third(w, half, step):
        to_row = lax.rem(row + step, ROWS)
        return remote(
            block(w, half, to_row), got3[w][half].at[step - 1], s3_send.at[w, half, step - 1],
            s3_recv.at[w, half, step - 1], (dp, to_row, col)
        )

    def total(w, half):
        height = out_refs[w].shape[1]
        step = 32

        def body(i, carry):
            rows = pl.ds(pl.multiple_of(i * step, step), step)
            value = block(w, half, row)[rows, :].astype(F32)
            for s in range(3):
                value = value + got3[w][half][s, rows, :].astype(F32)
            out_refs[w][half, rows, :] = value
            return carry

        lax.fori_loop(0, height // step, body, 0)

    sequence = [(w, half) for w in (0, 1, 2, 3) for half in range(2)]
    for w, half in sequence:
        first(w, half).start()
        fetch(w, half).start()

    def stage_two(w, half):
        fetch(w, half).wait()
        first(w, half).wait_recv()
        add_into(mine[w][half], got1[w][half])
        second(w, half).start()

    def stage_three(w, half):
        second(w, half).wait()
        add_into(keep(w, half, False), got2[w][half])
        for step in range(1, ROWS):
            third(w, half, step).start()

    def stage_four(w, half):
        for step in range(1, ROWS):
            third(w, half, step).wait()
        total(w, half)

    lag2, lag3 = 2, 4
    n = len(sequence)
    for i in range(n + lag3):
        if i < n:
            stage_two(*sequence[i])
        if 0 <= i - lag2 < n:
            stage_three(*sequence[i - lag2])
        if 0 <= i - lag3 < n:
            stage_four(*sequence[i - lag3])
    for w, half in sequence:
        first(w, half).wait_send()


def scatter(grads, cols):
    any_spec = pl.BlockSpec(memory_space=pl.ANY)
    vmem = pl.BlockSpec(memory_space=pltpu.VMEM)
    dma = pltpu.SemaphoreType.DMA
    outs, mine, got1, got2, got3 = [], [], [], [], []
    for w, grad in enumerate(grads):
        h, n = grad.shape[-2:]
        if w < 2:
            outs.append(jax.ShapeDtypeStruct((2, h, n), F32))
            mine += [pltpu.VMEM((ROWS, 2, h, n), BF)] * 2
            got1 += [pltpu.VMEM((ROWS, 2, h, n), BF)] * 2
            got2 += [pltpu.VMEM((ROWS, h, n), BF)] * 2
            got3 += [pltpu.VMEM((3, h, n), BF)] * 2
        else:
            outs.append(jax.ShapeDtypeStruct((2, h, 256), F32))
            mine += [pltpu.VMEM((2, h, n), BF)] * 2
            got1 += [pltpu.VMEM((2, h, n), BF)] * 2
            got2 += [pltpu.VMEM((h, n), BF)] * 2
            got3 += [pltpu.VMEM((3, h, 256), BF)] * 2
    return pl.pallas_call(
        functools.partial(scatter_kernel, cols, None),
        out_shape=outs,
        in_specs=[any_spec] * 4,
        out_specs=[vmem] * 4,
        scratch_shapes=mine + got1 + got2 + got3 + [
            dma((N_W, 2)), dma((N_W, 2)), dma((N_W, 2)), dma((N_W, 2)), dma((N_W, 2)), dma((N_W, 2, 3)), dma((N_W, 2, 3)),
        ],
        compiler_params=pltpu.CompilerParams(collective_id=1, has_side_effects=True, vmem_limit_bytes=48 << 20),
    )(*grads)


def angles_table():
    half_rot = ROT // 2
    places_ = jnp.arange(SEQ_LEN, dtype=F32)
    rates = jnp.exp(jnp.arange(half_rot, dtype=F32) * (-2.0 * math.log(10000.0) / ROT))
    turned = places_[:, None] * rates[None, :]
    return (jnp.cos(turned), jnp.sin(turned))


def rotate(paired, cos_table, sin_table):
    half_rot = cos_table.shape[1]
    cos_wide = cos_table[:, None, None, :]
    sin_wide = sin_table[:, None, None, :]
    first_half = paired[..., :half_rot]
    second_half = paired[..., half_rot : 2 * half_rot]
    return jnp.concatenate(
        [
            first_half * cos_wide - second_half * sin_wide,
            second_half * cos_wide + first_half * sin_wide,
            paired[..., 2 * half_rot :],
        ],
        axis=-1,
    )


def score_block(queries, key_rows, prefix_end):
    scores = jnp.einsum("qhd,khd->hqk", queries, key_rows, preferred_element_type=F32) * HD ** (-0.5)
    at = jnp.arange(SEQ_LEN)
    visible = (at[None, :] <= at[:, None]) | (at[None, :] < prefix_end)
    return jnp.where(visible[None], scores, NEGATIVE)


def attend_forward(queries, key_rows, value_rows, prefix_end):
    scores = score_block(queries, key_rows, prefix_end)
    highest = jnp.max(scores, axis=-1, keepdims=True)
    exp_total = jnp.sum(jnp.exp(scores - highest), axis=-1, keepdims=True)
    log_sum = highest + jnp.log(exp_total)
    weights = jnp.exp(scores - log_sum).astype(BF)
    outputs = jnp.einsum("hqk,khd->qhd", weights, value_rows, preferred_element_type=F32)
    return (outputs, log_sum[..., 0])


def attend_backward(queries, key_rows, value_rows, prefix_end, log_sum, upstream):
    scores = score_block(queries, key_rows, prefix_end)
    chances = jnp.exp(scores - log_sum[..., None])
    grad_values = jnp.einsum("hqk,qhd->khd", chances.astype(BF), upstream, preferred_element_type=F32)
    grad_chances = jnp.einsum("qhd,khd->hqk", upstream, value_rows, preferred_element_type=F32)
    inner_sum = jnp.sum(chances * grad_chances, axis=-1, keepdims=True)
    grad_scores = (chances * (grad_chances - inner_sum)).astype(BF)
    grad_queries = jnp.einsum("hqk,khd->qhd", grad_scores, key_rows, preferred_element_type=F32) * HD ** (-0.5)
    grad_keys = jnp.einsum("hqk,qhd->khd", grad_scores, queries, preferred_element_type=F32) * HD ** (-0.5)
    return (grad_queries, grad_keys, grad_values)


def contract_rows(left_side, right_side):
    return lax.dot_general(left_side, right_side, (((0,), (0,)), ((), ())), preferred_element_type=F32)


def contract_cols(left_side, right_side):
    return lax.dot_general(left_side, right_side, (((1,), (1,)), ((), ())), preferred_element_type=F32)


def shards(cols, tokens_in, prefix_len, first_gain, first_shift, second_gain, second_shift, qkv_weight, qkv_bias,
           up_weight, up_bias, dense_weight, dense_bias, down_weight, down_bias, cotangent):
    tok_col = tokens_in.shape[0]
    n_q, n_u = qkv_weight.shape[1], up_weight.shape[1]
    h_d, h_p = dense_weight.shape[0], down_weight.shape[0]
    heads = n_q // (3 * HD)
    width_att = heads * HD

    weights = (
        qkv_weight.astype(BF).reshape(2, 32, n_q),
        up_weight.astype(BF).reshape(2, 32, n_u),
        dense_weight.astype(BF).reshape(2, h_d // 2, 256),
        down_weight.astype(BF).reshape(2, h_p // 2, 256),
    )
    pieces = (first_gain, first_shift, second_gain, second_shift, dense_bias, down_bias, qkv_bias, up_bias)
    small = jnp.concatenate(pieces)
    size = -(-small.shape[0] // 1024) * 1024
    small = jnp.pad(small, (0, size - small.shape[0])).reshape(size // 128, 128)
    own_x, own_cot, smalls, wq, wu, wd, wp = gather(tokens_in, cotangent, small, weights, cols)
    wq = wq.reshape(D, n_q)
    wu = wu.reshape(D, n_u)
    wd = wd.reshape(width_att, D)
    wp = wp.reshape(h_p * DPS, D)
    flat = smalls.reshape(ROWS, DPS, size)
    gains = [flat[:, 0, 256 * i : 256 * (i + 1)].reshape(D) for i in range(4)]
    out_bias = [flat[:, :, 1024 + 64 * i : 1088 + 64 * i].reshape(D).astype(BF).astype(F32) for i in range(2)]
    n_qb, n_ub = qkv_bias.shape[0], up_bias.shape[0]
    q_bias = flat[0, :, 1152 : 1152 + n_qb].reshape(n_q).astype(BF).astype(F32)
    u_bias = flat[0, :, 1152 + n_qb : 1152 + n_qb + n_ub].reshape(n_u).astype(BF).astype(F32)

    wide = own_x.astype(F32)
    center = jnp.mean(wide, axis=1, keepdims=True)
    spread = jnp.mean(wide * wide, axis=1, keepdims=True) - center * center
    scale_inv = lax.rsqrt(spread + EPS)
    normed = (wide - center) * scale_inv
    first_in = (normed * gains[0] + gains[1]).astype(BF)
    second_in = (normed * gains[2] + gains[3]).astype(BF)

    mixed = jnp.dot(first_in, wq, preferred_element_type=F32) + q_bias
    hidden_pre = jnp.dot(second_in, wu, preferred_element_type=F32) + u_bias
    mixed_heads = mixed.reshape(SEQ_LEN, heads, 3, HD)
    cos_table, sin_table = angles_table()
    turned = rotate(mixed_heads[:, :, :2, :], cos_table, sin_table).astype(BF)
    queries, key_rows = turned[:, :, 0, :], turned[:, :, 1, :]
    value_rows = mixed_heads[:, :, 2, :].astype(BF)
    outputs, log_sums = attend_forward(queries, key_rows, value_rows, prefix_len[0])
    attended = outputs.reshape(SEQ_LEN, width_att).astype(BF)
    hidden = jax.nn.gelu(hidden_pre, approximate=False).astype(BF)
    branch = jnp.dot(attended, wd, preferred_element_type=F32) + jnp.dot(hidden, wp, preferred_element_type=F32)

    upstream = contract_cols(own_cot, wd).astype(BF).reshape(SEQ_LEN, heads, HD)
    grad_hidden = contract_cols(own_cot, wp)
    ignored, gelu_back = jax.vjp(functools.partial(jax.nn.gelu, approximate=False), hidden_pre)
    grad_hidden_pre = gelu_back(grad_hidden)[0].astype(BF)
    grad_q, grad_k, grad_v = attend_backward(queries, key_rows, value_rows, prefix_len[0], log_sums, upstream)
    ignored, rotate_back = jax.vjp(lambda paired: rotate(paired, cos_table, sin_table), mixed_heads[:, :, :2, :])
    grad_pair = rotate_back(jnp.stack([grad_q, grad_k], axis=2))[0]
    grad_mixed = jnp.concatenate([grad_pair, grad_v[:, :, None, :]], axis=2).reshape(SEQ_LEN, n_q).astype(BF)

    grads = (
        contract_rows(first_in, grad_mixed).astype(BF).reshape(ROWS, 2, 2, 2, 32, n_q),
        contract_rows(second_in, grad_hidden_pre).astype(BF).reshape(ROWS, 2, 2, 2, 32, n_u),
        contract_rows(attended, own_cot).astype(BF).reshape(2, 2, 2, h_d // 2, D),
        contract_rows(hidden, own_cot).astype(BF).reshape(2, 2, 2, h_p // 2, D),
    )
    out_q, out_u, out_d, out_p = scatter(grads, cols)

    grad_first = contract_cols(grad_mixed, wq)
    grad_second = contract_cols(grad_hidden_pre, wu)
    combined = grad_first * gains[0] + grad_second * gains[2]
    part = SEQ_LEN // cols

    def to_owner(partial):
        moved = lax.all_to_all(partial, "row", split_axis=1, concat_axis=0, tiled=True)
        return lax.psum_scatter(moved, "col", scatter_dimension=0, tiled=True)

    branch_sum = to_owner(branch)
    combined = lax.psum(combined, "col")
    gain_rows = jnp.stack([
        jnp.sum(normed * grad_first, axis=0), jnp.sum(grad_first, axis=0),
        jnp.sum(normed * grad_second, axis=0), jnp.sum(grad_second, axis=0),
    ])
    line_total = jnp.mean(combined, axis=1, keepdims=True)
    cross_total = jnp.mean(combined * normed, axis=1, keepdims=True)
    grad_tokens = (own_cot.astype(F32) + scale_inv * (combined - line_total - normed * cross_total)).astype(BF)
    grad_tokens = lax.all_to_all(grad_tokens, "row", split_axis=1, concat_axis=0, tiled=True)
    grad_tokens = lax.dynamic_slice_in_dim(grad_tokens, lax.axis_index("col") * tok_col, tok_col, 0)
    row = lax.axis_index("row")
    here = [lax.dynamic_slice_in_dim(b, row * 256, 256, 0) for b in out_bias]
    layer_out = (tokens_in.astype(F32) + branch_sum + here[0] + here[1]).astype(BF)

    gain_sums = lax.psum_scatter(
        lax.psum(gain_rows, ("dp", "col")), "row", scatter_dimension=1, tiled=True
    )
    out_b = lax.psum_scatter(jnp.sum(own_cot.astype(F32), axis=0), ("row", "dp"), scatter_dimension=0, tiled=True)
    q_b = lax.psum_scatter(
        lax.psum(jnp.sum(grad_mixed.astype(F32), axis=0), "row"), "dp", scatter_dimension=0, tiled=True
    )
    u_b = lax.psum_scatter(
        lax.psum(jnp.sum(grad_hidden_pre.astype(F32), axis=0), "row"), "dp", scatter_dimension=0, tiled=True
    )
    return (
        layer_out, grad_tokens, out_q.reshape(64, n_q), q_b, out_u.reshape(64, n_u), u_b,
        out_d.reshape(h_d, 256), out_b, out_p.reshape(h_p, 256), out_b,
        gain_sums[0], gain_sums[1], gain_sums[2], gain_sums[3],
    )


def solution(mesh):
    in_specs = (
        P(("dp", "col"), "row"), P(("dp", "row")), P("row"), P("row"), P("row"), P("row"),
        P(("row", "dp"), "col"), P(("col", "dp")), P(("row", "dp"), "col"), P(("col", "dp")),
        P(("col", "dp"), "row"), P(("row", "dp")), P(("col", "dp"), "row"), P(("row", "dp")),
        P(("dp", "col"), "row"),
    )
    out_specs = (
        P(("dp", "col"), "row"), P(("dp", "col"), "row"), P(("row", "dp"), "col"), P(("col", "dp")),
        P(("row", "dp"), "col"), P(("col", "dp")), P(("col", "dp"), "row"), P(("row", "dp")),
        P(("col", "dp"), "row"), P(("row", "dp")), P("row"), P("row"), P("row"), P("row"),
    )
    body = functools.partial(shards, mesh.shape["col"])
    return jax.shard_map(body, mesh=mesh, in_specs=in_specs, out_specs=out_specs, check_vma=False)
```

```python
import functools
import math

import jax
import jax.numpy as jnp
from jax import lax
from jax.experimental import pallas as pl
from jax.experimental.pallas import tpu as pltpu
from jax.sharding import PartitionSpec as P

D = 1024
HD = 64
ROT = 16
FF = 4096
SEQ_LEN = 1024
EPS = 1e-05
NEGATIVE = -1e30
ROWS = 4
DPS = 4
MESH = pl.DeviceIdType.MESH
BF = jnp.bfloat16
F32 = jnp.float32


def places():
    dp, row, col = lax.axis_index("dp"), lax.axis_index("row"), lax.axis_index("col")
    across = dp + 1 - 2 * lax.rem(dp, 2)
    along = lax.rem(dp + 2, 4)
    return dp, row, col, across, along


def line_order(row):
    far = row // 2
    side = row + far * (3 - 2 * row)
    at = lambda place: far * 3 + (1 - 2 * far) * place
    return side, at


def greet(targets):
    barrier = pltpu.get_barrier_semaphore()
    for target in targets:
        pl.semaphore_signal(barrier, inc=1, device_id=target, device_id_type=MESH)
    pl.semaphore_wait(barrier, len(targets))


def peers_of(dp, row, col, cols):
    group = []
    for step in range(1, ROWS * cols):
        flat = lax.rem(row * cols + col + step, ROWS * cols)
        group.append((dp, flat // cols, lax.rem(flat, cols)))
    for step in range(1, DPS):
        for other in range(ROWS):
            group.append((lax.rem(dp + step, DPS), lax.rem(row + other, ROWS), col))
    return group


def remote(src, dst, send, recv, target):
    return pltpu.make_async_remote_copy(
        src_ref=src, dst_ref=dst, send_sem=send, recv_sem=recv, device_id=target, device_id_type=MESH
    )


N_W = 4
QKV, UP, DENSE, DOWN = range(N_W)


def nt(left, right):
    return lax.dot_general(left, right, (((1,), (1,)), ((), ())), preferred_element_type=F32)


def nn(left, right):
    return jnp.dot(left, right, preferred_element_type=F32)


def span(start, size, unit):
    return pl.ds(pl.multiple_of(start, unit), size)


def slot(w, ref, row, dp, height, half=None):
    if w in (QKV, UP):
        if half is None:
            return ref.at[span((row * DPS + dp) * height, height, 64), :]
        return ref.at[span((row * DPS + dp) * height + half * (height // 2), height // 2, 32), :]
    if half is None:
        return ref.at[span(dp * height, height, 16), span(row * 256, 256, 256)]
    if w == DENSE:
        return ref.at[span(dp * height, height, 16), span(row * 256 + half * 128, 128, 128)]
    return ref.at[span(dp * height + half * (height // 2), height // 2, 16), span(row * 256, 256, 256)]


def half_of(w, ref, half):
    height = ref.shape[0]
    if w == DENSE:
        return ref.at[:, pl.ds(half * 128, 128)]
    return ref.at[pl.ds(half * (height // 2), height // 2), :]


def read_gains(smalls, gains):
    for r in range(ROWS):
        for g in range(4):
            for t in range(2):
                gains[g : g + 1, pl.ds(r * 256 + t * 128, 128)] = smalls[r * DPS, pl.ds(2 * g + t, 1), :]


def read_bias(smalls, bias, first_row, size):
    per = size // 128
    for d in range(DPS):
        for t in range(per):
            bias[0:1, pl.ds(d * size + t * 128, 128)] = smalls[d, pl.ds(first_row + t, 1), :]


def norm_rows(x):
    center = jnp.mean(x, axis=1, keepdims=True)
    spread = jnp.mean(x * x, axis=1, keepdims=True) - center * center
    scale_inv = lax.rsqrt(spread + EPS)
    return (x - center) * scale_inv, scale_inv


def norm_stage(x_ref, gains, which, plain, turned):
    def body(i, carry):
        rows = span(i * 128, 128, 128)
        normed, ignored = norm_rows(x_ref[rows, :].astype(F32))
        value = (normed * gains[which : which + 1, :] + gains[which + 1 : which + 2, :]).astype(BF)
        plain[rows, :] = value
        turned[:, rows] = value.T
        return carry

    lax.fori_loop(0, SEQ_LEN // 128, body, 0)


def project_stage(wq, first, bias_row, angles, q_t, k_t, v_t, k_n, v_n, heads):
    pair = min(heads, 2)
    width = 192 * pair

    def body(p, carry):
        cols = pl.ds(0, width) if heads == pair else span(p * width, width, 128)
        w_t = wq[:, cols].T
        bias = jnp.broadcast_to(bias_row[0:1, cols], (8, width)).T[:, 0:1]
        for j in range(SEQ_LEN // 256):
            toks = pl.ds(j * 256, 256)
            mixed = nt(w_t, first[toks, :]) + bias
            cos, sin = angles[0:8, toks], angles[8:16, toks]

            def turn(base):
                x1, x2 = mixed[base : base + 8], mixed[base + 8 : base + 16]
                return jnp.concatenate([x1 * cos - x2 * sin, x2 * cos + x1 * sin, mixed[base + 16 : base + 64]], axis=0)

            for e in range(pair):
                base, h = 192 * e, pair * p + e
                q_t[h, :, toks] = (turn(base) * HD ** (-0.5)).astype(BF)
                keys, values = turn(base + 64).astype(BF), mixed[base + 128 : base + 192].astype(BF)
                k_t[h, :, toks] = keys
                v_t[h, :, toks] = values
                k_n[h, toks, :] = keys.T
                v_n[h, toks, :] = values.T
        return carry

    lax.fori_loop(0, heads // pair, body, 0)


def upstream_stage(wd, c_ref, up_t, heads):
    for j in range(SEQ_LEN // 256):
        toks = pl.ds(j * 256, 256)
        grad = nt(wd[...], c_ref[toks, :]).astype(BF)
        for h in range(heads):
            up_t[h, :, toks] = grad[HD * h : HD * (h + 1)]


def attend_head(h, prefix, angles, q_t, k_t, v_t, k_n, v_n, up_t, att_t, gm_t, grad_q, grad_k, grad_v):
    done = 0
    for i in range(SEQ_LEN // 256):
        low = 256 * i
        seen = max(512, low + 256)
        spot = pl.ds(low, 256)
        q, up = q_t[h, :, spot], up_t[h, :, spot]
        scores = nn(k_n[h, 0:seen, :], q)
        plain = min(low, seen)
        keys = lax.broadcasted_iota(jnp.int32, (seen - plain, 256), 0) + plain
        queries = lax.broadcasted_iota(jnp.int32, (seen - plain, 256), 1) + low
        masked = jnp.where((keys <= queries) | (keys < prefix), scores[plain:], NEGATIVE)
        scores = jnp.concatenate([scores[:plain], masked], axis=0) if plain else masked
        exponent = jnp.exp(scores - jnp.max(scores, axis=0, keepdims=True))
        probs = exponent * (1.0 / jnp.sum(exponent, axis=0, keepdims=True))
        weights = probs.astype(BF)
        att_t[h, :, spot] = nn(v_t[h, :, 0:seen], weights).astype(BF)
        grad_probs = nn(v_n[h, 0:seen, :], up)
        inner = jnp.sum(probs * grad_probs, axis=0, keepdims=True)
        grad_scores = (probs * (grad_probs - inner)).astype(BF)
        grad_q[:, spot] = nn(k_t[h, :, 0:seen], grad_scores)
        for total, part in ((grad_v, nt(up, weights)), (grad_k, nt(q, grad_scores))):
            if done:
                total[:, 0:done] += part[:, :done]
            if seen > done:
                total[:, done:seen] = part[:, done:]
        done = seen
    cos, sin = angles[0:8, :], angles[8:16, :]

    def turn_back(grad):
        g1, g2 = grad[0:8], grad[8:16]
        return jnp.concatenate([g1 * cos + g2 * sin, g2 * cos - g1 * sin, grad[16:]], axis=0)

    base = h * 192
    gm_t[span(base, HD, HD), :] = (turn_back(grad_q[...]) * HD ** (-0.5)).astype(BF)
    gm_t[span(base + HD, HD, HD), :] = turn_back(grad_k[...]).astype(BF)
    gm_t[span(base + 2 * HD, HD, HD), :] = grad_v[...].astype(BF)


def gather_kernel(cols, aligned, *refs):
    (prefix_ref, tok_ref, cot_ref, small_ref, angles, bias_in) = refs[:6]
    masters = refs[6:10]
    (x_out, c_out, smalls_out, gq_ref, gu_ref, gd_ref, gp_ref, wgq_ref, wgd_ref, gm_ref, att_ref, gb_ref) = refs[10:22]
    own = refs[22:26]
    stage = refs[26:30]
    (x_ref, c_ref, smalls, wq, wd, gains, bias_row, first, first_t) = refs[30:39]
    (q_t, k_t, v_t, k_n, v_n, up_t, att_t, gm_t, grad_q, grad_k, grad_v) = refs[39:50]
    (z_send, z_recv, s1_send, s1_recv, s2_send, s2_recv, t_send, t_recv, a_send, a_recv, m_send, m_recv, l_sem) = refs[50:]
    full = (wq, gu_ref, wd, gp_ref)
    heads = q_t.shape[0]
    dp, row, col, across, along = places()
    side, at = line_order(row)
    order = [row, at(1 - side), at(2), at(3)]
    middle = side == 1
    tok_col = tok_ref.shape[0]
    part = SEQ_LEN // cols
    chunk = min(tok_col, SEQ_LEN)
    n_seq = tok_col // chunk
    n_part = chunk // part

    loads = [pltpu.make_async_copy(masters[w], stage[w], l_sem.at[w]) for w in range(N_W)]
    for load in loads:
        load.start()
    greet(peers_of(dp, row, col, cols))

    def token_copy(kind, j, i):
        src_ref, dst_ref = ((tok_ref, x_ref), (cot_ref, c_ref))[kind]
        start = col * tok_col + j * chunk
        to_row = start // SEQ_LEN
        piece = lax.rem(start, SEQ_LEN) // part + i
        src = src_ref.at[pl.ds(j * chunk + i * part, part), :]
        dst = dst_ref.at[span(piece * part, part, part), span(row * 256, 256, 256)]
        sends, recvs = t_send.at[kind, j * n_part + i], t_recv.at[kind, row]
        is_here = jnp.logical_and(to_row == row, piece == col)
        far = remote(src, dst, sends, recvs, (dp, to_row, piece))
        near = pltpu.make_async_copy(src, dst, recvs)
        return is_here, far, near

    def token_start(kind):
        for j in range(n_seq):
            for i in range(n_part):
                is_here, far, near = token_copy(kind, j, i)
                pl.when(jnp.logical_not(is_here))(far.start)
                pl.when(is_here)(near.start)

    def part_rows(piece):
        return span(piece * part, part, part)

    def spread_copy(kind, step):
        mine = (x_ref, c_ref)[kind].at[part_rows(col), :]
        to_col = lax.rem(col + step, cols)
        return remote(mine, mine, a_send.at[kind, step - 1], a_recv.at[kind, step - 1], (dp, row, to_col))

    def token_spread(kind):
        dst_ref = (x_ref, c_ref)[kind]
        for other in range(ROWS):
            block = dst_ref.at[part_rows(col), pl.ds(other * 256, 256)]
            pltpu.make_async_copy(block, block, t_recv.at[kind, other]).wait()
        for step in range(1, cols):
            spread_copy(kind, step).start()

    def token_finish(kind):
        dst_ref = (x_ref, c_ref)[kind]
        for step in range(1, cols):
            from_col = lax.rem(col + cols - step, cols)
            theirs = dst_ref.at[part_rows(from_col), :]
            pltpu.make_async_copy(theirs, theirs, a_recv.at[kind, step - 1]).wait()

    def token_drain(kind):
        for j in range(n_seq):
            for i in range(n_part):
                is_here, far, near = token_copy(kind, j, i)
                pl.when(jnp.logical_not(is_here))(far.wait_send)
        for step in range(1, cols):
            spread_copy(kind, step).wait_send()

    me = row * DPS + dp

    def small_copy(step):
        flat = lax.rem(me + step, ROWS * DPS)
        return remote(
            small_ref, smalls.at[me], m_send.at[step - 1], m_recv.at[step - 1], (lax.rem(flat, DPS), flat // DPS, col)
        )

    def place(w, r, d, half=None):
        return slot(w, full[w], r, d, own[w].shape[0], half)

    def source(w, k, half=None):
        if k == 0:
            return own[w] if half is None else half_of(w, own[w], half)
        return place(w, order[k], dp, half)

    def line_copies(w, k):
        src = source(w, k)
        dst = place(w, order[k], dp)
        recv = z_recv.at[w, order[k]]
        if k == 0:
            return [
                (None, remote(src, dst, z_send.at[w, 0], recv, (dp, at(1 - side), col))),
                (middle, remote(src, dst, z_send.at[w, 1], recv, (dp, at(2), col))),
            ]
        onward = at(2) if k == 1 else at(0)
        return [(middle, remote(src, dst, z_send.at[w, k + 1], recv, (dp, onward, col)))]

    def first_copies(w, k):
        out = []
        for half, target in ((0, across), (1, along)):
            out.append(
                remote(source(w, k, half), place(w, order[k], dp, half), s1_send.at[w, k, half],
                       s1_recv.at[w, k, half], (target, row, col))
            )
        return out

    def second_copies(w, k, which):
        out = []
        for half, target, other in ((0, along, across), (1, across, along)):
            if which == 0:
                src, owner = source(w, k, half), dp
            else:
                src, owner = place(w, order[k], other, half), other
            out.append(
                remote(src, place(w, order[k], owner, half), s2_send.at[w, k, which, half],
                       s2_recv.at[w, k, which, half], (target, row, col))
            )
        return out

    def arrived(w, k):
        if k > 0:
            block = place(w, order[k], dp)
            pltpu.make_async_copy(block, block, z_recv.at[w, order[k]]).wait()
        for cond, copy in line_copies(w, k):
            if cond is None:
                copy.start()
            else:
                pl.when(cond)(copy.start)
        for copy in first_copies(w, k) + second_copies(w, k, 0):
            copy.start()

    def passed(w, k):
        for copy in first_copies(w, k):
            copy.wait_recv()
        for copy in second_copies(w, k, 1):
            copy.start()

    def finished(w):
        for k in range(ROWS):
            for which in range(2):
                for copy in second_copies(w, k, which):
                    copy.wait_recv()

    def drained(w, k):
        for cond, copy in line_copies(w, k):
            if cond is None:
                copy.wait_send()
            else:
                pl.when(cond)(copy.wait_send)
        for copy in first_copies(w, k) + second_copies(w, k, 0) + second_copies(w, k, 1):
            copy.wait_send()

    def home(w):
        return pltpu.make_async_copy(own[w], place(w, row, dp), l_sem.at[w])

    def begin(w):
        loads[w].wait()
        own[w][...] = stage[w][...].astype(BF)
        arrived(w, 0)
        home(w).start()

    small_home = pltpu.make_async_copy(small_ref, smalls.at[me], l_sem.at[N_W])
    small_home.start()
    begin(QKV)
    for step in range(1, ROWS * DPS):
        small_copy(step).start()
    token_start(0)
    begin(DENSE)
    passed(QKV, 0)
    begin(UP)
    begin(DOWN)
    passed(DENSE, 0)
    arrived(QKV, 1)
    arrived(DENSE, 1)
    passed(QKV, 1)
    passed(DENSE, 1)
    passed(UP, 0)
    passed(DOWN, 0)
    token_spread(0)
    arrived(QKV, 2)
    arrived(DENSE, 2)
    token_start(1)
    token_finish(0)
    small_home.wait()
    for step in range(1, ROWS * DPS):
        small_copy(step).wait()
    read_gains(smalls, gains)
    if aligned:
        read_bias(smalls, bias_row, 9, bias_row.shape[1] // DPS)
    else:
        bias_row[...] = bias_in[...]
    norm_stage(x_ref, gains, 0, first, first_t)
    passed(QKV, 2)
    passed(DENSE, 2)
    arrived(QKV, 3)
    arrived(DENSE, 3)
    passed(QKV, 3)
    passed(DENSE, 3)
    arrived(UP, 1)
    arrived(DOWN, 1)
    home(QKV).wait()
    finished(QKV)
    keep_x = pltpu.make_async_copy(x_ref, x_out, l_sem.at[N_W])
    keep_wq = pltpu.make_async_copy(wq, gq_ref, l_sem.at[QKV])
    keep_x.start()
    keep_wq.start()
    project_stage(wq, first, bias_row, angles, q_t, k_t, v_t, k_n, v_n, heads)
    passed(UP, 1)
    passed(DOWN, 1)
    token_spread(1)
    arrived(UP, 2)
    home(DENSE).wait()
    finished(DENSE)
    token_finish(1)
    keep_c = pltpu.make_async_copy(c_ref, c_out, l_sem.at[N_W + 1])
    keep_wd = pltpu.make_async_copy(wd, gd_ref, l_sem.at[DENSE])
    keep_smalls = pltpu.make_async_copy(smalls, smalls_out, l_sem.at[N_W + 2])
    keep_c.start()
    keep_wd.start()
    keep_smalls.start()
    upstream_stage(wd, c_ref, up_t, heads)
    prefix = prefix_ref[0]

    services = [
        lambda: arrived(DOWN, 2),
        lambda: passed(UP, 2),
        lambda: passed(DOWN, 2),
        lambda: arrived(UP, 3),
        lambda: arrived(DOWN, 3),
        lambda: passed(UP, 3),
        lambda: passed(DOWN, 3),
    ]

    def head_body(h, carry):
        for n, service in enumerate(services):
            if n < heads - 1:
                pl.when(h == n)(service)
        attend_head(h, prefix, angles, q_t, k_t, v_t, k_n, v_n, up_t, att_t, gm_t, grad_q, grad_k, grad_v)
        return carry

    lax.fori_loop(0, heads, head_body, 0)
    for service in services[max(heads - 1, 0) :]:
        service()

    width = gm_t.shape[0]
    wide = min(512, width)

    def qkv_body(i, carry):
        rows = span(i * 256, 256, 256)
        for n in range(width // wide):
            wgq_ref[rows, n * wide : (n + 1) * wide] = nt(first_t[rows, :], gm_t[n * wide : (n + 1) * wide, :]).astype(BF)
        return carry

    lax.fori_loop(0, D // 256, qkv_body, 0)
    group = min(heads, 4)

    def dense_body(i, carry):
        block = att_t[pl.ds(i * group, group)].reshape(group * HD, SEQ_LEN)
        spot = pl.ds(0, group * HD) if heads == group else span(i * group * HD, group * HD, 128)
        wgd_ref[spot, :] = nn(block, c_ref[...]).astype(BF)
        att_ref[:, spot] = block.T
        return carry

    lax.fori_loop(0, heads // group, dense_body, 0)
    pair = min(heads, 2) * 192

    def turn_body(p, carry):
        spot = pl.ds(0, pair) if pair == width else span(p * pair, pair, 128)
        value = gm_t[spot, :].T
        gm_ref[:, spot] = value
        gb_ref[0:1, spot] = jnp.sum(value.astype(F32), axis=0, keepdims=True)
        return carry

    lax.fori_loop(0, width // pair, turn_body, 0)

    for w in (UP, DOWN):
        finished(w)
        home(w).wait()
    for w in range(N_W):
        for k in range(ROWS):
            drained(w, k)
    for kind in range(2):
        token_drain(kind)
    for keep in (keep_x, keep_wq, keep_c, keep_wd, keep_smalls):
        keep.wait()


def gather(prefix_len, tokens_in, cotangent, small, angles, bias, weights, cols, aligned):
    wq, wu, wd, wp = weights
    n_q, n_u = wq.shape[1], wu.shape[1]
    heads = n_q // 192
    width = heads * HD
    any_spec = pl.BlockSpec(memory_space=pl.ANY)
    vmem = pl.BlockSpec(memory_space=pltpu.VMEM)
    smem = pl.BlockSpec(memory_space=pltpu.SMEM)
    shape = jax.ShapeDtypeStruct
    smalls = (ROWS * DPS,) + small.shape
    out_shape = [
        shape((SEQ_LEN, D), BF), shape((SEQ_LEN, D), BF), shape(smalls, F32),
        shape((D, n_q), BF), shape((D, n_u), BF), shape((width, D), BF), shape((wp.shape[0] * DPS, D), BF),
        shape((D, n_q), BF), shape((width, D), BF), shape((SEQ_LEN, n_q), BF), shape((SEQ_LEN, width), BF),
        shape((1, n_q), F32),
    ]
    tok_col = tokens_in.shape[0]
    pieces = tok_col // (SEQ_LEN // cols)
    dma = pltpu.SemaphoreType.DMA
    buf = pltpu.VMEM
    turned = buf((heads, HD, SEQ_LEN), BF)
    plain = buf((heads, SEQ_LEN, HD), BF)
    scratch = [buf(w.shape, BF) for w in weights] + [buf(w.shape, F32) for w in weights]
    scratch += [
        buf((SEQ_LEN, D), BF), buf((SEQ_LEN, D), BF), buf(smalls, F32), buf((D, n_q), BF), buf((width, D), BF),
        buf((8, D), F32), buf((1, n_q), F32), buf((SEQ_LEN, D), BF), buf((D, SEQ_LEN), BF),
        turned, turned, turned, plain, plain, turned, turned, buf((n_q, SEQ_LEN), BF),
        buf((HD, SEQ_LEN), F32), buf((HD, SEQ_LEN), F32), buf((HD, SEQ_LEN), F32),
        dma((N_W, 5)), dma((N_W, 4)), dma((N_W, 4, 2)), dma((N_W, 4, 2)), dma((N_W, 4, 2, 2)), dma((N_W, 4, 2, 2)),
        dma((2, pieces)), dma((2, 4)), dma((2, cols - 1)), dma((2, cols - 1)),
        dma((ROWS * DPS - 1,)), dma((ROWS * DPS - 1,)), dma((N_W + 3,)),
    ]
    return pl.pallas_call(
        functools.partial(gather_kernel, cols, aligned),
        out_shape=out_shape,
        in_specs=[smem, any_spec, any_spec, any_spec, vmem, vmem] + [any_spec] * 4,
        out_specs=[any_spec] * 7 + [vmem] * 5,
        scratch_shapes=scratch,
        compiler_params=pltpu.CompilerParams(collective_id=0, has_side_effects=True, vmem_limit_bytes=60 << 20),
    )(prefix_len, tokens_in, cotangent, small, angles, bias, wq, wu, wd, wp)


def lead(name, y, x, half):
    return (slice(None), y, x, half) if name < 2 else (y, x, half)


def add_into(dst, src):
    shape = dst.shape
    outer, height = shape[:-2], shape[-2]
    step = 32
    per = height // step
    total = math.prod(outer) * per

    def body(i, carry):
        index, rest = [], i // per
        for size in reversed(outer):
            index.append(lax.rem(rest, size))
            rest = rest // size
        where = tuple(reversed(index)) + (pl.ds(pl.multiple_of(lax.rem(i, per) * step, step), step),)
        dst[where] = (dst[where].astype(F32) + src[where].astype(F32)).astype(BF)
        return carry

    lax.fori_loop(0, total, body, 0)


def scatter_kernel(cols, heights, *refs):
    g_refs = refs[:4]
    out_refs = refs[4:8]
    mine = (refs[8:10], refs[10:12], refs[12:14], refs[14:16])
    got1 = (refs[16:18], refs[18:20], refs[20:22], refs[22:24])
    got2 = (refs[24:26], refs[26:28], refs[28:30], refs[30:32])
    got3 = (refs[32:34], refs[34:36], refs[36:38], refs[38:40])
    l_sem, s1_send, s1_recv, s2_send, s2_recv, s3_send, s3_recv = refs[40:]
    dp, row, col, across, along = places()
    x, y = lax.rem(dp, 2), dp // 2

    greet(peers_of(dp, row, col, cols))

    def first(w, half):
        if half == 0:
            src, target = g_refs[w].at[lead(w, 1 - y, slice(None), 0)], along
        else:
            src, target = g_refs[w].at[lead(w, slice(None), 1 - x, 1)], across
        return remote(src, got1[w][half], s1_send.at[w, half], s1_recv.at[w, half], (target, row, col))

    def fetch(w, half):
        src = g_refs[w].at[lead(w, y, slice(None), 0)] if half == 0 else g_refs[w].at[lead(w, slice(None), x, 1)]
        return pltpu.make_async_copy(src, mine[w][half], l_sem.at[w, half])

    def keep(w, half, other):
        which = (x if half == 0 else y)
        which = 1 - which if other else which
        return mine[w][half].at[:, which] if w < 2 else mine[w][half].at[which]

    def second(w, half):
        target = across if half == 0 else along
        return remote(keep(w, half, True), got2[w][half], s2_send.at[w, half], s2_recv.at[w, half], (target, row, col))

    def block(w, half, r):
        kept = keep(w, half, False)
        if w < 2:
            return kept.at[r]
        return kept.at[:, pl.ds(pl.multiple_of(r * 256, 256), 256)]

    def third(w, half, step):
        to_row = lax.rem(row + step, ROWS)
        return remote(
            block(w, half, to_row), got3[w][half].at[step - 1], s3_send.at[w, half, step - 1],
            s3_recv.at[w, half, step - 1], (dp, to_row, col)
        )

    def total(w, half):
        height = out_refs[w].shape[1]
        step = 32

        def body(i, carry):
            rows = pl.ds(pl.multiple_of(i * step, step), step)
            value = block(w, half, row)[rows, :].astype(F32)
            for s in range(3):
                value = value + got3[w][half][s, rows, :].astype(F32)
            out_refs[w][half, rows, :] = value
            return carry

        lax.fori_loop(0, height // step, body, 0)

    sequence = [(w, half) for w in (2, 0, 1, 3) for half in range(2)]

    def begin(w, half):
        first(w, half).start()
        fetch(w, half).start()

    for w, half in sequence[:4]:
        begin(w, half)

    def stage_two(w, half):
        fetch(w, half).wait()
        first(w, half).wait_recv()
        add_into(mine[w][half], got1[w][half])
        second(w, half).start()

    def stage_three(w, half):
        second(w, half).wait()
        add_into(keep(w, half, False), got2[w][half])
        for step in range(1, ROWS):
            third(w, half, step).start()

    def stage_four(w, half):
        for step in range(1, ROWS):
            third(w, half, step).wait()
        total(w, half)

    lag2, lag3 = 2, 4
    n = len(sequence)
    for i in range(n + lag3):
        if i < n:
            stage_two(*sequence[i])
            if i + 4 < n:
                begin(*sequence[i + 4])
        if 0 <= i - lag2 < n:
            stage_three(*sequence[i - lag2])
        if 0 <= i - lag3 < n:
            stage_four(*sequence[i - lag3])
    for w, half in sequence:
        first(w, half).wait_send()


def scatter(grads, cols):
    any_spec = pl.BlockSpec(memory_space=pl.ANY)
    vmem = pl.BlockSpec(memory_space=pltpu.VMEM)
    dma = pltpu.SemaphoreType.DMA
    outs, mine, got1, got2, got3 = [], [], [], [], []
    for w, grad in enumerate(grads):
        h, n = grad.shape[-2:]
        if w < 2:
            outs.append(jax.ShapeDtypeStruct((2, h, n), F32))
            mine += [pltpu.VMEM((ROWS, 2, h, n), BF)] * 2
            got1 += [pltpu.VMEM((ROWS, 2, h, n), BF)] * 2
            got2 += [pltpu.VMEM((ROWS, h, n), BF)] * 2
            got3 += [pltpu.VMEM((3, h, n), BF)] * 2
        else:
            outs.append(jax.ShapeDtypeStruct((2, h, 256), F32))
            mine += [pltpu.VMEM((2, h, n), BF)] * 2
            got1 += [pltpu.VMEM((2, h, n), BF)] * 2
            got2 += [pltpu.VMEM((h, n), BF)] * 2
            got3 += [pltpu.VMEM((3, h, 256), BF)] * 2
    return pl.pallas_call(
        functools.partial(scatter_kernel, cols, None),
        out_shape=outs,
        in_specs=[any_spec] * 4,
        out_specs=[vmem] * 4,
        scratch_shapes=mine + got1 + got2 + got3 + [
            dma((N_W, 2)), dma((N_W, 2)), dma((N_W, 2)), dma((N_W, 2)), dma((N_W, 2)), dma((N_W, 2, 3)), dma((N_W, 2, 3)),
        ],
        compiler_params=pltpu.CompilerParams(collective_id=1, has_side_effects=True, vmem_limit_bytes=48 << 20),
    )(*grads)


def angles_table():
    half_rot = ROT // 2
    places_ = jnp.arange(SEQ_LEN, dtype=F32)
    rates = jnp.exp(jnp.arange(half_rot, dtype=F32) * (-2.0 * math.log(10000.0) / ROT))
    turned = places_[:, None] * rates[None, :]
    return (jnp.cos(turned), jnp.sin(turned))


def contract_rows(left_side, right_side):
    return lax.dot_general(left_side, right_side, (((0,), (0,)), ((), ())), preferred_element_type=F32)


def contract_cols(left_side, right_side):
    return lax.dot_general(left_side, right_side, (((1,), (1,)), ((), ())), preferred_element_type=F32)


def shards(cols, tokens_in, prefix_len, first_gain, first_shift, second_gain, second_shift, qkv_weight, qkv_bias,
           up_weight, up_bias, dense_weight, dense_bias, down_weight, down_bias, cotangent):
    tok_col = tokens_in.shape[0]
    n_q, n_u = qkv_weight.shape[1], up_weight.shape[1]
    h_d, h_p = dense_weight.shape[0], down_weight.shape[0]
    heads = n_q // (3 * HD)
    width_att = heads * HD

    out_part = dense_bias.astype(BF).astype(F32) + down_bias.astype(BF).astype(F32)
    q_part, u_part = qkv_bias.astype(BF).astype(F32), up_bias.astype(BF).astype(F32)
    n_qb, n_ub = q_part.shape[0], u_part.shape[0]
    aligned = n_qb % 128 == 0 and n_ub % 128 == 0
    small = jnp.concatenate((first_gain, first_shift, second_gain, second_shift, out_part, out_part, q_part, u_part))
    size = -(-small.shape[0] // 1024) * 1024
    small = jnp.pad(small, (0, size - small.shape[0])).reshape(size // 128, 128)
    if aligned:
        q_bias = jnp.zeros((1, n_q), F32)
    else:
        q_bias = lax.all_gather(q_part, "dp", axis=0, tiled=True).reshape(1, n_q)
    cos_table, sin_table = angles_table()
    angles = jnp.concatenate([cos_table.T, sin_table.T], axis=0)
    own_x, own_cot, smalls, wq, wu, wd, wp, wgrad_q, wgrad_d, grad_mixed, attended, sum_q = gather(
        prefix_len, tokens_in, cotangent, small, angles, q_bias, (qkv_weight, up_weight, dense_weight, down_weight), cols,
        aligned
    )
    flat = smalls.reshape(ROWS, DPS, size)
    gains = [flat[:, 0, 256 * i : 256 * (i + 1)].reshape(D) for i in range(4)]
    out_bias = flat[:, :, 1024:1088].reshape(D)
    u_bias = flat[0, :, 1152 + n_qb : 1152 + n_qb + n_ub].reshape(n_u)

    wide = own_x.astype(F32)
    center = jnp.mean(wide, axis=1, keepdims=True)
    spread = jnp.mean(wide * wide, axis=1, keepdims=True) - center * center
    scale_inv = lax.rsqrt(spread + EPS)
    normed = (wide - center) * scale_inv
    second_in = (normed * gains[2] + gains[3]).astype(BF)

    hidden_pre = jnp.dot(second_in, wu, preferred_element_type=F32) + u_bias
    hidden = jax.nn.gelu(hidden_pre, approximate=False).astype(BF)
    branch = jnp.dot(attended, wd, preferred_element_type=F32) + jnp.dot(hidden, wp, preferred_element_type=F32)
    grad_hidden = contract_cols(own_cot, wp)
    ignored, gelu_back = jax.vjp(functools.partial(jax.nn.gelu, approximate=False), hidden_pre)
    grad_hidden_pre = gelu_back(grad_hidden)[0].astype(BF)

    grads = (
        wgrad_q.reshape(ROWS, 2, 2, 2, 32, n_q),
        contract_rows(second_in, grad_hidden_pre).astype(BF).reshape(ROWS, 2, 2, 2, 32, n_u),
        wgrad_d.reshape(2, 2, 2, h_d // 2, D),
        contract_rows(hidden, own_cot).astype(BF).reshape(2, 2, 2, h_p // 2, D),
    )
    out_q, out_u, out_d, out_p = scatter(grads, cols)

    grad_first = contract_cols(grad_mixed, wq)
    grad_second = contract_cols(grad_hidden_pre, wu)
    combined = grad_first * gains[0] + grad_second * gains[2]
    part = SEQ_LEN // cols

    def to_owner(partial):
        moved = lax.all_to_all(partial, "row", split_axis=1, concat_axis=0, tiled=True)
        return lax.psum_scatter(moved, "col", scatter_dimension=0, tiled=True)

    branch_sum = to_owner(branch)
    combined = lax.psum(combined, "col")
    gain_rows = jnp.stack([
        jnp.sum(normed * grad_first, axis=0), jnp.sum(grad_first, axis=0),
        jnp.sum(normed * grad_second, axis=0), jnp.sum(grad_second, axis=0),
    ])
    line_total = jnp.mean(combined, axis=1, keepdims=True)
    cross_total = jnp.mean(combined * normed, axis=1, keepdims=True)
    grad_tokens = (own_cot.astype(F32) + scale_inv * (combined - line_total - normed * cross_total)).astype(BF)
    grad_tokens = lax.all_to_all(grad_tokens, "row", split_axis=1, concat_axis=0, tiled=True)
    grad_tokens = lax.dynamic_slice_in_dim(grad_tokens, lax.axis_index("col") * tok_col, tok_col, 0)
    row = lax.axis_index("row")
    here = lax.dynamic_slice_in_dim(out_bias, row * 256, 256, 0)
    layer_out = (tokens_in.astype(F32) + branch_sum + here).astype(BF)

    gain_sums = lax.psum_scatter(
        lax.psum(gain_rows, ("dp", "col")), "row", scatter_dimension=1, tiled=True
    )
    out_b = lax.psum_scatter(jnp.sum(own_cot.astype(F32), axis=0), ("row", "dp"), scatter_dimension=0, tiled=True)
    q_b = lax.psum_scatter(
        lax.psum(sum_q[0], "row"), "dp", scatter_dimension=0, tiled=True
    )
    u_b = lax.psum_scatter(
        lax.psum(jnp.sum(grad_hidden_pre.astype(F32), axis=0), "row"), "dp", scatter_dimension=0, tiled=True
    )
    return (
        layer_out, grad_tokens, out_q.reshape(64, n_q), q_b, out_u.reshape(64, n_u), u_b,
        out_d.reshape(h_d, 256), out_b, out_p.reshape(h_p, 256), out_b,
        gain_sums[0], gain_sums[1], gain_sums[2], gain_sums[3],
    )


def solution(mesh):
    in_specs = (
        P(("dp", "col"), "row"), P(("dp", "row")), P("row"), P("row"), P("row"), P("row"),
        P(("row", "dp"), "col"), P(("col", "dp")), P(("row", "dp"), "col"), P(("col", "dp")),
        P(("col", "dp"), "row"), P(("row", "dp")), P(("col", "dp"), "row"), P(("row", "dp")),
        P(("dp", "col"), "row"),
    )
    out_specs = (
        P(("dp", "col"), "row"), P(("dp", "col"), "row"), P(("row", "dp"), "col"), P(("col", "dp")),
        P(("row", "dp"), "col"), P(("col", "dp")), P(("col", "dp"), "row"), P(("row", "dp")),
        P(("col", "dp"), "row"), P(("row", "dp")), P("row"), P("row"), P("row"), P("row"),
    )
    body = functools.partial(shards, mesh.shape["col"])
    return jax.shard_map(body, mesh=mesh, in_specs=in_specs, out_specs=out_specs, check_vma=False)
```

```python
import functools
import math

import jax
import jax.numpy as jnp
from jax import lax
from jax.experimental import pallas as pl
from jax.experimental.pallas import tpu as pltpu
from jax.sharding import PartitionSpec as P

D = 1024
HD = 64
ROT = 16
FF = 4096
SEQ_LEN = 1024
EPS = 1e-05
NEGATIVE = -1e30
ROWS = 4
DPS = 4
MESH = pl.DeviceIdType.MESH
BF = jnp.bfloat16
F32 = jnp.float32


def places():
    dp, row, col = lax.axis_index("dp"), lax.axis_index("row"), lax.axis_index("col")
    across = dp + 1 - 2 * lax.rem(dp, 2)
    along = lax.rem(dp + 2, 4)
    return dp, row, col, across, along


def line_order(row):
    far = row // 2
    side = row + far * (3 - 2 * row)
    at = lambda place: far * 3 + (1 - 2 * far) * place
    return side, at


def greet(targets):
    barrier = pltpu.get_barrier_semaphore()
    for target in targets:
        pl.semaphore_signal(barrier, inc=1, device_id=target, device_id_type=MESH)
    pl.semaphore_wait(barrier, len(targets))


def peers_of(dp, row, col, cols):
    group = []
    for step in range(1, ROWS * cols):
        flat = lax.rem(row * cols + col + step, ROWS * cols)
        group.append((dp, flat // cols, lax.rem(flat, cols)))
    for step in range(1, DPS):
        for other in range(ROWS):
            group.append((lax.rem(dp + step, DPS), lax.rem(row + other, ROWS), col))
    return group


def remote(src, dst, send, recv, target):
    return pltpu.make_async_remote_copy(
        src_ref=src, dst_ref=dst, send_sem=send, recv_sem=recv, device_id=target, device_id_type=MESH
    )


N_W = 4
QKV, UP, DENSE, DOWN = range(N_W)


def nt(left, right):
    return lax.dot_general(left, right, (((1,), (1,)), ((), ())), preferred_element_type=F32)


def nn(left, right):
    return jnp.dot(left, right, preferred_element_type=F32)


def span(start, size, unit):
    return pl.ds(pl.multiple_of(start, unit), size)


def slot(w, ref, row, dp, height, half=None):
    if w in (QKV, UP):
        if half is None:
            return ref.at[span((row * DPS + dp) * height, height, 64), :]
        return ref.at[span((row * DPS + dp) * height + half * (height // 2), height // 2, 32), :]
    if half is None:
        return ref.at[span(dp * height, height, 16), span(row * 256, 256, 256)]
    if w == DENSE:
        return ref.at[span(dp * height, height, 16), span(row * 256 + half * 128, 128, 128)]
    return ref.at[span(dp * height + half * (height // 2), height // 2, 16), span(row * 256, 256, 256)]


def half_of(w, ref, half):
    height = ref.shape[0]
    if w == DENSE:
        return ref.at[:, pl.ds(half * 128, 128)]
    return ref.at[pl.ds(half * (height // 2), height // 2), :]


def read_gains(smalls, gains):
    for r in range(ROWS):
        for g in range(4):
            for t in range(2):
                gains[g : g + 1, pl.ds(r * 256 + t * 128, 128)] = smalls[r * DPS, pl.ds(2 * g + t, 1), :]


def read_bias(smalls, bias, first_row, size):
    per = size // 128
    for d in range(DPS):
        for t in range(per):
            bias[0:1, pl.ds(d * size + t * 128, 128)] = smalls[d, pl.ds(first_row + t, 1), :]


def norm_rows(x):
    center = jnp.mean(x, axis=1, keepdims=True)
    spread = jnp.mean(x * x, axis=1, keepdims=True) - center * center
    scale_inv = lax.rsqrt(spread + EPS)
    return (x - center) * scale_inv, scale_inv


def norm_stage(x_ref, gains, which, plain, turned):
    def body(i, carry):
        rows = span(i * 128, 128, 128)
        normed, ignored = norm_rows(x_ref[rows, :].astype(F32))
        value = (normed * gains[which : which + 1, :] + gains[which + 1 : which + 2, :]).astype(BF)
        plain[rows, :] = value
        turned[:, rows] = value.T
        return carry

    lax.fori_loop(0, SEQ_LEN // 128, body, 0)


def project_stage(wq, first, bias_row, angles, q_t, k_t, v_t, k_n, v_n, heads):
    pair = min(heads, 2)
    width = 192 * pair

    def body(p, carry):
        cols = pl.ds(0, width) if heads == pair else span(p * width, width, 128)
        w_t = wq[:, cols].T
        bias = jnp.broadcast_to(bias_row[0:1, cols], (8, width)).T[:, 0:1]
        for j in range(SEQ_LEN // 256):
            toks = pl.ds(j * 256, 256)
            mixed = nt(w_t, first[toks, :]) + bias
            cos, sin = angles[0:8, toks], angles[8:16, toks]

            def turn(base):
                x1, x2 = mixed[base : base + 8], mixed[base + 8 : base + 16]
                return jnp.concatenate([x1 * cos - x2 * sin, x2 * cos + x1 * sin, mixed[base + 16 : base + 64]], axis=0)

            for e in range(pair):
                base, h = 192 * e, pair * p + e
                q_t[h, :, toks] = (turn(base) * HD ** (-0.5)).astype(BF)
                keys, values = turn(base + 64).astype(BF), mixed[base + 128 : base + 192].astype(BF)
                k_t[h, :, toks] = keys
                v_t[h, :, toks] = values
                k_n[h, toks, :] = keys.T
                v_n[h, toks, :] = values.T
        return carry

    lax.fori_loop(0, heads // pair, body, 0)


def upstream_stage(wd, c_ref, up_t, heads):
    for j in range(SEQ_LEN // 256):
        toks = pl.ds(j * 256, 256)
        grad = nt(wd[...], c_ref[toks, :]).astype(BF)
        for h in range(heads):
            up_t[h, :, toks] = grad[HD * h : HD * (h + 1)]


def attend_head(h, prefix, angles, q_t, k_t, v_t, k_n, v_n, up_t, att_t, gm_t, grad_q, grad_k, grad_v):
    done = 0
    for i in range(SEQ_LEN // 256):
        low = 256 * i
        seen = max(512, low + 256)
        spot = pl.ds(low, 256)
        q, up = q_t[h, :, spot], up_t[h, :, spot]
        scores = nn(k_n[h, 0:seen, :], q)
        plain = min(low, seen)
        keys = lax.broadcasted_iota(jnp.int32, (seen - plain, 256), 0) + plain
        queries = lax.broadcasted_iota(jnp.int32, (seen - plain, 256), 1) + low
        masked = jnp.where((keys <= queries) | (keys < prefix), scores[plain:], NEGATIVE)
        scores = jnp.concatenate([scores[:plain], masked], axis=0) if plain else masked
        exponent = jnp.exp(scores - jnp.max(scores, axis=0, keepdims=True))
        probs = exponent * (1.0 / jnp.sum(exponent, axis=0, keepdims=True))
        weights = probs.astype(BF)
        att_t[h, :, spot] = nn(v_t[h, :, 0:seen], weights).astype(BF)
        grad_probs = nn(v_n[h, 0:seen, :], up)
        inner = jnp.sum(probs * grad_probs, axis=0, keepdims=True)
        grad_scores = (probs * (grad_probs - inner)).astype(BF)
        grad_q[:, spot] = nn(k_t[h, :, 0:seen], grad_scores)
        for total, part in ((grad_v, nt(up, weights)), (grad_k, nt(q, grad_scores))):
            if done:
                total[:, 0:done] += part[:, :done]
            if seen > done:
                total[:, done:seen] = part[:, done:]
        done = seen
    cos, sin = angles[0:8, :], angles[8:16, :]

    def turn_back(grad):
        g1, g2 = grad[0:8], grad[8:16]
        return jnp.concatenate([g1 * cos + g2 * sin, g2 * cos - g1 * sin, grad[16:]], axis=0)

    base = h * 192
    gm_t[span(base, HD, HD), :] = (turn_back(grad_q[...]) * HD ** (-0.5)).astype(BF)
    gm_t[span(base + HD, HD, HD), :] = turn_back(grad_k[...]).astype(BF)
    gm_t[span(base + 2 * HD, HD, HD), :] = grad_v[...].astype(BF)


def gather_kernel(cols, aligned, *refs):
    (prefix_ref, tok_ref, cot_ref, small_ref, angles, bias_in) = refs[:6]
    masters = refs[6:10]
    (x_out, c_out, smalls_out, gq_ref, gu_ref, gd_ref, gp_ref, wgq_out, wgd_out, gm_out, att_out) = refs[10:21]
    own = refs[21:25]
    stage = refs[25:29]
    (x_ref, c_ref, smalls, wq, wd, gains, bias_row, first, first_t) = refs[29:38]
    (q_t, k_t, v_t, k_n, v_n, up_t, att_t, gm_t, grad_q, grad_k, grad_v, wgq_ref, wgd_ref, att_ref) = refs[38:52]
    (z_send, z_recv, s1_send, s1_recv, s2_send, s2_recv, t_send, t_recv, a_send, a_recv, m_send, m_recv, l_sem) = refs[52:]
    full = (wq, gu_ref, wd, gp_ref)
    heads = q_t.shape[0]
    dp, row, col, across, along = places()
    side, at = line_order(row)
    order = [row, at(1 - side), at(2), at(3)]
    middle = side == 1
    tok_col = tok_ref.shape[0]
    part = SEQ_LEN // cols
    chunk = min(tok_col, SEQ_LEN)
    n_seq = tok_col // chunk
    n_part = chunk // part

    loads = [pltpu.make_async_copy(masters[w], stage[w], l_sem.at[w]) for w in range(N_W)]
    for load in loads:
        load.start()
    greet(peers_of(dp, row, col, cols))

    def token_copy(kind, j, i):
        src_ref, dst_ref = ((tok_ref, x_ref), (cot_ref, c_ref))[kind]
        start = col * tok_col + j * chunk
        to_row = start // SEQ_LEN
        piece = lax.rem(start, SEQ_LEN) // part + i
        src = src_ref.at[pl.ds(j * chunk + i * part, part), :]
        dst = dst_ref.at[span(piece * part, part, part), span(row * 256, 256, 256)]
        sends, recvs = t_send.at[kind, j * n_part + i], t_recv.at[kind, row]
        is_here = jnp.logical_and(to_row == row, piece == col)
        far = remote(src, dst, sends, recvs, (dp, to_row, piece))
        near = pltpu.make_async_copy(src, dst, recvs)
        return is_here, far, near

    def token_start(kind):
        for j in range(n_seq):
            for i in range(n_part):
                is_here, far, near = token_copy(kind, j, i)
                pl.when(jnp.logical_not(is_here))(far.start)
                pl.when(is_here)(near.start)

    def part_rows(piece):
        return span(piece * part, part, part)

    def spread_copy(kind, step):
        mine = (x_ref, c_ref)[kind].at[part_rows(col), :]
        to_col = lax.rem(col + step, cols)
        return remote(mine, mine, a_send.at[kind, step - 1], a_recv.at[kind, step - 1], (dp, row, to_col))

    def token_spread(kind):
        dst_ref = (x_ref, c_ref)[kind]
        for other in range(ROWS):
            block = dst_ref.at[part_rows(col), pl.ds(other * 256, 256)]
            pltpu.make_async_copy(block, block, t_recv.at[kind, other]).wait()
        for step in range(1, cols):
            spread_copy(kind, step).start()

    def token_finish(kind):
        dst_ref = (x_ref, c_ref)[kind]
        for step in range(1, cols):
            from_col = lax.rem(col + cols - step, cols)
            theirs = dst_ref.at[part_rows(from_col), :]
            pltpu.make_async_copy(theirs, theirs, a_recv.at[kind, step - 1]).wait()

    def token_drain(kind):
        for j in range(n_seq):
            for i in range(n_part):
                is_here, far, near = token_copy(kind, j, i)
                pl.when(jnp.logical_not(is_here))(far.wait_send)
        for step in range(1, cols):
            spread_copy(kind, step).wait_send()

    me = row * DPS + dp

    def small_copy(step):
        flat = lax.rem(me + step, ROWS * DPS)
        return remote(
            small_ref, smalls.at[me], m_send.at[step - 1], m_recv.at[step - 1], (lax.rem(flat, DPS), flat // DPS, col)
        )

    def place(w, r, d, half=None):
        return slot(w, full[w], r, d, own[w].shape[0], half)

    def source(w, k, half=None):
        if k == 0:
            return own[w] if half is None else half_of(w, own[w], half)
        return place(w, order[k], dp, half)

    def line_copies(w, k):
        src = source(w, k)
        dst = place(w, order[k], dp)
        recv = z_recv.at[w, order[k]]
        if k == 0:
            return [
                (None, remote(src, dst, z_send.at[w, 0], recv, (dp, at(1 - side), col))),
                (middle, remote(src, dst, z_send.at[w, 1], recv, (dp, at(2), col))),
            ]
        onward = at(2) if k == 1 else at(0)
        return [(middle, remote(src, dst, z_send.at[w, k + 1], recv, (dp, onward, col)))]

    def first_copies(w, k):
        out = []
        for half, target in ((0, across), (1, along)):
            out.append(
                remote(source(w, k, half), place(w, order[k], dp, half), s1_send.at[w, k, half],
                       s1_recv.at[w, k, half], (target, row, col))
            )
        return out

    def second_copies(w, k, which):
        out = []
        for half, target, other in ((0, along, across), (1, across, along)):
            if which == 0:
                src, owner = source(w, k, half), dp
            else:
                src, owner = place(w, order[k], other, half), other
            out.append(
                remote(src, place(w, order[k], owner, half), s2_send.at[w, k, which, half],
                       s2_recv.at[w, k, which, half], (target, row, col))
            )
        return out

    def arrived(w, k):
        if k > 0:
            block = place(w, order[k], dp)
            pltpu.make_async_copy(block, block, z_recv.at[w, order[k]]).wait()
        for cond, copy in line_copies(w, k):
            if cond is None:
                copy.start()
            else:
                pl.when(cond)(copy.start)
        for copy in first_copies(w, k) + second_copies(w, k, 0):
            copy.start()

    def passed(w, k):
        for copy in first_copies(w, k):
            copy.wait_recv()
        for copy in second_copies(w, k, 1):
            copy.start()

    def finished(w):
        for k in range(ROWS):
            for which in range(2):
                for copy in second_copies(w, k, which):
                    copy.wait_recv()

    def drained(w, k):
        for cond, copy in line_copies(w, k):
            if cond is None:
                copy.wait_send()
            else:
                pl.when(cond)(copy.wait_send)
        for copy in first_copies(w, k) + second_copies(w, k, 0) + second_copies(w, k, 1):
            copy.wait_send()

    def home(w):
        return pltpu.make_async_copy(own[w], place(w, row, dp), l_sem.at[w])

    def begin(w):
        loads[w].wait()
        own[w][...] = stage[w][...].astype(BF)
        arrived(w, 0)
        home(w).start()

    small_home = pltpu.make_async_copy(small_ref, smalls.at[me], l_sem.at[N_W])
    small_home.start()
    begin(QKV)
    for step in range(1, ROWS * DPS):
        small_copy(step).start()
    token_start(0)
    begin(DENSE)
    passed(QKV, 0)
    begin(UP)
    begin(DOWN)
    passed(DENSE, 0)
    arrived(QKV, 1)
    arrived(DENSE, 1)
    passed(QKV, 1)
    passed(DENSE, 1)
    passed(UP, 0)
    passed(DOWN, 0)
    token_spread(0)
    arrived(QKV, 2)
    arrived(DENSE, 2)
    token_start(1)
    token_finish(0)
    small_home.wait()
    for step in range(1, ROWS * DPS):
        small_copy(step).wait()
    read_gains(smalls, gains)
    if aligned:
        read_bias(smalls, bias_row, 9, bias_row.shape[1] // DPS)
    else:
        bias_row[...] = bias_in[...]
    norm_stage(x_ref, gains, 0, first, first_t)
    passed(QKV, 2)
    passed(DENSE, 2)
    arrived(QKV, 3)
    arrived(DENSE, 3)
    passed(QKV, 3)
    passed(DENSE, 3)
    arrived(UP, 1)
    arrived(DOWN, 1)
    home(QKV).wait()
    finished(QKV)
    keep_x = pltpu.make_async_copy(x_ref, x_out, l_sem.at[N_W])
    keep_wq = pltpu.make_async_copy(wq, gq_ref, l_sem.at[QKV])
    keep_x.start()
    keep_wq.start()
    project_stage(wq, first, bias_row, angles, q_t, k_t, v_t, k_n, v_n, heads)
    passed(UP, 1)
    passed(DOWN, 1)
    token_spread(1)
    arrived(UP, 2)
    home(DENSE).wait()
    finished(DENSE)
    token_finish(1)
    keep_c = pltpu.make_async_copy(c_ref, c_out, l_sem.at[N_W + 1])
    keep_wd = pltpu.make_async_copy(wd, gd_ref, l_sem.at[DENSE])
    keep_smalls = pltpu.make_async_copy(smalls, smalls_out, l_sem.at[N_W + 2])
    keep_c.start()
    keep_wd.start()
    keep_smalls.start()
    upstream_stage(wd, c_ref, up_t, heads)
    prefix = prefix_ref[0]

    services = [
        lambda: arrived(DOWN, 2),
        lambda: passed(UP, 2),
        lambda: passed(DOWN, 2),
        lambda: arrived(UP, 3),
        lambda: arrived(DOWN, 3),
        lambda: passed(UP, 3),
        lambda: passed(DOWN, 3),
    ]

    def head_body(h, carry):
        for n, service in enumerate(services):
            if n < heads - 1:
                pl.when(h == n)(service)
        attend_head(h, prefix, angles, q_t, k_t, v_t, k_n, v_n, up_t, att_t, gm_t, grad_q, grad_k, grad_v)
        return carry

    lax.fori_loop(0, heads, head_body, 0)
    for service in services[max(heads - 1, 0) :]:
        service()

    width = gm_t.shape[0]
    wide = min(512, width)
    keep_gm = pltpu.make_async_copy(gm_t, gm_out, l_sem.at[N_W + 3])
    keep_gm.start()

    def qkv_body(i, carry):
        rows = span(i * 256, 256, 256)
        for n in range(width // wide):
            wgq_ref[rows, n * wide : (n + 1) * wide] = nt(first_t[rows, :], gm_t[n * wide : (n + 1) * wide, :]).astype(BF)
        return carry

    lax.fori_loop(0, D // 256, qkv_body, 0)
    keep_wgq = pltpu.make_async_copy(wgq_ref, wgq_out, l_sem.at[N_W + 4])
    keep_wgq.start()
    group = min(heads, 4)

    def dense_body(i, carry):
        block = att_t[pl.ds(i * group, group)].reshape(group * HD, SEQ_LEN)
        spot = pl.ds(0, group * HD) if heads == group else span(i * group * HD, group * HD, 128)
        wgd_ref[spot, :] = nn(block, c_ref[...]).astype(BF)
        att_ref[:, spot] = block.T
        return carry

    lax.fori_loop(0, heads // group, dense_body, 0)
    keep_wgd = pltpu.make_async_copy(wgd_ref, wgd_out, l_sem.at[N_W + 5])
    keep_att = pltpu.make_async_copy(att_ref, att_out, l_sem.at[N_W + 6])
    keep_wgd.start()
    keep_att.start()

    for w in (UP, DOWN):
        finished(w)
        home(w).wait()
    for w in range(N_W):
        for k in range(ROWS):
            drained(w, k)
    for kind in range(2):
        token_drain(kind)
    for keep in (keep_x, keep_wq, keep_c, keep_wd, keep_smalls, keep_gm, keep_wgq, keep_wgd, keep_att):
        keep.wait()


def gather(prefix_len, tokens_in, cotangent, small, angles, bias, weights, cols, aligned):
    wq, wu, wd, wp = weights
    n_q, n_u = wq.shape[1], wu.shape[1]
    heads = n_q // 192
    width = heads * HD
    any_spec = pl.BlockSpec(memory_space=pl.ANY)
    vmem = pl.BlockSpec(memory_space=pltpu.VMEM)
    smem = pl.BlockSpec(memory_space=pltpu.SMEM)
    shape = jax.ShapeDtypeStruct
    smalls = (ROWS * DPS,) + small.shape
    out_shape = [
        shape((SEQ_LEN, D), BF), shape((SEQ_LEN, D), BF), shape(smalls, F32),
        shape((D, n_q), BF), shape((D, n_u), BF), shape((width, D), BF), shape((wp.shape[0] * DPS, D), BF),
        shape((D, n_q), BF), shape((width, D), BF), shape((n_q, SEQ_LEN), BF), shape((SEQ_LEN, width), BF),
    ]
    tok_col = tokens_in.shape[0]
    pieces = tok_col // (SEQ_LEN // cols)
    dma = pltpu.SemaphoreType.DMA
    buf = pltpu.VMEM
    turned = buf((heads, HD, SEQ_LEN), BF)
    plain = buf((heads, SEQ_LEN, HD), BF)
    scratch = [buf(w.shape, BF) for w in weights] + [buf(w.shape, F32) for w in weights]
    scratch += [
        buf((SEQ_LEN, D), BF), buf((SEQ_LEN, D), BF), buf(smalls, F32), buf((D, n_q), BF), buf((width, D), BF),
        buf((8, D), F32), buf((1, n_q), F32), buf((SEQ_LEN, D), BF), buf((D, SEQ_LEN), BF),
        turned, turned, turned, plain, plain, turned, turned, buf((n_q, SEQ_LEN), BF),
        buf((HD, SEQ_LEN), F32), buf((HD, SEQ_LEN), F32), buf((HD, SEQ_LEN), F32),
        buf((D, n_q), BF), buf((width, D), BF), buf((SEQ_LEN, width), BF),
        dma((N_W, 5)), dma((N_W, 4)), dma((N_W, 4, 2)), dma((N_W, 4, 2)), dma((N_W, 4, 2, 2)), dma((N_W, 4, 2, 2)),
        dma((2, pieces)), dma((2, 4)), dma((2, cols - 1)), dma((2, cols - 1)),
        dma((ROWS * DPS - 1,)), dma((ROWS * DPS - 1,)), dma((N_W + 7,)),
    ]
    return pl.pallas_call(
        functools.partial(gather_kernel, cols, aligned),
        out_shape=out_shape,
        in_specs=[smem, any_spec, any_spec, any_spec, vmem, vmem] + [any_spec] * 4,
        out_specs=[any_spec] * 11,
        scratch_shapes=scratch,
        compiler_params=pltpu.CompilerParams(collective_id=0, has_side_effects=True, vmem_limit_bytes=60 << 20),
    )(prefix_len, tokens_in, cotangent, small, angles, bias, wq, wu, wd, wp)


def add_into(dst, src):
    shape = dst.shape
    outer, height = shape[:-2], shape[-2]
    step = min(32, height)
    per = height // step
    total = math.prod(outer) * per

    def body(i, carry):
        index, rest = [], i // per
        for size in reversed(outer):
            index.append(lax.rem(rest, size))
            rest = rest // size
        where = tuple(reversed(index)) + (span(lax.rem(i, per) * step, step, step),)
        dst[where] = (dst[where].astype(F32) + src[where].astype(F32)).astype(BF)
        return carry

    lax.fori_loop(0, total, body, 0)


def pieces_of(n_q, n_u, h_d, h_p):
    out = [(DENSE, 0, h_d // 2)]
    for w, n in ((QKV, n_q), (UP, n_u)):
        size = 512 if n % 512 == 0 else n
        out += [(w, start, size) for start in range(0, n, size)]
    half = h_p // 2
    size = 64 if half % 64 == 0 else half
    return out + [(DOWN, start, size) for start in range(0, half, size)]


def gelu_parts(x):
    below = 0.5 * (1.0 + lax.erf(x * (0.5**0.5)))
    density = jnp.exp(-0.5 * x * x) * (1.0 / math.sqrt(2.0 * math.pi))
    return x * below, below + x * density


def scatter_kernel(cols, aligned, pieces, *refs):
    n_p = len(pieces)
    (x_in, c_in, smalls, wu_in, wp_in, wq_in, wd_in, gq_in, gd_in, gm_in, att_in, ub_in) = refs[:12]
    (lo_out, gt_out, oq, ou, od, op, sm_out) = refs[12:19]
    (wu, wp, x_ref, c_ref, second, second_t, hid_t, ghp, gu, gp, branch, comb, branch_got, comb_got) = refs[19:33]
    (gains, bias_row, out_bias, sm, sm_got, gain_sum, att_spare, wq_spare) = refs[33:41]
    mine_q, mine_d = refs[41:43], refs[43:45]
    base = 45
    got1 = [refs[base + 2 * i : base + 2 * i + 2] for i in range(n_p)]
    base += 2 * n_p
    got2 = [refs[base + 2 * i : base + 2 * i + 2] for i in range(n_p)]
    base += 2 * n_p
    got_end = [refs[base + 2 * i : base + 2 * i + 2] for i in range(n_p)]
    base += 2 * n_p
    got_mid = [refs[base + 2 * i : base + 2 * i + 2] for i in range(n_p)]
    base += 2 * n_p
    got_back = [refs[base + 2 * i : base + 2 * i + 2] for i in range(n_p)]
    base += 2 * n_p
    (l_sem, f_sem, s1_send, s1_recv, s2_send, s2_recv, e_send, e_recv, m_send, m_recv, b_send, b_recv, d_send, d_recv,
     t_send, t_recv, v_send, v_recv) = refs[base:]
    dp, row, col, across, along = places()
    x, y = lax.rem(dp, 2), dp // 2
    side, at = line_order(row)
    far_end = row // 2
    middle, end = side == 1, side == 0
    n_q, n_u = wq_in.shape[1], wu_in.shape[1]
    tok_col = lo_out.shape[0]
    part = SEQ_LEN // cols
    width = ghp.shape[1]
    blocks = n_u // width

    def load(src, dst, n):
        return pltpu.make_async_copy(src, dst, l_sem.at[n])

    att_width = att_in.shape[1]
    att_buf = ghp.at[:, pl.ds(0, att_width)] if att_width % 128 == 0 else att_spare
    wq_buf = wu.at[:, pl.ds(0, n_q)] if n_q % 128 == 0 else wq_spare
    loads = [
        load(x_in, x_ref, 0), load(att_in, att_buf, 1), load(wd_in, hid_t.at[pl.ds(0, att_width), :], 2),
        load(c_in, c_ref, 3), load(wu_in, wu.at[:, pl.ds(0, n_u)], 4), load(wp_in, wp.at[pl.ds(0, n_u), :], 5),
    ]
    for one in loads:
        one.start()
    group = [(dp, lax.rem(row + step, ROWS), lax.rem(col + other, cols)) for step in range(ROWS) for other in range(cols)]
    greet([(across, row, col), (along, row, col)] + group[1:])

    def view(i, half, other):
        w, start, size = pieces[i]
        if half == 0:
            place_y, place_x = (1 - y if other else y), slice(None)
        else:
            place_y, place_x = slice(None), (1 - x if other else x)
        cut = pl.ds(start, size)
        if w in (QKV, UP):
            if w == QKV and not other:
                return mine_q[half].at[:, :, :, cut]
            return (gq_in if w == QKV else gu).at[:, place_y, place_x, half, :, cut]
        if w == DENSE and not other:
            return mine_d[half].at[:, cut, :]
        return (gd_in if w == DENSE else gp).at[place_y, place_x, half, cut, :]

    def fetch(i, half):
        w, start, size = pieces[i]
        place_y, place_x = (y, slice(None)) if half == 0 else (slice(None), x)
        cut = pl.ds(start, size)
        src = gq_in.at[:, place_y, place_x, half, :, cut] if w == QKV else gd_in.at[place_y, place_x, half, cut, :]
        return pltpu.make_async_copy(src, view(i, half, False), f_sem.at[i, half])

    def first(i, half):
        target = along if half == 0 else across
        return remote(view(i, half, True), got1[i][half], s1_send.at[i, half], s1_recv.at[i, half], (target, row, col))

    def keep(i, half, other):
        which = x if half == 0 else y
        which = 1 - which if other else which
        kept = view(i, half, False)
        return kept.at[:, which] if pieces[i][0] in (QKV, UP) else kept.at[which]

    def second_copy(i, half):
        target = across if half == 0 else along
        return remote(keep(i, half, True), got2[i][half], s2_send.at[i, half], s2_recv.at[i, half], (target, row, col))

    def lines(i, ref, start, count):
        if pieces[i][0] in (QKV, UP):
            return ref.at[pl.ds(start, count)]
        return ref.at[:, span(start * 256, count * 256, 256)]

    def end_copy(i, half):
        src = lines(i, keep(i, half, False), 1 - far_end, 3)
        return remote(src, got_end[i][half], e_send.at[i, half], e_recv.at[i, half], (dp, at(1), col))

    def mid_copy(i, half):
        src = lines(i, keep(i, half, False), 2 * (1 - far_end), 2)
        return remote(src, got_mid[i][half], m_send.at[i, half], m_recv.at[i, half], (dp, at(2), col))

    def back_copy(i, half):
        src = lines(i, keep(i, half, False), at(0), 1)
        return remote(src, got_back[i][half], b_send.at[i, half], b_recv.at[i, half], (dp, at(0), col))

    def begin(i):
        for half in range(2):
            first(i, half).start()
            if pieces[i][0] in (QKV, DENSE):
                fetch(i, half).start()

    def stage_two(i):
        for half in range(2):
            if pieces[i][0] in (QKV, DENSE):
                fetch(i, half).wait()
            first(i, half).wait_recv()
            add_into(view(i, half, False), got1[i][half])
            second_copy(i, half).start()

    def stage_three(i):
        for half in range(2):
            second_copy(i, half).wait_recv()
            add_into(keep(i, half, False), got2[i][half])

            @pl.when(end)
            def _():
                end_copy(i, half).start()

    def stage_four(i):
        @pl.when(middle)
        def _():
            for half in range(2):
                end_copy(i, half).wait_recv()
                add_into(lines(i, keep(i, half, False), 2 * (1 - far_end), 2), lines(i, got_end[i][half], 1 - far_end, 2))
                mid_copy(i, half).start()

    def stage_five(i):
        @pl.when(middle)
        def _():
            for half in range(2):
                mid_copy(i, half).wait_recv()
                add_into(lines(i, keep(i, half, False), at(0), 1), lines(i, got_mid[i][half], far_end, 1))
                back_copy(i, half).start()

    def stage_six(i):
        w, start, size = pieces[i]
        out = (oq, ou, od, op)[w]
        for half in range(2):
            mine = lines(i, keep(i, half, False), row, 1)

            def total(others):
                if w in (QKV, UP):
                    value = mine[0].astype(F32)
                    for other in others:
                        value = value + other[0].astype(F32)
                    out[half, :, pl.ds(start, size)] = value
                else:
                    value = mine[...].astype(F32)
                    for other in others:
                        value = value + other[...].astype(F32)
                    out[half, pl.ds(start, size), :] = value

            @pl.when(end)
            def _():
                back_copy(i, half).wait_recv()
                total([got_back[i][half]])

            @pl.when(middle)
            def _():
                total([lines(i, got_end[i][half], 2 * far_end, 1), lines(i, got_mid[i][half], 1 - far_end, 1)])

    def drain(i):
        for half in range(2):
            first(i, half).wait_send()
            second_copy(i, half).wait_send()

            @pl.when(end)
            def _():
                end_copy(i, half).wait_send()

            @pl.when(middle)
            def _():
                mid_copy(i, half).wait_send()
                back_copy(i, half).wait_send()

    ahead, lag = 2, (0, 2, 3, 4, 5)
    stages = (stage_two, stage_three, stage_four, stage_five, stage_six)

    def step(s):
        for stage, late in zip(stages, lag):
            if 0 <= s - late < n_p:
                stage(s - late)
            if stage is stage_two and ahead <= s + ahead < n_p:
                begin(s + ahead)

    def part_rows(piece):
        return span(piece * part, part, part)

    def col_copy(kind, n):
        other = lax.rem(col + n, cols)
        src = (branch, comb)[kind].at[part_rows(other), :]
        dst = (branch_got, comb_got)[kind].at[n - 1]
        return remote(src, dst, d_send.at[kind, n - 1], d_recv.at[kind, n - 1], (dp, row, other))

    start = row * SEQ_LEN + col * part
    owner, offset = start // tok_col, lax.rem(start, tok_col)

    def out_copy(kind, r):
        src = second.at[pl.ds(kind * part, part), pl.ds(r * 256, 256)]
        dst = (lo_out, gt_out)[kind].at[span(offset, part, part), :]
        recv = t_recv.at[kind, offset // part]
        here = jnp.logical_and(row == r, owner == col)
        far = remote(src, dst, t_send.at[kind, r], recv, (dp, r, owner))
        return here, far, pltpu.make_async_copy(src, dst, recv)

    def out_start(kind):
        for r in range(ROWS):
            here, far, near = out_copy(kind, r)
            pl.when(jnp.logical_not(here))(far.start)
            pl.when(here)(near.start)

    def out_finish(kind):
        for r in range(ROWS):
            here, far, near = out_copy(kind, r)
            pl.when(jnp.logical_not(here))(far.wait_send)
        out = (lo_out, gt_out)[kind]
        for n in range(tok_col // part):
            block = out.at[pl.ds(n * part, part), :]
            pltpu.make_async_copy(block, block, t_recv.at[kind, n]).wait()

    height = min(128, part)

    def finish_rows(kind):
        for n in range(1, cols):
            col_copy(kind, n).wait_recv()

        def body(i, carry):
            here = span(i * height, height, height)
            rows = span(col * part + i * height, height, height)
            value = (branch, comb)[kind][rows, :]
            for n in range(1, cols):
                value = value + (branch_got, comb_got)[kind][n - 1, here, :]
            wide = x_ref[rows, :].astype(F32)
            if kind == 0:
                value = wide + value + out_bias[0:1, :]
            else:
                normed, scale_inv = norm_rows(wide)
                mean = jnp.mean(value, axis=1, keepdims=True)
                cross = jnp.mean(value * normed, axis=1, keepdims=True)
                value = c_ref[rows, :].astype(F32) + scale_inv * (value - mean - normed * cross)
            second[span(kind * part + i * height, height, height), :] = value.astype(BF)
            return carry

        lax.fori_loop(0, part // height, body, 0)

    def small_copy(n):
        if n < 2:
            return remote(sm.at[n], sm_got.at[n], v_send.at[n], v_recv.at[n], ((across, along)[n], row, col))
        if n < 5:
            target = (dp, lax.rem(row + n - 1, ROWS), col)
            return remote(sm.at[2], sm_got.at[n], v_send.at[n], v_recv.at[n], target)
        target = (dp, row, lax.rem(col + n - 4, cols))
        return remote(sm.at[3], sm_got.at[n], v_send.at[n], v_recv.at[n], target)

    def small_step(n):
        if n > 0:
            waits = ((0,), (1,), (2, 3, 4), tuple(range(5, 4 + cols)))[n - 1]
            for m in waits:
                small_copy(m).wait_recv()
            value = sm[n - 1]
            if n < 4:
                for m in waits:
                    value = value + sm_got[m]
                sm[n] = value
            else:
                sm_out[...] = value
                value = value[0:4]
                for m in waits:
                    value = value + sm_got[m, 0:4, :]
                sm_out[0:4, :] = value
        for m in ((0,), (1,), (2, 3, 4), tuple(range(5, 4 + cols)), ())[n]:
            small_copy(m).start()

    for i in range(min(ahead, n_p)):
        begin(i)

    read_gains(smalls, gains)
    lanes = lax.broadcasted_iota(jnp.int32, (1, 128), 1)
    for r in range(ROWS):
        for d in range(0, DPS, 2):
            pair = jnp.where(lanes < 64, smalls[r * DPS + d, 8:9, :], smalls[r * DPS + d + 1, 8:9, :])
            out_bias[0:1, pl.ds(r * 256 + d * 64, 128)] = pair
    if aligned:
        read_bias(smalls, bias_row, 9 + n_q // (DPS * 128), n_u // DPS)
    else:
        bias_row[...] = ub_in[...]
    loads[0].wait()
    norm_stage(x_ref, gains, 2, second, second_t)
    loads[1].wait()
    loads[2].wait()
    for j in range(SEQ_LEN // 256):
        rows = pl.ds(j * 256, 256)
        branch[rows, :] = nn(att_buf[rows, :], hid_t[0:att_width, :])
    for one in loads[3:]:
        one.wait()
    sm[0] = jnp.zeros(sm.shape[1:], F32)

    def feed(n):
        cut = span(n * width, width, width)

        def body(j, carry):
            rows = span(j * 256, 256, 256)
            pre = nn(second[rows, :], wu[:, cut]) + bias_row[0:1, cut]
            grad = nt(c_ref[rows, :], wp[cut, :])
            hidden, slope = gelu_parts(pre)
            hidden = hidden.astype(BF)
            grad = (grad * slope).astype(BF)
            hid_t[0:width, rows] = hidden.T
            ghp[rows, 0:width] = grad
            branch[rows, :] += nn(hidden, wp[cut, :])
            back = nt(grad, wu[:, cut])

            @pl.when(n == 0)
            def _():
                comb[rows, :] = back

            @pl.when(n > 0)
            def _():
                comb[rows, :] += back

            sm[0, 6:7, cut] += jnp.sum(grad.astype(F32), axis=0, keepdims=True)
            return carry

        lax.fori_loop(0, SEQ_LEN // 256, body, 0)

        def up_body(r, carry):
            value = nn(second_t[span(r * 256, 256, 256), :], ghp[:, 0:width]).astype(BF)
            gu[r, :, :, :, :, cut] = value.reshape(2, 2, 2, 32, width)
            return carry

        lax.fori_loop(0, ROWS, up_body, 0)
        h = gp.shape[3]
        if blocks == DPS:
            for half in range(2):
                gp[n // 2, lax.rem(n, 2), half] = nn(hid_t[half * h : (half + 1) * h, :], c_ref[...]).astype(BF)
        else:
            gp[...] = nn(hid_t[0:width, :], c_ref[...]).astype(BF).reshape(2, 2, 2, h, D)

    def feed_body(n, carry):
        feed(n)
        for s in range(blocks):
            pl.when(n == s)(functools.partial(step, s))
        return carry

    lax.fori_loop(0, blocks, feed_body, 0)
    load_wq = load(wq_in, wq_buf, 4)
    load_gm = load(gm_in, wp.at[pl.ds(0, n_q), :], 5)
    load_wq.start()
    load_gm.start()
    for n in range(1, cols):
        col_copy(0, n).start()
    step(blocks)
    load_wq.wait()
    load_gm.wait()
    for n in range(8):
        gain_sum[n : n + 1, :] = jnp.zeros((1, D), F32)

    def first_body(j, carry):
        rows = span(j * 256, 256, 256)
        grad = wp[0:n_q, rows].T
        grad_first = nt(grad, wq_buf[...])
        grad_second = comb[rows, :]
        normed, ignored = norm_rows(x_ref[rows, :].astype(F32))
        for n, value in enumerate((normed * grad_first, grad_first, normed * grad_second, grad_second,
                                   c_ref[rows, :].astype(F32))):
            gain_sum[n : n + 1, :] += jnp.sum(value, axis=0, keepdims=True)
        sm[0, 5:6, 0:n_q] += jnp.sum(grad.astype(F32), axis=0, keepdims=True)
        comb[rows, :] = gains[0:1, :] * grad_first + gains[2:3, :] * grad_second
        return carry

    lax.fori_loop(0, SEQ_LEN // 256, first_body, 0)
    for n in range(1, cols):
        col_copy(1, n).start()
    sm[0, 0:5, 0:D] = gain_sum[0:5, :]
    small_step(0)
    finish_rows(0)
    out_start(0)
    step(blocks + 1)
    finish_rows(1)
    out_start(1)
    small_step(1)
    step(blocks + 2)
    small_step(2)
    step(blocks + 3)
    small_step(3)
    step(blocks + 4)
    small_step(4)
    for s in range(blocks + 5, n_p + lag[-1]):
        step(s)
    for i in range(n_p):
        drain(i)
    for kind in range(2):
        out_finish(kind)
        for n in range(1, cols):
            col_copy(kind, n).wait_send()
    for n in range(4 + cols):
        small_copy(n).wait_send()


def scatter(own_x, own_cot, smalls, wu, wp, wq, wd, wgrad_q, wgrad_d, grad_mixed, attended, u_bias, cols, aligned, tok_col):
    any_spec = pl.BlockSpec(memory_space=pl.ANY)
    vmem = pl.BlockSpec(memory_space=pltpu.VMEM)
    dma = pltpu.SemaphoreType.DMA
    buf = pltpu.VMEM
    shape = jax.ShapeDtypeStruct
    n_q, n_u = wq.shape[1], wu.shape[1]
    h_d, h_p = wd.shape[0] // DPS, wp.shape[0] // DPS
    pieces = pieces_of(n_q, n_u, h_d, h_p)
    n_p = len(pieces)
    part = SEQ_LEN // cols
    width = 512 if n_u % (DPS * 512) == 0 and n_u == DPS * 512 else n_u
    most = max(n_q, n_u)
    line = max(most, D)
    block = max(width, wd.shape[0])
    scratch = [
        buf((D, most), BF), buf((most, D), BF), buf((SEQ_LEN, D), BF), buf((SEQ_LEN, D), BF), buf((SEQ_LEN, D), BF),
        buf((D, SEQ_LEN), BF), buf((block, SEQ_LEN), BF), buf((SEQ_LEN, block), BF),
        buf((ROWS, 2, 2, 2, 32, n_u), BF), buf((2, 2, 2, h_p // 2, D), BF), buf((SEQ_LEN, D), F32), buf((SEQ_LEN, D), F32),
        buf((cols - 1, part, D), F32), buf((cols - 1, part, D), F32),
        buf((8, D), F32), buf((1, n_u), F32), buf((1, D), F32), buf((4, 8, line), F32), buf((4 + cols, 8, line), F32),
        buf((8, D), F32), buf((SEQ_LEN, wd.shape[0]) if wd.shape[0] % 128 else (8, 128), BF),
        buf((D, n_q) if n_q % 128 else (8, 128), BF),
    ]
    scratch += [buf((ROWS, 2, 32, n_q), BF)] * 2 + [buf((2, h_d // 2, D), BF)] * 2
    wide = [w in (QKV, UP) for w, start, size in pieces]
    sizes = [size for w, start, size in pieces]
    for lead, count in (((ROWS, 2), None), ((ROWS,), None), ((3,), 3), ((2,), 2), ((1,), 1)):
        for is_wide, size in zip(wide, sizes):
            if is_wide:
                one = lead + (32, size)
            elif count is None:
                one = ((2,) if len(lead) == 2 else ()) + (size, D)
            else:
                one = (size, 256 * count)
            scratch += [buf(one, BF)] * 2
    scratch += [
        dma((6,)), dma((n_p, 2)), dma((n_p, 2)), dma((n_p, 2)), dma((n_p, 2)), dma((n_p, 2)), dma((n_p, 2)), dma((n_p, 2)),
        dma((n_p, 2)), dma((n_p, 2)), dma((n_p, 2)), dma((n_p, 2)), dma((2, cols - 1)), dma((2, cols - 1)),
        dma((2, ROWS)), dma((2, tok_col // part)), dma((4 + cols,)), dma((4 + cols,)),
    ]
    return pl.pallas_call(
        functools.partial(scatter_kernel, cols, aligned, pieces),
        out_shape=[
            shape((tok_col, 256), BF), shape((tok_col, 256), BF), shape((2, 32, n_q), F32), shape((2, 32, n_u), F32),
            shape((2, h_d // 2, 256), F32), shape((2, h_p // 2, 256), F32), shape((8, line), F32),
        ],
        in_specs=[any_spec] * 2 + [vmem] + [any_spec] * 8 + [vmem],
        out_specs=[any_spec] * 2 + [vmem] * 5,
        scratch_shapes=scratch,
        compiler_params=pltpu.CompilerParams(collective_id=1, has_side_effects=True, vmem_limit_bytes=63 << 20),
    )(own_x, own_cot, smalls, wu, wp, wq, wd, wgrad_q.reshape(ROWS, 2, 2, 2, 32, n_q),
      wgrad_d.reshape(2, 2, 2, h_d // 2, D), grad_mixed, attended, u_bias)


def angles_table():
    half_rot = ROT // 2
    places_ = jnp.arange(SEQ_LEN, dtype=F32)
    rates = jnp.exp(jnp.arange(half_rot, dtype=F32) * (-2.0 * math.log(10000.0) / ROT))
    turned = places_[:, None] * rates[None, :]
    return (jnp.cos(turned), jnp.sin(turned))


def shards(cols, tokens_in, prefix_len, first_gain, first_shift, second_gain, second_shift, qkv_weight, qkv_bias,
           up_weight, up_bias, dense_weight, dense_bias, down_weight, down_bias, cotangent):
    tok_col = tokens_in.shape[0]
    n_q, n_u = qkv_weight.shape[1], up_weight.shape[1]
    h_d, h_p = dense_weight.shape[0], down_weight.shape[0]

    out_part = dense_bias.astype(BF).astype(F32) + down_bias.astype(BF).astype(F32)
    q_part, u_part = qkv_bias.astype(BF).astype(F32), up_bias.astype(BF).astype(F32)
    n_qb, n_ub = q_part.shape[0], u_part.shape[0]
    aligned = n_qb % 128 == 0 and n_ub % 128 == 0
    small = jnp.concatenate((first_gain, first_shift, second_gain, second_shift, out_part, out_part, q_part, u_part))
    size = -(-small.shape[0] // 1024) * 1024
    small = jnp.pad(small, (0, size - small.shape[0])).reshape(size // 128, 128)
    if aligned:
        q_bias, u_bias = jnp.zeros((1, n_q), F32), jnp.zeros((1, n_u), F32)
    else:
        q_bias = lax.all_gather(q_part, "dp", axis=0, tiled=True).reshape(1, n_q)
        u_bias = lax.all_gather(u_part, "dp", axis=0, tiled=True).reshape(1, n_u)
    cos_table, sin_table = angles_table()
    angles = jnp.concatenate([cos_table.T, sin_table.T], axis=0)
    own_x, own_cot, smalls, wq, wu, wd, wp, wgrad_q, wgrad_d, grad_mixed, attended = gather(
        prefix_len, tokens_in, cotangent, small, angles, q_bias, (qkv_weight, up_weight, dense_weight, down_weight), cols,
        aligned
    )
    layer_out, grad_tokens, out_q, out_u, out_d, out_p, sums = scatter(
        own_x, own_cot, smalls, wu, wp, wq, wd, wgrad_q, wgrad_d, grad_mixed, attended, u_bias, cols, aligned, tok_col
    )
    dp, row = lax.axis_index("dp"), lax.axis_index("row")
    gain_sums = lax.dynamic_slice(sums, (0, row * 256), (4, 256))
    out_b = lax.dynamic_slice(sums, (4, (row * DPS + dp) * 64), (1, 64))[0]
    q_b = lax.dynamic_slice(sums, (5, dp * n_qb), (1, n_qb))[0]
    u_b = lax.dynamic_slice(sums, (6, dp * n_ub), (1, n_ub))[0]
    return (
        layer_out, grad_tokens, out_q.reshape(64, n_q), q_b, out_u.reshape(64, n_u), u_b,
        out_d.reshape(h_d, 256), out_b, out_p.reshape(h_p, 256), out_b,
        gain_sums[0], gain_sums[1], gain_sums[2], gain_sums[3],
    )


def solution(mesh):
    in_specs = (
        P(("dp", "col"), "row"), P(("dp", "row")), P("row"), P("row"), P("row"), P("row"),
        P(("row", "dp"), "col"), P(("col", "dp")), P(("row", "dp"), "col"), P(("col", "dp")),
        P(("col", "dp"), "row"), P(("row", "dp")), P(("col", "dp"), "row"), P(("row", "dp")),
        P(("dp", "col"), "row"),
    )
    out_specs = (
        P(("dp", "col"), "row"), P(("dp", "col"), "row"), P(("row", "dp"), "col"), P(("col", "dp")),
        P(("row", "dp"), "col"), P(("col", "dp")), P(("col", "dp"), "row"), P(("row", "dp")),
        P(("col", "dp"), "row"), P(("row", "dp")), P("row"), P("row"), P("row"), P("row"),
    )
    body = functools.partial(shards, mesh.shape["col"])
    return jax.shard_map(body, mesh=mesh, in_specs=in_specs, out_specs=out_specs, check_vma=False)
```

```python
import functools
import math

import jax
import jax.numpy as jnp
import numpy as np
from jax import lax
from jax.experimental import pallas as pl
from jax.experimental.pallas import tpu as pltpu
from jax.sharding import PartitionSpec as P

D = 1024
HD = 64
ROT = 16
FF = 4096
SEQ_LEN = 1024
EPS = 1e-05
NEGATIVE = -1e30
ROWS = 4
DPS = 4
MESH = pl.DeviceIdType.MESH
BF = jnp.bfloat16
F32 = jnp.float32


def places():
    dp, row, col = lax.axis_index("dp"), lax.axis_index("row"), lax.axis_index("col")
    across = dp + 1 - 2 * lax.rem(dp, 2)
    along = lax.rem(dp + 2, 4)
    return dp, row, col, across, along


def line_order(row):
    far = row // 2
    side = row + far * (3 - 2 * row)
    at = lambda place: far * 3 + (1 - 2 * far) * place
    return side, at


def greet(targets):
    barrier = pltpu.get_barrier_semaphore()
    for target in targets:
        pl.semaphore_signal(barrier, inc=1, device_id=target, device_id_type=MESH)
    pl.semaphore_wait(barrier, len(targets))


def peers_of(dp, row, col, cols):
    group = []
    for step in range(1, ROWS * cols):
        flat = lax.rem(row * cols + col + step, ROWS * cols)
        group.append((dp, flat // cols, lax.rem(flat, cols)))
    for step in range(1, DPS):
        for other in range(ROWS):
            group.append((lax.rem(dp + step, DPS), lax.rem(row + other, ROWS), col))
    return group


def remote(src, dst, send, recv, target):
    return pltpu.make_async_remote_copy(
        src_ref=src, dst_ref=dst, send_sem=send, recv_sem=recv, device_id=target, device_id_type=MESH
    )


N_W = 4
QKV, UP, DENSE, DOWN = range(N_W)
BEFORE = (
    "b1", "z10", "b0", "b3", "b2", "z20", "s10", "z11", "s11", "z12", "z30", "m", "s12", "z13", "s30", "t0", "z31",
    "p10", "p11", "s31", "s13", "s00", "p31", "z32", "t1", "p12", "p13", "s32", "z33", "s20", "d0", "z00", "p30",
    "z21", "s33", "N", "p32",
)
BETWEEN = (
    ("d1",),
    (),
    (),
    ("z01", "p33",),
    ("s01",),
    ("s21",),
    ("z02", "p00",),
    ("s02", "z22", "z23",),
    (),
    ("z03",),
    (),
    ("s23",),
    (),
    ("p23", "s22", "p20", "p21",),
    (),
    ("p22", "p02", "s03",),
    ("p01",),
    (),
    (),
    ("p03",),
)


def nt(left, right):
    return lax.dot_general(left, right, (((1,), (1,)), ((), ())), preferred_element_type=F32)


def nn(left, right):
    return jnp.dot(left, right, preferred_element_type=F32)


def span(start, size, unit):
    return pl.ds(pl.multiple_of(start, unit), size)


def slot(w, ref, row, dp, height, half=None):
    if w in (QKV, UP):
        if half is None:
            return ref.at[span((row * DPS + dp) * height, height, 64), :]
        return ref.at[span((row * DPS + dp) * height + half * (height // 2), height // 2, 32), :]
    if half is None:
        return ref.at[span(dp * height, height, 16), span(row * 256, 256, 256)]
    if w == DENSE:
        return ref.at[span(dp * height, height, 16), span(row * 256 + half * 128, 128, 128)]
    return ref.at[span(dp * height + half * (height // 2), height // 2, 16), span(row * 256, 256, 256)]


def half_of(w, ref, half):
    height = ref.shape[0]
    if w == DENSE:
        return ref.at[:, pl.ds(half * 128, 128)]
    return ref.at[pl.ds(half * (height // 2), height // 2), :]


def read_gains(smalls, gains):
    for r in range(ROWS):
        for g in range(4):
            for t in range(2):
                gains[g : g + 1, pl.ds(r * 256 + t * 128, 128)] = smalls[r * DPS, pl.ds(2 * g + t, 1), :]


def rounded(value):
    return value.astype(BF).astype(F32)


def read_bias(smalls, bias, first_row, size):
    per = size // 128
    for d in range(DPS):
        for t in range(per):
            bias[0:1, pl.ds(d * size + t * 128, 128)] = rounded(smalls[d, pl.ds(first_row + t, 1), :])


def norm_rows(x):
    center = jnp.mean(x, axis=1, keepdims=True)
    spread = jnp.mean(x * x, axis=1, keepdims=True) - center * center
    scale_inv = lax.rsqrt(spread + EPS)
    return (x - center) * scale_inv, scale_inv


def norm_stage(x_ref, gains, outs):
    def body(i, carry):
        rows = span(i * 128, 128, 128)
        normed, ignored = norm_rows(x_ref[rows, :].astype(F32))
        for which, plain, turned in outs:
            value = (normed * gains[which : which + 1, :] + gains[which + 1 : which + 2, :]).astype(BF)
            plain[rows, :] = value
            turned[:, rows] = value.T
        return carry

    lax.fori_loop(0, SEQ_LEN // 128, body, 0)


def project_stage(wq, first, bias_row, angles, q_t, k_t, v_t, heads):
    pair = min(heads, 2)
    width = 192 * pair

    def body(p, carry):
        cols = pl.ds(0, width) if heads == pair else span(p * width, width, 128)
        w_t = wq[:, cols].T
        bias = jnp.broadcast_to(bias_row[0:1, cols], (8, width)).T[:, 0:1]
        for j in range(SEQ_LEN // 256):
            toks = pl.ds(j * 256, 256)
            mixed = nt(w_t, first[toks, :]) + bias
            cos, sin = angles[0:8, toks], angles[8:16, toks]

            def turn(base):
                x1, x2 = mixed[base : base + 8], mixed[base + 8 : base + 16]
                return jnp.concatenate([x1 * cos - x2 * sin, x2 * cos + x1 * sin, mixed[base + 16 : base + 64]], axis=0)

            for e in range(pair):
                base, h = 192 * e, pair * p + e
                q_t[h, :, toks] = (turn(base) * HD ** (-0.5)).astype(BF)
                k_t[h, :, toks] = turn(base + 64).astype(BF)
                v_t[h, :, toks] = mixed[base + 128 : base + 192].astype(BF)
        return carry

    lax.fori_loop(0, heads // pair, body, 0)


def upstream_stage(wd, c_ref, up_t, heads):
    for j in range(SEQ_LEN // 256):
        toks = pl.ds(j * 256, 256)
        grad = nt(wd[...], c_ref[toks, :]).astype(BF)
        for h in range(heads):
            up_t[h, :, toks] = grad[HD * h : HD * (h + 1)]


def attend_head(h, prefix, angles, q_t, k_t, v_t, up_t, att_t, gm_t, grad_q, grad_k, grad_v, middle):
    keys_plain, values_plain = k_t[h].T, v_t[h].T
    done = 0
    for i in range(SEQ_LEN // 256):
        if i == 2:
            middle()
        low = 256 * i
        seen = max(512, low + 256)
        spot = pl.ds(low, 256)
        q, up = q_t[h, :, spot], up_t[h, :, spot]
        scores = nn(keys_plain[0:seen], q)
        plain = min(low, seen)
        keys = lax.broadcasted_iota(jnp.int32, (seen - plain, 256), 0) + plain
        queries = lax.broadcasted_iota(jnp.int32, (seen - plain, 256), 1) + low
        masked = jnp.where((keys <= queries) | (keys < prefix), scores[plain:], NEGATIVE)
        scores = jnp.concatenate([scores[:plain], masked], axis=0) if plain else masked
        exponent = jnp.exp(scores - jnp.max(scores, axis=0, keepdims=True))
        probs = exponent * (1.0 / jnp.sum(exponent, axis=0, keepdims=True))
        weights = probs.astype(BF)
        att_t[h, :, spot] = nn(v_t[h, :, 0:seen], weights).astype(BF)
        grad_probs = nn(values_plain[0:seen], up)
        inner = jnp.sum(probs * grad_probs, axis=0, keepdims=True)
        grad_scores = (probs * (grad_probs - inner)).astype(BF)
        grad_q[:, spot] = nn(k_t[h, :, 0:seen], grad_scores)
        for total, part in ((grad_v, nt(up, weights)), (grad_k, nt(q, grad_scores))):
            if done:
                total[:, 0:done] += part[:, :done]
            if seen > done:
                total[:, done:seen] = part[:, done:]
        done = seen
    cos, sin = angles[0:8, :], angles[8:16, :]

    def turn_back(grad):
        g1, g2 = grad[0:8], grad[8:16]
        return jnp.concatenate([g1 * cos + g2 * sin, g2 * cos - g1 * sin, grad[16:]], axis=0)

    base = h * 192
    gm_t[span(base, HD, HD), :] = (turn_back(grad_q[...]) * HD ** (-0.5)).astype(BF)
    gm_t[span(base + HD, HD, HD), :] = turn_back(grad_k[...]).astype(BF)
    gm_t[span(base + 2 * HD, HD, HD), :] = grad_v[...].astype(BF)


def gelu_parts(x):
    below = 0.5 * (1.0 + lax.erf(x * (0.5**0.5)))
    density = jnp.exp(-0.5 * x * x) * (1.0 / math.sqrt(2.0 * math.pi))
    return x * below, below + x * density


def gather_kernel(cols, aligned, *refs):
    (tok_ref, cot_ref, small_ref, bias_in) = refs[:4]
    masters = refs[4:8]
    (x_out, c_out, smalls_out, gq_ref, gd_ref, first_out, first_t_out, gu_out, gp_out, branch_out, comb_out, sum_out) = refs[8:20]
    own = refs[20:24]
    stage = refs[24:28]
    (x_ref, c_ref, smalls, wu, wp, gains, bias_row, second, second_t) = refs[28:37]
    (hidden, slope, ghp, gu, gp, branch, comb) = refs[37:44]
    (z_send, z_recv, s1_send, s1_recv, s2_send, s2_recv, t_send, t_recv, a_send, a_recv, m_send, m_recv, l_sem) = refs[44:]
    full = (gq_ref, wu, gd_ref, wp)
    n_q, n_u = gq_ref.shape[1], wu.shape[1]
    width = ghp.shape[1]
    blocks = n_u // width
    dp, row, col, across, along = places()
    side, at = line_order(row)
    order = [row, at(1 - side), at(2), at(3)]
    middle = side == 1
    tok_col = tok_ref.shape[0]
    part = SEQ_LEN // cols
    chunk = min(tok_col, SEQ_LEN)
    n_seq = tok_col // chunk
    n_part = chunk // part

    loads = [pltpu.make_async_copy(masters[w], stage[w], l_sem.at[w]) for w in range(N_W)]
    for load in loads:
        load.start()
    greet(peers_of(dp, row, col, cols))

    def token_copy(kind, j, i):
        src_ref, dst_ref = ((tok_ref, x_ref), (cot_ref, c_ref))[kind]
        n = j * n_part + i
        if n_seq > 1:
            j = lax.rem(j + (n_seq - 1) * (1 - col), n_seq)
        start = col * tok_col + j * chunk
        to_row = start // SEQ_LEN
        piece = lax.rem(start, SEQ_LEN) // part + i
        src = src_ref.at[span(j * chunk + i * part, part, part), :]
        dst = dst_ref.at[span(piece * part, part, part), span(row * 256, 256, 256)]
        sends, recvs = t_send.at[kind, n], t_recv.at[kind, row]
        is_here = jnp.logical_and(to_row == row, piece == col)
        far = remote(src, dst, sends, recvs, (dp, to_row, piece))
        near = pltpu.make_async_copy(src, dst, recvs)
        return is_here, far, near

    def token_start(kind):
        for j in range(n_seq):
            for i in range(n_part):
                is_here, far, near = token_copy(kind, j, i)
                pl.when(jnp.logical_not(is_here))(far.start)
                pl.when(is_here)(near.start)

    def part_rows(piece):
        return span(piece * part, part, part)

    def spread_copy(kind, step):
        mine = (x_ref, c_ref)[kind].at[part_rows(col), :]
        to_col = lax.rem(col + step, cols)
        return remote(mine, mine, a_send.at[kind, step - 1], a_recv.at[kind, step - 1], (dp, row, to_col))

    def token_spread(kind):
        dst_ref = (x_ref, c_ref)[kind]
        for other in range(ROWS):
            block = dst_ref.at[part_rows(col), pl.ds(other * 256, 256)]
            pltpu.make_async_copy(block, block, t_recv.at[kind, other]).wait()
        for step in range(1, cols):
            spread_copy(kind, step).start()

    def token_finish(kind):
        dst_ref = (x_ref, c_ref)[kind]
        for step in range(1, cols):
            from_col = lax.rem(col + cols - step, cols)
            theirs = dst_ref.at[part_rows(from_col), :]
            pltpu.make_async_copy(theirs, theirs, a_recv.at[kind, step - 1]).wait()

    def token_drain(kind):
        for j in range(n_seq):
            for i in range(n_part):
                is_here, far, near = token_copy(kind, j, i)
                pl.when(jnp.logical_not(is_here))(far.wait_send)
        for step in range(1, cols):
            spread_copy(kind, step).wait_send()

    me = row * DPS + dp

    def small_copy(step):
        flat = lax.rem(me + step, ROWS * DPS)
        return remote(
            small_ref, smalls.at[me], m_send.at[step - 1], m_recv.at[step - 1], (lax.rem(flat, DPS), flat // DPS, col)
        )

    def place(w, r, d, half=None):
        return slot(w, full[w], r, d, own[w].shape[0], half)

    def source(w, k, half=None):
        if k == 0:
            return own[w] if half is None else half_of(w, own[w], half)
        return place(w, order[k], dp, half)

    def line_copies(w, k):
        src = source(w, k)
        dst = place(w, order[k], dp)
        recv = z_recv.at[w, order[k]]
        if k == 0:
            return [
                (None, remote(src, dst, z_send.at[w, 0], recv, (dp, at(1 - side), col))),
                (middle, remote(src, dst, z_send.at[w, 1], recv, (dp, at(2), col))),
            ]
        onward = at(2) if k == 1 else at(0)
        return [(middle, remote(src, dst, z_send.at[w, k + 1], recv, (dp, onward, col)))]

    def first_copies(w, k):
        out = []
        for half, target in ((0, across), (1, along)):
            out.append(
                remote(source(w, k, half), place(w, order[k], dp, half), s1_send.at[w, k, half],
                       s1_recv.at[w, k, half], (target, row, col))
            )
        return out

    def second_copies(w, k, which):
        out = []
        for half, target, other in ((0, along, across), (1, across, along)):
            if which == 0:
                src, owner = source(w, k, half), dp
            else:
                src, owner = place(w, order[k], other, half), other
            out.append(
                remote(src, place(w, order[k], owner, half), s2_send.at[w, k, which, half],
                       s2_recv.at[w, k, which, half], (target, row, col))
            )
        return out

    def onward(w, k):
        if k > 0:
            block = place(w, order[k], dp)
            pltpu.make_async_copy(block, block, z_recv.at[w, order[k]]).wait()
        for cond, copy in line_copies(w, k):
            if cond is None:
                copy.start()
            else:
                pl.when(cond)(copy.start)

    def sideways(w, k):
        for copy in first_copies(w, k) + second_copies(w, k, 0):
            copy.start()

    def arrived(w, k):
        onward(w, k)
        sideways(w, k)

    def passed(w, k):
        for copy in first_copies(w, k):
            copy.wait_recv()
        for copy in second_copies(w, k, 1):
            copy.start()

    def finished(w):
        for k in range(ROWS):
            for which in range(2):
                for copy in second_copies(w, k, which):
                    copy.wait_recv()

    def drained(w, k):
        for cond, copy in line_copies(w, k):
            if cond is None:
                copy.wait_send()
            else:
                pl.when(cond)(copy.wait_send)
        for copy in first_copies(w, k) + second_copies(w, k, 0) + second_copies(w, k, 1):
            copy.wait_send()

    def home(w):
        return pltpu.make_async_copy(own[w], place(w, row, dp), l_sem.at[w])

    def begin(w):
        loads[w].wait()
        own[w][...] = stage[w][...].astype(BF)
        home(w).start()

    small_home = pltpu.make_async_copy(small_ref, smalls.at[me], l_sem.at[N_W])
    kept = []

    def keep(src, dst):
        copy = pltpu.make_async_copy(src, dst, l_sem.at[N_W + 1 + len(kept)])
        copy.start()
        kept.append(copy)

    def smalls_start():
        small_home.start()
        for step in range(1, ROWS * DPS):
            small_copy(step).start()

    def norm():
        small_home.wait()
        for step in range(1, ROWS * DPS):
            small_copy(step).wait()
        read_gains(smalls, gains)
        if aligned:
            read_bias(smalls, bias_row, 9 + n_q // (DPS * 128), n_u // DPS)
        else:
            bias_row[...] = bias_in[...]
        branch[...] = jnp.zeros(branch.shape, F32)
        comb[...] = jnp.zeros(comb.shape, F32)
        token_finish(0)
        first, first_t = hidden.at[:, pl.ds(0, D)], hidden.at[:, pl.ds(D, D)]
        norm_stage(x_ref, gains, ((0, first, first_t), (2, second, second_t)))
        keep(x_ref, x_out)
        keep(smalls, smalls_out)
        keep(first, first_out)
        keep(first_t, first_t_out)

    def act(word):
        kind, rest = word[0], [int(d) for d in word[1:]]
        {
            "b": begin, "z": onward, "s": sideways, "p": passed, "t": token_start, "d": token_spread, "m": smalls_start,
            "N": norm,
        }[kind](*rest)

    def serve_at(when, unit):
        if blocks == DPS and BETWEEN[unit]:

            @pl.when(when)
            def _():
                for word in BETWEEN[unit]:
                    act(word)

    for word in BEFORE:
        act(word)
    if blocks < DPS:
        for words in BETWEEN:
            for word in words:
                act(word)
    home(UP).wait()
    finished(UP)
    for copy in kept[2:4]:
        copy.wait()

    def forward_block(n, carry):
        cut = span(n * width, width, width)

        def body(j, carry):
            rows = span(j * 256, 256, 256)
            value, slant = gelu_parts(nn(second[rows, :], wu[:, cut]) + bias_row[0:1, cut])
            hidden[rows, cut] = value.astype(BF)
            slope[rows, cut] = slant
            return carry

        lax.fori_loop(0, SEQ_LEN // 256, body, 0)
        for m in range(DPS):
            serve_at(n == m, m)
        return carry

    lax.fori_loop(0, blocks, forward_block, 0)
    token_finish(1)
    keep(c_ref, c_out)
    h = gp.shape[3]

    def down_block(n, carry):
        cut = span(n * width, width, width)
        turned = hidden[:, cut].T
        if blocks == DPS:
            for half in range(2):
                gp[n // 2, lax.rem(n, 2), half] = nn(turned[half * h : (half + 1) * h, :], c_ref[...]).astype(BF)
        else:
            gp[...] = nn(turned, c_ref[...]).astype(BF).reshape(2, 2, 2, h, D)
        for m in range(DPS):
            serve_at(n == m, DPS + m)
        return carry

    lax.fori_loop(0, blocks, down_block, 0)
    keep(gp, gp_out)
    home(DOWN).wait()
    finished(DOWN)
    sum_out[...] = jnp.zeros(sum_out.shape, F32)

    def backward_block(n, carry):
        cut = span(n * width, width, width)

        def body(j, carry):
            rows = span(j * 256, 256, 256)
            grad = (nt(c_ref[rows, :], wp[cut, :]) * slope[rows, cut]).astype(BF)
            ghp[rows, :] = grad
            branch[rows, :] += nn(hidden[rows, cut], wp[cut, :])
            comb[rows, :] += nt(grad, wu[:, cut])
            sum_out[0:1, cut] += jnp.sum(grad.astype(F32), axis=0, keepdims=True)
            return carry

        for part_of in range(2):
            lax.fori_loop(2 * part_of, 2 * part_of + 2, body, 0)
            for m in range(DPS):
                serve_at(n == m, 2 * DPS + 3 * m + part_of)

        def up_body(r, carry):
            value = nn(second_t[span(r * 256, 256, 256), :], ghp[...]).astype(BF)
            gu[r, :, :, :, :, cut] = value.reshape(2, 2, 2, 32, width)
            return carry

        lax.fori_loop(0, ROWS, up_body, 0)
        for m in range(DPS):
            serve_at(n == m, 2 * DPS + 3 * m + 2)
        return carry

    lax.fori_loop(0, blocks, backward_block, 0)
    for src, dst in ((gu, gu_out), (branch, branch_out), (comb, comb_out)):
        keep(src, dst)
    for w in (QKV, DENSE):
        home(w).wait()
        finished(w)
    for w in range(N_W):
        for k in range(ROWS):
            drained(w, k)
    for kind in range(2):
        token_drain(kind)
    for copy in kept[:2] + kept[4:]:
        copy.wait()


def gather(tokens_in, cotangent, small, bias, weights, cols, aligned):
    wq, wu, wd, wp = weights
    n_q, n_u = wq.shape[1], wu.shape[1]
    att_width, h_p = wd.shape[0] * DPS, wp.shape[0]
    width = 512 if n_u == DPS * 512 else n_u
    any_spec = pl.BlockSpec(memory_space=pl.ANY)
    vmem = pl.BlockSpec(memory_space=pltpu.VMEM)
    shape = jax.ShapeDtypeStruct
    smalls = (ROWS * DPS,) + small.shape
    square = (SEQ_LEN, D)
    up_shape, down_shape = (ROWS, 2, 2, 2, 32, n_u), (2, 2, 2, h_p // 2, D)
    out_shape = [
        shape(square, BF), shape(square, BF), shape(smalls, F32), shape((D, n_q), BF), shape((att_width, D), BF),
        shape(square, BF), shape(square, BF), shape(up_shape, BF), shape(down_shape, BF), shape(square, F32),
        shape(square, F32), shape((1, n_u), F32),
    ]
    tok_col = tokens_in.shape[0]
    pieces = tok_col // (SEQ_LEN // cols)
    dma = pltpu.SemaphoreType.DMA
    buf = pltpu.VMEM
    scratch = [buf(w.shape, BF) for w in weights] + [buf(w.shape, F32) for w in weights]
    scratch += [
        buf(square, BF), buf(square, BF), buf(smalls, F32), buf((D, n_u), BF), buf((n_u, D), BF),
        buf((8, D), F32), buf((1, n_u), F32), buf(square, BF), buf(square, BF),
        buf((SEQ_LEN, max(n_u, 2 * D)), BF), buf((SEQ_LEN, n_u), F32), buf((SEQ_LEN, width), BF), buf(up_shape, BF), buf(down_shape, BF), buf(square, F32),
        buf(square, F32),
        dma((N_W, 5)), dma((N_W, 4)), dma((N_W, 4, 2)), dma((N_W, 4, 2)), dma((N_W, 4, 2, 2)), dma((N_W, 4, 2, 2)),
        dma((2, pieces)), dma((2, 4)), dma((2, cols - 1)), dma((2, cols - 1)),
        dma((ROWS * DPS - 1,)), dma((ROWS * DPS - 1,)), dma((N_W + 10,)),
    ]
    return pl.pallas_call(
        functools.partial(gather_kernel, cols, aligned),
        out_shape=out_shape,
        in_specs=[any_spec] * 3 + [vmem] + [any_spec] * 4,
        out_specs=[any_spec] * 11 + [vmem],
        scratch_shapes=scratch,
        compiler_params=pltpu.CompilerParams(collective_id=0, has_side_effects=True, vmem_limit_bytes=60 << 20),
    )(tokens_in, cotangent, small, bias, wq, wu, wd, wp)


BEFORE_HEADS = (
    "f0", "f1", "J", "f2", "U",
)
AMONG_HEADS = (
    (),
    (),
    (),
    ("g0", "f3",),
    (),
    (),
    (),
    ("g1",),
    ("f4",),
    ("h0", "g2",),
    (),
    ("h1", "g3", "g4", "q0",),
    (),
    ("h2", "h3",),
    (),
    ("f5", "q1",),
)
AFTER_HEADS = (
    "q2", "h4", "T", "q3", "r0", "q4", "r1", "g5", "f6", "u0", "X", "W", "g6", "r2", "f7", "u1", "f8", "h5", "G",
    "g7", "h6", "Y", "g8", "f9", "u2", "r3", "h7", "f10", "q5", "h8", "v0", "q6", "g9", "v1", "f11", "v2", "q7",
    "h9", "u3", "g10", "h10", "g11", "q8", "r4", "r5", "q9", "r6", "u4", "v3", "u5", "r7", "r8", "q10", "h11",
    "q11", "u6", "u7", "u8", "r9", "u9", "r10", "v4", "u10", "r11", "u11",
)
PIECES = 12


def add_into(dst, src):
    shape = dst.shape
    outer, height = shape[:-2], shape[-2]
    step = min(32, height)
    per = height // step
    total = math.prod(outer) * per

    def body(i, carry):
        index, rest = [], i // per
        for size in reversed(outer):
            index.append(lax.rem(rest, size))
            rest = rest // size
        where = tuple(reversed(index)) + (span(lax.rem(i, per) * step, step, step),)
        dst[where] = (dst[where].astype(F32) + src[where].astype(F32)).astype(BF)
        return carry

    lax.fori_loop(0, total, body, 0)


def pieces_of(n_q, n_u, h_d, h_p):
    out = []

    def columns(w, n):
        size = 512 if n % 512 == 0 else n
        out.extend((w, start, size) for start in range(0, n, size))

    columns(UP, n_u)
    half = h_p // 2
    size = 64 if half % 64 == 0 else half
    out.extend((DOWN, start, size) for start in range(0, half, size))
    out.append((DENSE, 0, h_d // 2))
    columns(QKV, n_q)
    return out


def scatter_kernel(cols, aligned, pieces, *refs):
    n_p = len(pieces)
    (prefix_ref, smalls, angles, bias_in, sum_u, x_in, c_in, wq_in, wd_in, first_in, first_t_in, gu_in, gp_in, branch_in,
     comb_in) = refs[:15]
    (lo_out, gt_out, oq, ou, od, op, sm_out) = refs[15:22]
    (wq, wd, x_ref, c_ref, first, first_t, q_t, k_t, v_t, up_t, att_t, gm_t, grad_q, grad_k, grad_v) = refs[22:37]
    (gq, gd, att, total_ref, branch_got, comb_got, gains, bias_row, out_bias, sm, sm_got, gain_sum) = refs[37:49]
    mine_u, mine_p = refs[49:51], refs[51:53]
    base = 53

    def buffers(start):
        return [refs[start + 2 * i : start + 2 * i + 2] for i in range(n_p)]

    got1, got2, got_end, got_mid = [buffers(base + 2 * n_p * n) for n in range(4)]
    (l_sem, f_sem, s1_send, s1_recv, s2_send, s2_recv, e_send, e_recv, m_send, m_recv, b_send, b_recv, d_send, d_recv,
     t_send, t_recv, v_send, v_recv) = refs[base + 8 * n_p :]
    dp, row, col, across, along = places()
    x, y = lax.rem(dp, 2), dp // 2
    side, at = line_order(row)
    far_end = row // 2
    middle, end = side == 1, side == 0
    n_q, n_u = wq_in.shape[1], sum_u.shape[1]
    heads = q_t.shape[0]
    tok_col = lo_out.shape[0]
    part = SEQ_LEN // cols

    def load(src, dst, n):
        return pltpu.make_async_copy(src, dst, l_sem.at[n])

    loads = [load(first_in, first, 0), load(wq_in, wq, 1), load(wd_in, wd, 2), load(c_in, c_ref, 3), load(first_t_in, first_t, 4),
             load(x_in, x_ref, 5), load(branch_in, total_ref, 6)]
    for one in loads:
        one.start()
    group = [(dp, lax.rem(row + step, ROWS), lax.rem(col + other, cols)) for step in range(ROWS) for other in range(cols)]
    greet([(across, row, col), (along, row, col)] + group[1:])

    def view(i, half, other):
        w, start, size = pieces[i]
        if half == 0:
            place_y, place_x = (1 - y if other else y), slice(None)
        else:
            place_y, place_x = slice(None), (1 - x if other else x)
        cut = pl.ds(start, size)
        if w in (QKV, UP):
            if w == UP and not other:
                return mine_u[half].at[:, :, :, cut]
            return (gu_in if w == UP else gq).at[:, place_y, place_x, half, :, cut]
        if w == DOWN and not other:
            return mine_p[half].at[:, cut, :]
        return (gp_in if w == DOWN else gd).at[place_y, place_x, half, cut, :]

    def fetch(i, half):
        w, start, size = pieces[i]
        place_y, place_x = (y, slice(None)) if half == 0 else (slice(None), x)
        cut = pl.ds(start, size)
        src = gu_in.at[:, place_y, place_x, half, :, cut] if w == UP else gp_in.at[place_y, place_x, half, cut, :]
        return pltpu.make_async_copy(src, view(i, half, False), f_sem.at[i, half])

    def first_copy(i, half):
        target = along if half == 0 else across
        return remote(view(i, half, True), got1[i][half], s1_send.at[i, half], s1_recv.at[i, half], (target, row, col))

    def keep(i, half, other):
        which = x if half == 0 else y
        which = 1 - which if other else which
        kept = view(i, half, False)
        return kept.at[:, which] if pieces[i][0] in (QKV, UP) else kept.at[which]

    def second_copy(i, half):
        target = across if half == 0 else along
        return remote(keep(i, half, True), got2[i][half], s2_send.at[i, half], s2_recv.at[i, half], (target, row, col))

    def lines(i, ref, start, count):
        if pieces[i][0] in (QKV, UP):
            return ref.at[pl.ds(start, count)]
        return ref.at[:, span(start * 256, count * 256, 256)]

    def end_copy(i, half):
        src = lines(i, keep(i, half, False), 1 - far_end, 3)
        return remote(src, got_end[i][half], e_send.at[i, half], e_recv.at[i, half], (dp, at(1), col))

    def mid_copy(i, half):
        src = lines(i, keep(i, half, False), 2 * (1 - far_end), 2)
        return remote(src, got_mid[i][half], m_send.at[i, half], m_recv.at[i, half], (dp, at(2), col))

    def back_copy(i, half):
        src = lines(i, keep(i, half, False), at(0), 1)
        return remote(src, lines(i, got_mid[i][half], 0, 1), b_send.at[i, half], b_recv.at[i, half], (dp, at(0), col))

    def begin(i):
        for half in range(2):
            first_copy(i, half).start()
            if pieces[i][0] in (UP, DOWN):
                fetch(i, half).start()

    def stage_two(i):
        for half in range(2):
            if pieces[i][0] in (UP, DOWN):
                fetch(i, half).wait()
            first_copy(i, half).wait_recv()
            add_into(view(i, half, False), got1[i][half])
            second_copy(i, half).start()

    def stage_three(i):
        for half in range(2):
            second_copy(i, half).wait_recv()
            add_into(keep(i, half, False), got2[i][half])

            @pl.when(end)
            def _():
                end_copy(i, half).start()

    def stage_four(i):
        @pl.when(middle)
        def _():
            for half in range(2):
                end_copy(i, half).wait_recv()
                add_into(lines(i, keep(i, half, False), 2 * (1 - far_end), 2), lines(i, got_end[i][half], 1 - far_end, 2))
                mid_copy(i, half).start()

    def stage_five(i):
        @pl.when(middle)
        def _():
            for half in range(2):
                mid_copy(i, half).wait_recv()
                add_into(lines(i, keep(i, half, False), at(0), 1), lines(i, got_mid[i][half], far_end, 1))
                back_copy(i, half).start()

    def stage_six(i):
        w, start, size = pieces[i]
        out = (oq, ou, od, op)[w]
        for half in range(2):
            mine = lines(i, keep(i, half, False), row, 1)

            def total(others):
                if w in (QKV, UP):
                    value = mine[0].astype(F32)
                    for other in others:
                        value = value + other[0].astype(F32)
                    out[half, :, pl.ds(start, size)] = value
                else:
                    value = mine[...].astype(F32)
                    for other in others:
                        value = value + other[...].astype(F32)
                    out[half, pl.ds(start, size), :] = value

            @pl.when(end)
            def _():
                back_copy(i, half).wait_recv()
                total([lines(i, got_mid[i][half], 0, 1)])

            @pl.when(middle)
            def _():
                total([lines(i, got_end[i][half], 2 * far_end, 1), lines(i, got_mid[i][half], 1 - far_end, 1)])

    def drain(i):
        for half in range(2):
            first_copy(i, half).wait_send()
            second_copy(i, half).wait_send()

            @pl.when(end)
            def _():
                end_copy(i, half).wait_send()

            @pl.when(middle)
            def _():
                mid_copy(i, half).wait_send()
                back_copy(i, half).wait_send()

    def part_rows(piece):
        return span(piece * part, part, part)

    def col_copy(kind, n):
        other = lax.rem(col + n, cols)
        src = total_ref.at[part_rows(other), :]
        dst = (branch_got, comb_got)[kind].at[n - 1]
        return remote(src, dst, d_send.at[kind, n - 1], d_recv.at[kind, n - 1], (dp, row, other))

    start = row * SEQ_LEN + col * part
    owner, offset = start // tok_col, lax.rem(start, tok_col)

    def out_copy(kind, r):
        src = first.at[pl.ds(kind * part, part), span(r * 256, 256, 256)]
        dst = (lo_out, gt_out)[kind].at[span(offset, part, part), :]
        recv = t_recv.at[kind, offset // part]
        here = jnp.logical_and(row == r, owner == col)
        far = remote(src, dst, t_send.at[kind, r], recv, (dp, r, owner))
        return here, far, pltpu.make_async_copy(src, dst, recv)

    def out_start(kind):
        for r in (at(1 - side), at(2), at(3), row):
            here, far, near = out_copy(kind, r)
            pl.when(jnp.logical_not(here))(far.start)
            pl.when(here)(near.start)

    def out_finish(kind):
        for r in range(ROWS):
            here, far, near = out_copy(kind, r)
            pl.when(jnp.logical_not(here))(far.wait_send)
        out = (lo_out, gt_out)[kind]
        for n in range(tok_col // part):
            block = out.at[pl.ds(n * part, part), :]
            pltpu.make_async_copy(block, block, t_recv.at[kind, n]).wait()

    height = min(128, part)

    def finish_rows(kind):
        for n in range(1, cols):
            col_copy(kind, n).wait_recv()

        def body(i, carry):
            here = span(i * height, height, height)
            rows = span(col * part + i * height, height, height)
            value = total_ref[rows, :]
            for n in range(1, cols):
                value = value + (branch_got, comb_got)[kind][n - 1, here, :]
            wide = x_ref[rows, :].astype(F32)
            if kind == 0:
                value = wide + value + out_bias[0:1, :]
            else:
                normed, scale_inv = norm_rows(wide)
                mean = jnp.mean(value, axis=1, keepdims=True)
                cross = jnp.mean(value * normed, axis=1, keepdims=True)
                value = c_ref[rows, :].astype(F32) + scale_inv * (value - mean - normed * cross)
            first[span(kind * part + i * height, height, height), :] = value.astype(BF)
            return carry

        lax.fori_loop(0, part // height, body, 0)

    def small_copy(n):
        if n < 2:
            return remote(sm.at[n], sm_got.at[n], v_send.at[n], v_recv.at[n], ((across, along)[n], row, col))
        if n < 5:
            target = (dp, lax.rem(row + n - 1, ROWS), col)
            return remote(sm.at[2], sm_got.at[n], v_send.at[n], v_recv.at[n], target)
        target = (dp, row, lax.rem(col + n - 4, cols))
        return remote(sm.at[3], sm_got.at[n], v_send.at[n], v_recv.at[n], target)

    def small_step(n):
        if n > 0:
            waits = ((0,), (1,), (2, 3, 4), tuple(range(5, 4 + cols)))[n - 1]
            for m in waits:
                small_copy(m).wait_recv()
            value = sm[n - 1]
            if n < 4:
                for m in waits:
                    value = value + sm_got[m]
                sm[n] = value
            else:
                sm_out[...] = value
                value = value[0:4]
                for m in waits:
                    value = value + sm_got[m, 0:4, :]
                sm_out[0:4, :] = value
        for m in ((0,), (1,), (2, 3, 4), tuple(range(5, 4 + cols)), ())[n]:
            small_copy(m).start()

    def project():
        read_gains(smalls, gains)
        lanes = lax.broadcasted_iota(jnp.int32, (1, 128), 1)
        for r in range(ROWS):
            for d in range(0, DPS, 2):
                both = [rounded(smalls[r * DPS + d + n, 8:9, :]) for n in range(2)]
                both = [value + pltpu.roll(value, 64, 1) for value in both]
                out_bias[0:1, pl.ds(r * 256 + d * 64, 128)] = jnp.where(lanes < 64, both[0], both[1])
        if aligned:
            read_bias(smalls, bias_row, 9, n_q // DPS)
        else:
            bias_row[...] = bias_in[...]
        sm[0] = jnp.zeros(sm.shape[1:], F32)
        sm[0, 6:7, 0:n_u] = sum_u[...]
        loads[0].wait()
        loads[1].wait()
        project_stage(wq, first, bias_row, angles, q_t, k_t, v_t, heads)

    def upstream():
        loads[2].wait()
        loads[3].wait()
        upstream_stage(wd, c_ref, up_t, heads)

    def attended():
        group_h = min(heads, 4)

        def turn_body(i, carry):
            block = att_t[pl.ds(i * group_h, group_h)].reshape(group_h * HD, SEQ_LEN)
            spot = pl.ds(0, group_h * HD) if heads == group_h else span(i * group_h * HD, group_h * HD, 128)
            att[:, spot] = block.T
            return carry

        lax.fori_loop(0, heads // group_h, turn_body, 0)
        loads[6].wait()

        def out_body(j, carry):
            rows = span(j * 256, 256, 256)
            total_ref[rows, :] += nn(att[rows, :], wd[...])
            return carry

        lax.fori_loop(0, SEQ_LEN // 256, out_body, 0)
        for n in range(1, cols):
            col_copy(0, n).start()

    def weight_grads():
        all_heads = att_t[...].reshape(heads * HD, SEQ_LEN)
        gd[...] = nn(all_heads, c_ref[...]).astype(BF).reshape(gd.shape)
        loads[4].wait()
        wide = min(512, n_q)

        def qkv_body(r, carry):
            rows = span(r * 256, 256, 256)
            for n in range(n_q // wide):
                cut = pl.ds(n * wide, wide)
                gq[r, :, :, :, :, cut] = nt(first_t[rows, :], gm_t[cut, :]).astype(BF).reshape(2, 2, 2, 32, wide)
            return carry

        lax.fori_loop(0, ROWS, qkv_body, 0)

    load_comb = load(comb_in, total_ref, 6)

    def output_home():
        loads[5].wait()
        finish_rows(0)
        out_start(0)
        for n in range(1, cols):
            col_copy(0, n).wait_send()
        load_comb.start()

    def features():
        load_comb.wait()
        for n in range(8):
            gain_sum[n : n + 1, :] = jnp.zeros((1, D), F32)

        def body(j, carry):
            rows = span(j * 256, 256, 256)
            grad = gm_t[:, rows].T
            grad_first = nt(grad, wq[...])
            grad_second = total_ref[rows, :]
            normed, ignored = norm_rows(x_ref[rows, :].astype(F32))
            for n, value in enumerate((normed * grad_first, grad_first, normed * grad_second, grad_second,
                                       c_ref[rows, :].astype(F32))):
                gain_sum[n : n + 1, :] += jnp.sum(value, axis=0, keepdims=True)
            sm[0, 5:6, 0:n_q] += jnp.sum(grad.astype(F32), axis=0, keepdims=True)
            total_ref[rows, :] = gains[0:1, :] * grad_first + gains[2:3, :] * grad_second
            return carry

        lax.fori_loop(0, SEQ_LEN // 256, body, 0)
        for n in range(1, cols):
            col_copy(1, n).start()
        sm[0, 0:5, 0:D] = gain_sum[0:5, :]

    def gradient_home():
        finish_rows(1)
        out_start(1)

    stages = {"f": begin, "g": stage_two, "h": stage_three, "q": stage_four, "r": stage_five, "u": stage_six}
    others = {"J": project, "U": upstream, "T": attended, "W": weight_grads, "X": output_home, "G": features, "Y": gradient_home}

    def act(word):
        kind, rest = word[0], word[1:]
        if kind in others:
            others[kind]()
        elif kind == "v":
            small_step(int(rest))
        else:
            stages[kind](int(rest))

    plan = (BEFORE_HEADS, AMONG_HEADS, AFTER_HEADS)
    if n_p != PIECES:
        late = [i for i in range(n_p) if pieces[i][0] in (QKV, DENSE)]
        early = [i for i in range(n_p) if i not in late]
        after = ["T", "W", "X", "G", "Y"] + ["f%d" % i for i in late] + [s + str(i) for s in "ghqru" for i in range(n_p)]
        plan = (["f%d" % i for i in early] + ["J", "U"], ((),) * 16, after + ["v%d" % i for i in range(5)])
    before_heads, among_heads, after_heads = plan

    def serve_at(when, unit):
        if among_heads[unit]:

            @pl.when(when)
            def _():
                for word in among_heads[unit]:
                    act(word)

    for word in before_heads:
        act(word)
    prefix = prefix_ref[0]
    units = len(among_heads) // 2

    def head_body(h, carry):
        for n in range(min(units, heads)):
            serve_at(h == n, 2 * n)

        def middle():
            for n in range(min(units, heads)):
                serve_at(h == n, 2 * n + 1)

        attend_head(h, prefix, angles, q_t, k_t, v_t, up_t, att_t, gm_t, grad_q, grad_k, grad_v, middle)
        return carry

    lax.fori_loop(0, heads, head_body, 0)
    for unit in range(2 * min(units, heads), 2 * units):
        for word in among_heads[unit]:
            act(word)
    for word in after_heads:
        act(word)
    for i in range(n_p):
        drain(i)
    for kind in range(2):
        out_finish(kind)
    for n in range(1, cols):
        col_copy(1, n).wait_send()
    for n in range(4 + cols):
        small_copy(n).wait_send()


def scatter(prefix_len, smalls, angles, bias, sum_u, own_x, own_cot, wq, wd, first, first_t, gu, gp, branch, comb, cols, aligned,
            tok_col):
    any_spec = pl.BlockSpec(memory_space=pl.ANY)
    vmem = pl.BlockSpec(memory_space=pltpu.VMEM)
    smem = pl.BlockSpec(memory_space=pltpu.SMEM)
    dma = pltpu.SemaphoreType.DMA
    buf = pltpu.VMEM
    shape = jax.ShapeDtypeStruct
    n_q, n_u = wq.shape[1], sum_u.shape[1]
    heads = n_q // 192
    h_d, h_p = wd.shape[0] // DPS, 2 * gp.shape[3]
    pieces = pieces_of(n_q, n_u, h_d, h_p)
    n_p = len(pieces)
    part = SEQ_LEN // cols
    line = max(n_q, n_u, D)
    square = (SEQ_LEN, D)
    turned = buf((heads, HD, SEQ_LEN), BF)
    scratch = [
        buf((D, n_q), BF), buf(wd.shape, BF), buf(square, BF), buf(square, BF), buf(square, BF), buf(square, BF),
        turned, turned, turned, turned, turned, buf((n_q, SEQ_LEN), BF),
        buf((HD, SEQ_LEN), F32), buf((HD, SEQ_LEN), F32), buf((HD, SEQ_LEN), F32),
        buf((ROWS, 2, 2, 2, 32, n_q), BF), buf((2, 2, 2, h_d // 2, D), BF), buf((SEQ_LEN, heads * HD), BF), buf(square, F32),
        buf((cols - 1, part, D), F32), buf((cols - 1, part, D), F32),
        buf((8, D), F32), buf((1, n_q), F32), buf((1, D), F32), buf((4, 8, line), F32), buf((4 + cols, 8, line), F32),
        buf((8, D), F32),
    ]
    scratch += [buf((ROWS, 2, 32, n_u), BF)] * 2 + [buf((2, h_p // 2, D), BF)] * 2
    for lead, count in (((ROWS, 2), None), ((ROWS,), None), ((3,), 3), ((2,), 2)):
        for w, start, size in pieces:
            if w in (QKV, UP):
                one = lead + (32, size)
            elif count is None:
                one = ((2,) if len(lead) == 2 else ()) + (size, D)
            else:
                one = (size, 256 * count)
            scratch += [buf(one, BF)] * 2
    scratch += [
        dma((7,)), dma((n_p, 2)), dma((n_p, 2)), dma((n_p, 2)), dma((n_p, 2)), dma((n_p, 2)), dma((n_p, 2)), dma((n_p, 2)),
        dma((n_p, 2)), dma((n_p, 2)), dma((n_p, 2)), dma((n_p, 2)), dma((2, cols - 1)), dma((2, cols - 1)),
        dma((2, ROWS)), dma((2, tok_col // part)), dma((4 + cols,)), dma((4 + cols,)),
    ]
    return pl.pallas_call(
        functools.partial(scatter_kernel, cols, aligned, pieces),
        out_shape=[
            shape((tok_col, 256), BF), shape((tok_col, 256), BF), shape((2, 32, n_q), F32), shape((2, 32, n_u), F32),
            shape((2, h_d // 2, 256), F32), shape((2, h_p // 2, 256), F32), shape((8, line), F32),
        ],
        in_specs=[smem, vmem, vmem, vmem, vmem] + [any_spec] * 10,
        out_specs=[any_spec] * 2 + [vmem] * 5,
        scratch_shapes=scratch,
        compiler_params=pltpu.CompilerParams(collective_id=1, has_side_effects=True, vmem_limit_bytes=63 << 20),
    )(prefix_len, smalls, angles, bias, sum_u, own_x, own_cot, wq, wd, first, first_t, gu, gp, branch, comb)


def angles_table():
    half_rot = ROT // 2
    rates = np.exp(np.arange(half_rot, dtype=np.float32) * np.float32(-2.0 * math.log(10000.0) / ROT))
    turned = rates.astype(np.float32)[:, None] * np.arange(SEQ_LEN, dtype=np.float32)[None, :]
    return np.concatenate([np.cos(turned), np.sin(turned)], axis=0).astype(np.float32)


def shards(cols, tokens_in, prefix_len, first_gain, first_shift, second_gain, second_shift, qkv_weight, qkv_bias,
           up_weight, up_bias, dense_weight, dense_bias, down_weight, down_bias, cotangent):
    tok_col = tokens_in.shape[0]
    n_q, n_u = qkv_weight.shape[1], up_weight.shape[1]
    h_d, h_p = dense_weight.shape[0], down_weight.shape[0]

    n_qb, n_ub = qkv_bias.shape[0], up_bias.shape[0]
    aligned = n_qb % 128 == 0 and n_ub % 128 == 0
    small = jnp.concatenate((first_gain, first_shift, second_gain, second_shift, dense_bias, down_bias, qkv_bias, up_bias))
    size = -(-small.shape[0] // 1024) * 1024
    small = jnp.pad(small, (0, size - small.shape[0])).reshape(size // 128, 128)
    if aligned:
        q_bias = u_bias = small
    else:
        q_bias = lax.all_gather(rounded(qkv_bias), "dp", axis=0, tiled=True).reshape(1, n_q)
        u_bias = lax.all_gather(rounded(up_bias), "dp", axis=0, tiled=True).reshape(1, n_u)
    own_x, own_cot, smalls, wq, wd, first, first_t, gu, gp, branch, comb, sum_u = gather(
        tokens_in, cotangent, small, u_bias, (qkv_weight, up_weight, dense_weight, down_weight), cols, aligned
    )
    layer_out, grad_tokens, out_q, out_u, out_d, out_p, sums = scatter(
        prefix_len, smalls, jnp.asarray(angles_table()), q_bias, sum_u, own_x, own_cot, wq, wd, first, first_t, gu, gp, branch,
        comb, cols, aligned, tok_col
    )
    dp, row = lax.axis_index("dp"), lax.axis_index("row")
    gain_sums = lax.dynamic_slice(sums, (0, row * 256), (4, 256))
    out_b = lax.dynamic_slice(sums, (4, (row * DPS + dp) * 64), (1, 64))[0]
    q_b = lax.dynamic_slice(sums, (5, dp * n_qb), (1, n_qb))[0]
    u_b = lax.dynamic_slice(sums, (6, dp * n_ub), (1, n_ub))[0]
    return (
        layer_out, grad_tokens, out_q.reshape(64, n_q), q_b, out_u.reshape(64, n_u), u_b,
        out_d.reshape(h_d, 256), out_b, out_p.reshape(h_p, 256), out_b,
        gain_sums[0], gain_sums[1], gain_sums[2], gain_sums[3],
    )


def solution(mesh):
    in_specs = (
        P(("dp", "col"), "row"), P(("dp", "row")), P("row"), P("row"), P("row"), P("row"),
        P(("row", "dp"), "col"), P(("col", "dp")), P(("row", "dp"), "col"), P(("col", "dp")),
        P(("col", "dp"), "row"), P(("row", "dp")), P(("col", "dp"), "row"), P(("row", "dp")),
        P(("dp", "col"), "row"),
    )
    out_specs = (
        P(("dp", "col"), "row"), P(("dp", "col"), "row"), P(("row", "dp"), "col"), P(("col", "dp")),
        P(("row", "dp"), "col"), P(("col", "dp")), P(("col", "dp"), "row"), P(("row", "dp")),
        P(("col", "dp"), "row"), P(("row", "dp")), P("row"), P("row"), P("row"), P("row"),
    )
    body = functools.partial(shards, mesh.shape["col"])
    return jax.shard_map(body, mesh=mesh, in_specs=in_specs, out_specs=out_specs, check_vma=False)
```

```python
import functools
import math

import jax
import jax.numpy as jnp
import numpy as np
from jax import lax
from jax.experimental import pallas as pl
from jax.experimental.pallas import tpu as pltpu
from jax.sharding import PartitionSpec as P

D = 1024
HD = 64
ROT = 16
FF = 4096
SEQ_LEN = 1024
EPS = 1e-05
NEGATIVE = -1e30
ROWS = 4
DPS = 4
MESH = pl.DeviceIdType.MESH
BF = jnp.bfloat16
F32 = jnp.float32


def places():
    dp, row, col = lax.axis_index("dp"), lax.axis_index("row"), lax.axis_index("col")
    across = dp + 1 - 2 * lax.rem(dp, 2)
    along = lax.rem(dp + 2, 4)
    return dp, row, col, across, along


def line_order(row):
    far = row // 2
    side = row + far * (3 - 2 * row)
    at = lambda place: far * 3 + (1 - 2 * far) * place
    return side, at


def greet(targets):
    barrier = pltpu.get_barrier_semaphore()
    for target in targets:
        pl.semaphore_signal(barrier, inc=1, device_id=target, device_id_type=MESH)
    pl.semaphore_wait(barrier, len(targets))


def peers_of(dp, row, col, cols):
    group = []
    for step in range(1, ROWS * cols):
        flat = lax.rem(row * cols + col + step, ROWS * cols)
        group.append((dp, flat // cols, lax.rem(flat, cols)))
    for step in range(1, DPS):
        for other in range(ROWS):
            group.append((lax.rem(dp + step, DPS), lax.rem(row + other, ROWS), col))
    return group


def remote(src, dst, send, recv, target):
    return pltpu.make_async_remote_copy(
        src_ref=src, dst_ref=dst, send_sem=send, recv_sem=recv, device_id=target, device_id_type=MESH
    )


N_W = 4
QKV, UP, DENSE, DOWN = range(N_W)
GATHER_PLAN = (
    "b1", "z10", "b0", "b3", "b2", "z20", "s10", "z11", "s11", "z12", "z30", "m", "s12", "z13", "s30", "t0", "z31",
    "p10", "p11", "s31", "s13", "s00", "p31", "z32", "t1", "p12", "p13", "s32", "z33", "s20", "d0", "z00", "p30",
    "z21", "s33", "N0", "N1", "N2", "N3", "N4", "N5", "N6", "N7", "p32", "P0", "d1", "P1", "P2", "P3", "z01",
    "p33", "D0", "s01", "D1", "s21", "D2", "z02", "p00", "D3", "s02", "z22", "z23", "B0", "B1", "z03", "B2", "B3",
    "s23", "B4", "B5", "p23", "s22", "p20", "p21", "B6", "B7", "p22", "p02", "s03", "B8", "p01", "B9", "B10",
    "B11", "p03",
)


def run(words, loops, act):
    i = 0
    while i < len(words):
        kind = words[i][0]
        if kind not in loops:
            act(words[i])
            i += 1
            continue
        count, body = loops[kind]
        groups = [[]]
        i += 1
        while len(groups) < count:
            if words[i][0] == kind:
                groups.append([])
            else:
                groups[-1].append(words[i])
            i += 1

        def served(index, first=0, stride=1):
            for n, group in enumerate(groups[first::stride]):
                if group:

                    @pl.when(index == n)
                    def _():
                        for word in group:
                            act(word)

        body(served)


def parts_of(kind, count):
    return ["%s%d" % (kind, n) for n in range(count)]


def nt(left, right):
    return lax.dot_general(left, right, (((1,), (1,)), ((), ())), preferred_element_type=F32)


def nn(left, right):
    return jnp.dot(left, right, preferred_element_type=F32)


def span(start, size, unit):
    return pl.ds(pl.multiple_of(start, unit), size)


def slot(w, ref, row, dp, height, half=None):
    if w in (QKV, UP):
        if half is None:
            return ref.at[span((row * DPS + dp) * height, height, 64), :]
        return ref.at[span((row * DPS + dp) * height + half * (height // 2), height // 2, 32), :]
    if half is None:
        return ref.at[span(dp * height, height, 16), span(row * 256, 256, 256)]
    if w == DENSE:
        return ref.at[span(dp * height, height, 16), span(row * 256 + half * 128, 128, 128)]
    return ref.at[span(dp * height + half * (height // 2), height // 2, 16), span(row * 256, 256, 256)]


def half_of(w, ref, half):
    height = ref.shape[0]
    if w == DENSE:
        return ref.at[:, pl.ds(half * 128, 128)]
    return ref.at[pl.ds(half * (height // 2), height // 2), :]


def read_gains(smalls, gains):
    for r in range(ROWS):
        for g in range(4):
            for t in range(2):
                gains[g : g + 1, pl.ds(r * 256 + t * 128, 128)] = smalls[r * DPS, pl.ds(2 * g + t, 1), :]


def rounded(value):
    return value.astype(BF).astype(F32)


def read_bias(smalls, bias, first_row, size):
    per = size // 128
    for d in range(DPS):
        for t in range(per):
            bias[0:1, pl.ds(d * size + t * 128, 128)] = rounded(smalls[d, pl.ds(first_row + t, 1), :])


def norm_rows(x):
    center = jnp.mean(x, axis=1, keepdims=True)
    spread = jnp.mean(x * x, axis=1, keepdims=True) - center * center
    scale_inv = lax.rsqrt(spread + EPS)
    return (x - center) * scale_inv, scale_inv


def norm_stage(x_ref, gains, outs, served):
    def body(i, carry):
        rows = span(i * 128, 128, 128)
        normed, ignored = norm_rows(x_ref[rows, :].astype(F32))
        for which, plain, turned in outs:
            value = (normed * gains[which : which + 1, :] + gains[which + 1 : which + 2, :]).astype(BF)
            plain[rows, :] = value
            turned[:, rows] = value.T
        served(i)
        return carry

    lax.fori_loop(0, SEQ_LEN // 128, body, 0)


def project_stage(wq, first, bias_row, angles, q_t, k_t, v_t, heads, served):
    pair = min(heads, 2)
    width = 192 * pair

    def body(p, carry):
        cols = pl.ds(0, width) if heads == pair else span(p * width, width, 128)
        w_t = wq[:, cols].T
        bias = jnp.broadcast_to(bias_row[0:1, cols], (8, width)).T[:, 0:1]
        for j in range(SEQ_LEN // 256):
            toks = pl.ds(j * 256, 256)
            mixed = nt(w_t, first[toks, :]) + bias
            cos, sin = angles[0:8, toks], angles[8:16, toks]

            def turn(base):
                x1, x2 = mixed[base : base + 8], mixed[base + 8 : base + 16]
                return jnp.concatenate([x1 * cos - x2 * sin, x2 * cos + x1 * sin, mixed[base + 16 : base + 64]], axis=0)

            for e in range(pair):
                base, h = 192 * e, pair * p + e
                q_t[h, :, toks] = (turn(base) * HD ** (-0.5)).astype(BF)
                k_t[h, :, toks] = turn(base + 64).astype(BF)
                v_t[h, :, toks] = mixed[base + 128 : base + 192].astype(BF)
        served(p)
        return carry

    lax.fori_loop(0, heads // pair, body, 0)


def upstream_stage(wd, c_ref, up_t, heads):
    for j in range(SEQ_LEN // 256):
        toks = pl.ds(j * 256, 256)
        grad = nt(wd[...], c_ref[toks, :]).astype(BF)
        for h in range(heads):
            up_t[h, :, toks] = grad[HD * h : HD * (h + 1)]


def attend_head(h, prefix, angles, q_t, k_t, v_t, up_t, att_t, gm_t, grad_q, grad_k, grad_v, served):
    keys_plain, values_plain = k_t[h].T, v_t[h].T
    done = 0
    for i in range(SEQ_LEN // 256):
        low = 256 * i
        seen = max(512, low + 256)
        spot = pl.ds(low, 256)
        q, up = q_t[h, :, spot], up_t[h, :, spot]
        scores = nn(keys_plain[0:seen], q)
        plain = min(low, seen)
        keys = lax.broadcasted_iota(jnp.int32, (seen - plain, 256), 0) + plain
        queries = lax.broadcasted_iota(jnp.int32, (seen - plain, 256), 1) + low
        masked = jnp.where((keys <= queries) | (keys < prefix), scores[plain:], NEGATIVE)
        scores = jnp.concatenate([scores[:plain], masked], axis=0) if plain else masked
        exponent = jnp.exp(scores - jnp.max(scores, axis=0, keepdims=True))
        probs = exponent * (1.0 / jnp.sum(exponent, axis=0, keepdims=True))
        weights = probs.astype(BF)
        outputs = nn(v_t[h, :, 0:seen], weights)
        att_t[h, :, spot] = outputs.astype(BF)
        inner = jnp.sum(outputs * up.astype(F32), axis=0, keepdims=True)
        grad_probs = nn(values_plain[0:seen], up)
        grad_scores = (probs * (grad_probs - inner)).astype(BF)
        grad_q[:, spot] = nn(k_t[h, :, 0:seen], grad_scores)
        for total, part in ((grad_v, nt(up, weights)), (grad_k, nt(q, grad_scores))):
            if done:
                total[:, 0:done] += part[:, :done]
            if seen > done:
                total[:, done:seen] = part[:, done:]
        done = seen
        served(h, i, SEQ_LEN // 256)
    cos, sin = angles[0:8, :], angles[8:16, :]

    def turn_back(grad):
        g1, g2 = grad[0:8], grad[8:16]
        return jnp.concatenate([g1 * cos + g2 * sin, g2 * cos - g1 * sin, grad[16:]], axis=0)

    base = h * 192
    gm_t[span(base, HD, HD), :] = (turn_back(grad_q[...]) * HD ** (-0.5)).astype(BF)
    gm_t[span(base + HD, HD, HD), :] = turn_back(grad_k[...]).astype(BF)
    gm_t[span(base + 2 * HD, HD, HD), :] = grad_v[...].astype(BF)


def gelu_parts(x):
    below = 0.5 * (1.0 + lax.erf(x * (0.5**0.5)))
    density = jnp.exp(-0.5 * x * x) * (1.0 / math.sqrt(2.0 * math.pi))
    return x * below, below + x * density


def gather_kernel(cols, aligned, *refs):
    (tok_ref, cot_ref, small_ref, bias_in) = refs[:4]
    masters = refs[4:8]
    (x_out, c_out, smalls_out, gq_ref, gd_ref, first_out, first_t_out, gu_out, gp_out, branch_out, comb_out, sum_out) = refs[8:20]
    own = refs[20:24]
    stage = refs[24:28]
    (x_ref, c_ref, smalls, wu, wp, gains, bias_row, second, second_t) = refs[28:37]
    (hidden, slope, ghp, gu, gp, branch, comb) = refs[37:44]
    (z_send, z_recv, s1_send, s1_recv, s2_send, s2_recv, t_send, t_recv, a_send, a_recv, m_send, m_recv, l_sem) = refs[44:]
    full = (gq_ref, wu, gd_ref, wp)
    n_q, n_u = gq_ref.shape[1], wu.shape[1]
    width = ghp.shape[1]
    blocks = n_u // width
    dp, row, col, across, along = places()
    side, at = line_order(row)
    order = [row, at(1 - side), at(2), at(3)]
    middle = side == 1
    tok_col = tok_ref.shape[0]
    part = SEQ_LEN // cols
    chunk = min(tok_col, SEQ_LEN)
    n_seq = tok_col // chunk
    n_part = chunk // part

    loads = [pltpu.make_async_copy(masters[w], stage[w], l_sem.at[w]) for w in range(N_W)]
    for load in loads:
        load.start()
    greet(peers_of(dp, row, col, cols))

    def token_copy(kind, j, i):
        src_ref, dst_ref = ((tok_ref, x_ref), (cot_ref, c_ref))[kind]
        n = j * n_part + i
        if n_seq > 1:
            j = lax.rem(j + (n_seq - 1) * (1 - col), n_seq)
        start = col * tok_col + j * chunk
        to_row = start // SEQ_LEN
        piece = lax.rem(start, SEQ_LEN) // part + i
        src = src_ref.at[span(j * chunk + i * part, part, part), :]
        dst = dst_ref.at[span(piece * part, part, part), span(row * 256, 256, 256)]
        sends, recvs = t_send.at[kind, n], t_recv.at[kind, row]
        is_here = jnp.logical_and(to_row == row, piece == col)
        far = remote(src, dst, sends, recvs, (dp, to_row, piece))
        near = pltpu.make_async_copy(src, dst, recvs)
        return is_here, far, near

    def token_start(kind):
        for j in range(n_seq):
            for i in range(n_part):
                is_here, far, near = token_copy(kind, j, i)
                pl.when(jnp.logical_not(is_here))(far.start)
                pl.when(is_here)(near.start)

    def part_rows(piece):
        return span(piece * part, part, part)

    def spread_copy(kind, step):
        mine = (x_ref, c_ref)[kind].at[part_rows(col), :]
        to_col = lax.rem(col + step, cols)
        return remote(mine, mine, a_send.at[kind, step - 1], a_recv.at[kind, step - 1], (dp, row, to_col))

    def token_spread(kind):
        dst_ref = (x_ref, c_ref)[kind]
        for other in range(ROWS):
            block = dst_ref.at[part_rows(col), pl.ds(other * 256, 256)]
            pltpu.make_async_copy(block, block, t_recv.at[kind, other]).wait()
        for step in range(1, cols):
            spread_copy(kind, step).start()

    def token_finish(kind):
        dst_ref = (x_ref, c_ref)[kind]
        for step in range(1, cols):
            from_col = lax.rem(col + cols - step, cols)
            theirs = dst_ref.at[part_rows(from_col), :]
            pltpu.make_async_copy(theirs, theirs, a_recv.at[kind, step - 1]).wait()

    def token_drain(kind):
        for j in range(n_seq):
            for i in range(n_part):
                is_here, far, near = token_copy(kind, j, i)
                pl.when(jnp.logical_not(is_here))(far.wait_send)
        for step in range(1, cols):
            spread_copy(kind, step).wait_send()

    me = row * DPS + dp

    def small_copy(step):
        flat = lax.rem(me + step, ROWS * DPS)
        return remote(
            small_ref, smalls.at[me], m_send.at[step - 1], m_recv.at[step - 1], (lax.rem(flat, DPS), flat // DPS, col)
        )

    def place(w, r, d, half=None):
        return slot(w, full[w], r, d, own[w].shape[0], half)

    def source(w, k, half=None):
        if k == 0:
            return own[w] if half is None else half_of(w, own[w], half)
        return place(w, order[k], dp, half)

    def line_copies(w, k):
        src = source(w, k)
        dst = place(w, order[k], dp)
        recv = z_recv.at[w, order[k]]
        if k == 0:
            return [
                (None, remote(src, dst, z_send.at[w, 0], recv, (dp, at(1 - side), col))),
                (middle, remote(src, dst, z_send.at[w, 1], recv, (dp, at(2), col))),
            ]
        onward = at(2) if k == 1 else at(0)
        return [(middle, remote(src, dst, z_send.at[w, k + 1], recv, (dp, onward, col)))]

    def first_copies(w, k):
        out = []
        for half, target in ((0, across), (1, along)):
            out.append(
                remote(source(w, k, half), place(w, order[k], dp, half), s1_send.at[w, k, half],
                       s1_recv.at[w, k, half], (target, row, col))
            )
        return out

    def second_copies(w, k, which):
        out = []
        for half, target, other in ((0, along, across), (1, across, along)):
            if which == 0:
                src, owner = source(w, k, half), dp
            else:
                src, owner = place(w, order[k], other, half), other
            out.append(
                remote(src, place(w, order[k], owner, half), s2_send.at[w, k, which, half],
                       s2_recv.at[w, k, which, half], (target, row, col))
            )
        return out

    def onward(w, k):
        if k > 0:
            block = place(w, order[k], dp)
            pltpu.make_async_copy(block, block, z_recv.at[w, order[k]]).wait()
        for cond, copy in line_copies(w, k):
            if cond is None:
                copy.start()
            else:
                pl.when(cond)(copy.start)

    def sideways(w, k):
        for copy in first_copies(w, k) + second_copies(w, k, 0):
            copy.start()

    def arrived(w, k):
        onward(w, k)
        sideways(w, k)

    def passed(w, k):
        for copy in first_copies(w, k):
            copy.wait_recv()
        for copy in second_copies(w, k, 1):
            copy.start()

    def finished(w):
        for k in range(ROWS):
            for which in range(2):
                for copy in second_copies(w, k, which):
                    copy.wait_recv()

    def drained(w, k):
        for cond, copy in line_copies(w, k):
            if cond is None:
                copy.wait_send()
            else:
                pl.when(cond)(copy.wait_send)
        for copy in first_copies(w, k) + second_copies(w, k, 0) + second_copies(w, k, 1):
            copy.wait_send()

    def home(w):
        return pltpu.make_async_copy(own[w], place(w, row, dp), l_sem.at[w])

    def begin(w):
        loads[w].wait()
        own[w][...] = stage[w][...].astype(BF)
        home(w).start()

    small_home = pltpu.make_async_copy(small_ref, smalls.at[me], l_sem.at[N_W])
    kept = []

    def keep(src, dst):
        copy = pltpu.make_async_copy(src, dst, l_sem.at[N_W + 1 + len(kept)])
        copy.start()
        kept.append(copy)

    def smalls_start():
        small_home.start()
        for step in range(1, ROWS * DPS):
            small_copy(step).start()

    def norm(served):
        small_home.wait()
        for step in range(1, ROWS * DPS):
            small_copy(step).wait()
        read_gains(smalls, gains)
        if aligned:
            read_bias(smalls, bias_row, 9 + n_q // (DPS * 128), n_u // DPS)
        else:
            bias_row[...] = bias_in[...]
        branch[...] = jnp.zeros(branch.shape, F32)
        comb[...] = jnp.zeros(comb.shape, F32)
        token_finish(0)
        first, first_t = hidden.at[:, pl.ds(0, D)], hidden.at[:, pl.ds(D, D)]
        norm_stage(x_ref, gains, ((0, first, first_t), (2, second, second_t)), served)
        keep(x_ref, x_out)
        keep(smalls, smalls_out)
        keep(first, first_out)
        keep(first_t, first_t_out)

    def act(word):
        kind, rest = word[0], [int(d) for d in word[1:]]
        {
            "b": begin, "z": onward, "s": sideways, "p": passed, "t": token_start, "d": token_spread, "m": smalls_start,
        }[kind](*rest)

    def forward(served):
        home(UP).wait()
        finished(UP)
        for copy in kept[2:4]:
            copy.wait()

        def block(n, carry):
            cut = span(n * width, width, width)

            def body(j, carry):
                rows = span(j * 256, 256, 256)
                value, slant = gelu_parts(nn(second[rows, :], wu[:, cut]) + bias_row[0:1, cut])
                hidden[rows, cut] = value.astype(BF)
                slope[rows, cut] = slant
                return carry

            lax.fori_loop(0, SEQ_LEN // 256, body, 0)
            served(n)
            return carry

        lax.fori_loop(0, blocks, block, 0)

    def down_grads(served):
        token_finish(1)
        keep(c_ref, c_out)
        h = gp.shape[3]

        def block(n, carry):
            turned = hidden[:, span(n * width, width, width)].T
            if blocks == DPS:
                for half in range(2):
                    gp[n // 2, lax.rem(n, 2), half] = nn(turned[half * h : (half + 1) * h, :], c_ref[...]).astype(BF)
            else:
                gp[...] = nn(turned, c_ref[...]).astype(BF).reshape(2, 2, 2, h, D)
            served(n)
            return carry

        lax.fori_loop(0, blocks, block, 0)
        keep(gp, gp_out)

    def backward(served):
        home(DOWN).wait()
        finished(DOWN)
        sum_out[...] = jnp.zeros(sum_out.shape, F32)

        def block(n, carry):
            cut = span(n * width, width, width)

            def body(j, carry):
                rows = span(j * 256, 256, 256)
                grad = (nt(c_ref[rows, :], wp[cut, :]) * slope[rows, cut]).astype(BF)
                ghp[rows, :] = grad
                branch[rows, :] += nn(hidden[rows, cut], wp[cut, :])
                comb[rows, :] += nt(grad, wu[:, cut])
                sum_out[0:1, cut] += jnp.sum(grad.astype(F32), axis=0, keepdims=True)
                return carry

            for part_of in range(2):
                lax.fori_loop(2 * part_of, 2 * part_of + 2, body, 0)
                served(n, part_of, 3)

            def up_body(r, carry):
                value = nn(second_t[span(r * 256, 256, 256), :], ghp[...]).astype(BF)
                gu[r, :, :, :, :, cut] = value.reshape(2, 2, 2, 32, width)
                return carry

            lax.fori_loop(0, ROWS, up_body, 0)
            served(n, 2, 3)
            return carry

        lax.fori_loop(0, blocks, block, 0)

    loops = {"N": (8, norm), "P": (blocks, forward), "D": (blocks, down_grads), "B": (3 * blocks, backward)}
    plan = GATHER_PLAN
    if blocks != DPS:
        plan = [word for word in plan if word[0] not in loops]
        for kind in "NPDB":
            plan = plan + parts_of(kind, loops[kind][0])
    run(plan, loops, act)
    for src, dst in ((gu, gu_out), (branch, branch_out), (comb, comb_out)):
        keep(src, dst)
    for w in (QKV, DENSE):
        home(w).wait()
        finished(w)
    for w in range(N_W):
        for k in range(ROWS):
            drained(w, k)
    for kind in range(2):
        token_drain(kind)
    for copy in kept[:2] + kept[4:]:
        copy.wait()


def gather(tokens_in, cotangent, small, bias, weights, cols, aligned):
    wq, wu, wd, wp = weights
    n_q, n_u = wq.shape[1], wu.shape[1]
    att_width, h_p = wd.shape[0] * DPS, wp.shape[0]
    width = 512 if n_u == DPS * 512 else n_u
    any_spec = pl.BlockSpec(memory_space=pl.ANY)
    vmem = pl.BlockSpec(memory_space=pltpu.VMEM)
    shape = jax.ShapeDtypeStruct
    smalls = (ROWS * DPS,) + small.shape
    square = (SEQ_LEN, D)
    up_shape, down_shape = (ROWS, 2, 2, 2, 32, n_u), (2, 2, 2, h_p // 2, D)
    out_shape = [
        shape(square, BF), shape(square, BF), shape(smalls, F32), shape((D, n_q), BF), shape((att_width, D), BF),
        shape(square, BF), shape(square, BF), shape(up_shape, BF), shape(down_shape, BF), shape(square, F32),
        shape(square, F32), shape((1, n_u), F32),
    ]
    tok_col = tokens_in.shape[0]
    pieces = tok_col // (SEQ_LEN // cols)
    dma = pltpu.SemaphoreType.DMA
    buf = pltpu.VMEM
    scratch = [buf(w.shape, BF) for w in weights] + [buf(w.shape, F32) for w in weights]
    scratch += [
        buf(square, BF), buf(square, BF), buf(smalls, F32), buf((D, n_u), BF), buf((n_u, D), BF),
        buf((8, D), F32), buf((1, n_u), F32), buf(square, BF), buf(square, BF),
        buf((SEQ_LEN, max(n_u, 2 * D)), BF), buf((SEQ_LEN, n_u), F32), buf((SEQ_LEN, width), BF), buf(up_shape, BF), buf(down_shape, BF), buf(square, F32),
        buf(square, F32),
        dma((N_W, 5)), dma((N_W, 4)), dma((N_W, 4, 2)), dma((N_W, 4, 2)), dma((N_W, 4, 2, 2)), dma((N_W, 4, 2, 2)),
        dma((2, pieces)), dma((2, 4)), dma((2, cols - 1)), dma((2, cols - 1)),
        dma((ROWS * DPS - 1,)), dma((ROWS * DPS - 1,)), dma((N_W + 10,)),
    ]
    return pl.pallas_call(
        functools.partial(gather_kernel, cols, aligned),
        out_shape=out_shape,
        in_specs=[any_spec] * 3 + [vmem] + [any_spec] * 4,
        out_specs=[any_spec] * 11 + [vmem],
        scratch_shapes=scratch,
        compiler_params=pltpu.CompilerParams(collective_id=0, has_side_effects=True, vmem_limit_bytes=60 << 20),
    )(tokens_in, cotangent, small, bias, wq, wu, wd, wp)


SCATTER_PLAN = (
    "f0", "f1", "J0", "J1", "J2", "J3", "f2", "U", "H0", "H1", "H2", "H3", "H4", "H5", "g0", "f3", "H6", "H7",
    "H8", "H9", "H10", "H11", "H12", "H13", "g1", "H14", "H15", "f4", "H16", "H17", "h0", "g2", "H18", "H19",
    "H20", "H21", "h1", "g3", "g4", "q0", "H22", "H23", "H24", "H25", "h2", "h3", "H26", "H27", "H28", "H29", "f5",
    "q1", "H30", "H31", "q2", "h4", "T", "q3", "r0", "q4", "r1", "g5", "f6", "u0", "X", "W0", "W1", "W2", "W3",
    "g6", "r2", "f7", "u1", "f8", "h5", "G0", "G1", "G2", "G3", "g7", "h6", "Y", "g8", "f9", "u2", "r3", "h7",
    "f10", "q5", "h8", "v0", "q6", "g9", "v1", "f11", "v2", "q7", "h9", "u3", "g10", "h10", "g11", "q8", "r4",
    "r5", "q9", "r6", "u4", "v3", "u5", "r7", "r8", "q10", "h11", "q11", "u6", "u7", "u8", "r9", "u9", "r10", "v4",
    "u10", "r11", "u11",
)
PIECES = 12


def add_into(dst, src):
    shape = dst.shape
    outer, height = shape[:-2], shape[-2]
    step = min(32, height)
    per = height // step
    total = math.prod(outer) * per

    def body(i, carry):
        index, rest = [], i // per
        for size in reversed(outer):
            index.append(lax.rem(rest, size))
            rest = rest // size
        where = tuple(reversed(index)) + (span(lax.rem(i, per) * step, step, step),)
        dst[where] = (dst[where].astype(F32) + src[where].astype(F32)).astype(BF)
        return carry

    lax.fori_loop(0, total, body, 0)


def pieces_of(n_q, n_u, h_d, h_p):
    out = []

    def columns(w, n):
        size = 512 if n % 512 == 0 else n
        out.extend((w, start, size) for start in range(0, n, size))

    columns(UP, n_u)
    half = h_p // 2
    size = 64 if half % 64 == 0 else half
    out.extend((DOWN, start, size) for start in range(0, half, size))
    out.append((DENSE, 0, h_d // 2))
    columns(QKV, n_q)
    return out


def scatter_kernel(cols, aligned, pieces, *refs):
    n_p = len(pieces)
    (prefix_ref, smalls, angles, bias_in, sum_u, x_in, c_in, wq_in, wd_in, first_in, first_t_in, gu_in, gp_in, branch_in,
     comb_in) = refs[:15]
    (lo_out, gt_out, oq, ou, od, op, sm_out) = refs[15:22]
    (wq, wd, x_ref, c_ref, first, first_t, q_t, k_t, v_t, up_t, att_t, gm_t, grad_q, grad_k, grad_v) = refs[22:37]
    (gq, gd, att, branch, comb, branch_got, comb_got, gains, bias_row, out_bias, sm, sm_got, gain_sum) = refs[37:50]
    mine_u, mine_p = refs[50:52], refs[52:54]
    base = 54

    def buffers(start):
        return [refs[start + 2 * i : start + 2 * i + 2] for i in range(n_p)]

    got1, got2, got_end, got_mid = [buffers(base + 2 * n_p * n) for n in range(4)]
    (l_sem, f_sem, s1_send, s1_recv, s2_send, s2_recv, e_send, e_recv, m_send, m_recv, b_send, b_recv, d_send, d_recv,
     t_send, t_recv, v_send, v_recv) = refs[base + 8 * n_p :]
    dp, row, col, across, along = places()
    x, y = lax.rem(dp, 2), dp // 2
    side, at = line_order(row)
    far_end = row // 2
    middle, end = side == 1, side == 0
    n_q, n_u = wq_in.shape[1], sum_u.shape[1]
    heads = q_t.shape[0]
    tok_col = lo_out.shape[0]
    part = SEQ_LEN // cols

    def load(src, dst, n):
        return pltpu.make_async_copy(src, dst, l_sem.at[n])

    loads = [load(first_in, first, 0), load(wq_in, wq, 1), load(wd_in, wd, 2), load(c_in, c_ref, 3), load(first_t_in, first_t, 4),
             load(branch_in, branch, 5), load(comb_in, comb, 6), load(x_in, x_ref, 7)]
    for one in loads:
        one.start()
    group = [(dp, lax.rem(row + step, ROWS), lax.rem(col + other, cols)) for step in range(ROWS) for other in range(cols)]
    greet([(across, row, col), (along, row, col)] + group[1:])

    def view(i, half, other):
        w, start, size = pieces[i]
        if half == 0:
            place_y, place_x = (1 - y if other else y), slice(None)
        else:
            place_y, place_x = slice(None), (1 - x if other else x)
        cut = pl.ds(start, size)
        if w in (QKV, UP):
            if w == UP and not other:
                return mine_u[half].at[:, :, :, cut]
            return (gu_in if w == UP else gq).at[:, place_y, place_x, half, :, cut]
        if w == DOWN and not other:
            return mine_p[half].at[:, cut, :]
        return (gp_in if w == DOWN else gd).at[place_y, place_x, half, cut, :]

    def fetch(i, half):
        w, start, size = pieces[i]
        place_y, place_x = (y, slice(None)) if half == 0 else (slice(None), x)
        cut = pl.ds(start, size)
        src = gu_in.at[:, place_y, place_x, half, :, cut] if w == UP else gp_in.at[place_y, place_x, half, cut, :]
        return pltpu.make_async_copy(src, view(i, half, False), f_sem.at[i, half])

    def first_copy(i, half):
        target = along if half == 0 else across
        return remote(view(i, half, True), got1[i][half], s1_send.at[i, half], s1_recv.at[i, half], (target, row, col))

    def keep(i, half, other):
        which = x if half == 0 else y
        which = 1 - which if other else which
        kept = view(i, half, False)
        return kept.at[:, which] if pieces[i][0] in (QKV, UP) else kept.at[which]

    def second_copy(i, half):
        target = across if half == 0 else along
        return remote(keep(i, half, True), got2[i][half], s2_send.at[i, half], s2_recv.at[i, half], (target, row, col))

    def lines(i, ref, start, count):
        if pieces[i][0] in (QKV, UP):
            return ref.at[pl.ds(start, count)]
        return ref.at[:, span(start * 256, count * 256, 256)]

    def end_copy(i, half):
        src = lines(i, keep(i, half, False), 1 - far_end, 3)
        return remote(src, got_end[i][half], e_send.at[i, half], e_recv.at[i, half], (dp, at(1), col))

    def mid_copy(i, half):
        src = lines(i, keep(i, half, False), 2 * (1 - far_end), 2)
        return remote(src, got_mid[i][half], m_send.at[i, half], m_recv.at[i, half], (dp, at(2), col))

    def back_copy(i, half):
        src = lines(i, keep(i, half, False), at(0), 1)
        return remote(src, lines(i, got_mid[i][half], 0, 1), b_send.at[i, half], b_recv.at[i, half], (dp, at(0), col))

    def begin(i):
        for half in range(2):
            first_copy(i, half).start()
            if pieces[i][0] in (UP, DOWN):
                fetch(i, half).start()

    def stage_two(i):
        for half in range(2):
            if pieces[i][0] in (UP, DOWN):
                fetch(i, half).wait()
            first_copy(i, half).wait_recv()
            add_into(view(i, half, False), got1[i][half])
            second_copy(i, half).start()

    def stage_three(i):
        for half in range(2):
            second_copy(i, half).wait_recv()
            add_into(keep(i, half, False), got2[i][half])

            @pl.when(end)
            def _():
                end_copy(i, half).start()

    def stage_four(i):
        @pl.when(middle)
        def _():
            for half in range(2):
                end_copy(i, half).wait_recv()
                add_into(lines(i, keep(i, half, False), 2 * (1 - far_end), 2), lines(i, got_end[i][half], 1 - far_end, 2))
                mid_copy(i, half).start()

    def stage_five(i):
        @pl.when(middle)
        def _():
            for half in range(2):
                mid_copy(i, half).wait_recv()
                add_into(lines(i, keep(i, half, False), at(0), 1), lines(i, got_mid[i][half], far_end, 1))
                back_copy(i, half).start()

    def stage_six(i):
        w, start, size = pieces[i]
        out = (oq, ou, od, op)[w]
        for half in range(2):
            mine = lines(i, keep(i, half, False), row, 1)

            def total(others):
                if w in (QKV, UP):
                    value = mine[0].astype(F32)
                    for other in others:
                        value = value + other[0].astype(F32)
                    out[half, :, pl.ds(start, size)] = value
                else:
                    value = mine[...].astype(F32)
                    for other in others:
                        value = value + other[...].astype(F32)
                    out[half, pl.ds(start, size), :] = value

            @pl.when(end)
            def _():
                back_copy(i, half).wait_recv()
                total([lines(i, got_mid[i][half], 0, 1)])

            @pl.when(middle)
            def _():
                total([lines(i, got_end[i][half], 2 * far_end, 1), lines(i, got_mid[i][half], 1 - far_end, 1)])

    def drain(i):
        for half in range(2):
            first_copy(i, half).wait_send()
            second_copy(i, half).wait_send()

            @pl.when(end)
            def _():
                end_copy(i, half).wait_send()

            @pl.when(middle)
            def _():
                mid_copy(i, half).wait_send()
                back_copy(i, half).wait_send()

    def part_rows(piece):
        return span(piece * part, part, part)

    def col_copy(kind, n):
        other = lax.rem(col + n, cols)
        src = (branch, comb)[kind].at[part_rows(other), :]
        dst = (branch_got, comb_got)[kind].at[n - 1]
        return remote(src, dst, d_send.at[kind, n - 1], d_recv.at[kind, n - 1], (dp, row, other))

    start = row * SEQ_LEN + col * part
    owner, offset = start // tok_col, lax.rem(start, tok_col)

    def out_copy(kind, r):
        src = first.at[pl.ds(kind * part, part), span(r * 256, 256, 256)]
        dst = (lo_out, gt_out)[kind].at[span(offset, part, part), :]
        recv = t_recv.at[kind, offset // part]
        here = jnp.logical_and(row == r, owner == col)
        far = remote(src, dst, t_send.at[kind, r], recv, (dp, r, owner))
        return here, far, pltpu.make_async_copy(src, dst, recv)

    def out_start(kind):
        for r in (at(1 - side), at(2), at(3), row):
            here, far, near = out_copy(kind, r)
            pl.when(jnp.logical_not(here))(far.start)
            pl.when(here)(near.start)

    def out_finish(kind):
        for r in range(ROWS):
            here, far, near = out_copy(kind, r)
            pl.when(jnp.logical_not(here))(far.wait_send)
        out = (lo_out, gt_out)[kind]
        for n in range(tok_col // part):
            block = out.at[pl.ds(n * part, part), :]
            pltpu.make_async_copy(block, block, t_recv.at[kind, n]).wait()

    height = min(128, part)

    def finish_rows(kind):
        for n in range(1, cols):
            col_copy(kind, n).wait_recv()

        def body(i, carry):
            here = span(i * height, height, height)
            rows = span(col * part + i * height, height, height)
            value = (branch, comb)[kind][rows, :]
            for n in range(1, cols):
                value = value + (branch_got, comb_got)[kind][n - 1, here, :]
            wide = x_ref[rows, :].astype(F32)
            if kind == 0:
                value = wide + value + out_bias[0:1, :]
            else:
                normed, scale_inv = norm_rows(wide)
                mean = jnp.mean(value, axis=1, keepdims=True)
                cross = jnp.mean(value * normed, axis=1, keepdims=True)
                value = c_ref[rows, :].astype(F32) + scale_inv * (value - mean - normed * cross)
            first[span(kind * part + i * height, height, height), :] = value.astype(BF)
            return carry

        lax.fori_loop(0, part // height, body, 0)

    def small_copy(n):
        if n < 2:
            return remote(sm.at[n], sm_got.at[n], v_send.at[n], v_recv.at[n], ((across, along)[n], row, col))
        if n < 5:
            target = (dp, lax.rem(row + n - 1, ROWS), col)
            return remote(sm.at[2], sm_got.at[n], v_send.at[n], v_recv.at[n], target)
        target = (dp, row, lax.rem(col + n - 4, cols))
        return remote(sm.at[3], sm_got.at[n], v_send.at[n], v_recv.at[n], target)

    def small_step(n):
        if n > 0:
            waits = ((0,), (1,), (2, 3, 4), tuple(range(5, 4 + cols)))[n - 1]
            for m in waits:
                small_copy(m).wait_recv()
            value = sm[n - 1]
            if n < 4:
                for m in waits:
                    value = value + sm_got[m]
                sm[n] = value
            else:
                sm_out[...] = value
                value = value[0:4]
                for m in waits:
                    value = value + sm_got[m, 0:4, :]
                sm_out[0:4, :] = value
        for m in ((0,), (1,), (2, 3, 4), tuple(range(5, 4 + cols)), ())[n]:
            small_copy(m).start()

    def project(served):
        read_gains(smalls, gains)
        lanes = lax.broadcasted_iota(jnp.int32, (1, 128), 1)
        for r in range(ROWS):
            for d in range(0, DPS, 2):
                both = [rounded(smalls[r * DPS + d + n, 8:9, :]) for n in range(2)]
                both = [value + pltpu.roll(value, 64, 1) for value in both]
                out_bias[0:1, pl.ds(r * 256 + d * 64, 128)] = jnp.where(lanes < 64, both[0], both[1])
        if aligned:
            read_bias(smalls, bias_row, 9, n_q // DPS)
        else:
            bias_row[...] = bias_in[...]
        sm[0] = jnp.zeros(sm.shape[1:], F32)
        sm[0, 6:7, 0:n_u] = sum_u[...]
        loads[0].wait()
        loads[1].wait()
        project_stage(wq, first, bias_row, angles, q_t, k_t, v_t, heads, served)

    def upstream():
        loads[2].wait()
        loads[3].wait()
        upstream_stage(wd, c_ref, up_t, heads)

    def attended():
        group_h = min(heads, 4)

        def turn_body(i, carry):
            block = att_t[pl.ds(i * group_h, group_h)].reshape(group_h * HD, SEQ_LEN)
            spot = pl.ds(0, group_h * HD) if heads == group_h else span(i * group_h * HD, group_h * HD, 128)
            att[:, spot] = block.T
            return carry

        lax.fori_loop(0, heads // group_h, turn_body, 0)
        loads[5].wait()

        def out_body(j, carry):
            rows = span(j * 256, 256, 256)
            branch[rows, :] += nn(att[rows, :], wd[...])
            return carry

        lax.fori_loop(0, SEQ_LEN // 256, out_body, 0)
        for n in range(1, cols):
            col_copy(0, n).start()

    def weight_grads(n):
        if n == 0:
            all_heads = att_t[...].reshape(heads * HD, SEQ_LEN)
            gd[...] = nn(all_heads, c_ref[...]).astype(BF).reshape(gd.shape)
            return
        if n == 1:
            loads[4].wait()
        wide = min(512, n_q)
        cut = pl.ds((n - 1) * wide, wide)

        def qkv_body(r, carry):
            rows = span(r * 256, 256, 256)
            gq[r, :, :, :, :, cut] = nt(first_t[rows, :], gm_t[cut, :]).astype(BF).reshape(2, 2, 2, 32, wide)
            return carry

        lax.fori_loop(0, ROWS, qkv_body, 0)

    need_x = [loads[7]]

    def output_home():
        if len(need_x):
            need_x.pop().wait()
        finish_rows(0)
        out_start(0)

    def features(served):
        loads[6].wait()
        if len(need_x):
            need_x.pop().wait()
        for n in range(8):
            gain_sum[n : n + 1, :] = jnp.zeros((1, D), F32)

        def body(j, carry):
            rows = span(j * 256, 256, 256)
            grad = gm_t[:, rows].T
            grad_first = nt(grad, wq[...])
            grad_second = comb[rows, :]
            normed, ignored = norm_rows(x_ref[rows, :].astype(F32))
            for n, value in enumerate((normed * grad_first, grad_first, normed * grad_second, grad_second,
                                       c_ref[rows, :].astype(F32))):
                gain_sum[n : n + 1, :] += jnp.sum(value, axis=0, keepdims=True)
            sm[0, 5:6, 0:n_q] += jnp.sum(grad.astype(F32), axis=0, keepdims=True)
            comb[rows, :] = gains[0:1, :] * grad_first + gains[2:3, :] * grad_second
            served(j)
            return carry

        lax.fori_loop(0, SEQ_LEN // 256, body, 0)
        for n in range(1, cols):
            col_copy(1, n).start()
        sm[0, 0:5, 0:D] = gain_sum[0:5, :]

    def gradient_home():
        finish_rows(1)
        out_start(1)

    stages = {"f": begin, "g": stage_two, "h": stage_three, "q": stage_four, "r": stage_five, "u": stage_six}
    others = {"U": upstream, "T": attended, "X": output_home, "Y": gradient_home}

    def act(word):
        kind, rest = word[0], word[1:]
        if kind in others:
            others[kind]()
        elif kind == "W":
            weight_grads(int(rest))
        elif kind == "v":
            small_step(int(rest))
        else:
            stages[kind](int(rest))

    def attention(served):
        prefix = prefix_ref[0]

        def head_body(h, carry):
            attend_head(h, prefix, angles, q_t, k_t, v_t, up_t, att_t, gm_t, grad_q, grad_k, grad_v, served)
            return carry

        lax.fori_loop(0, heads, head_body, 0)

    loops = {
        "J": (heads // min(heads, 2), project), "H": (heads * (SEQ_LEN // 256), attention), "G": (SEQ_LEN // 256, features),
    }
    plan = SCATTER_PLAN
    if n_p != PIECES:
        late = [i for i in range(n_p) if pieces[i][0] in (QKV, DENSE)]
        plan = ["f%d" % i for i in range(n_p) if i not in late] + parts_of("J", loops["J"][0]) + ["U"]
        plan = plan + parts_of("H", loops["H"][0]) + ["T", "W0", "W1", "X"] + parts_of("G", loops["G"][0]) + ["Y"]
        plan = plan + ["f%d" % i for i in late] + [s + str(i) for s in "ghqru" for i in range(n_p)] + parts_of("v", 5)
    run(plan, loops, act)
    for i in range(n_p):
        drain(i)
    for kind in range(2):
        out_finish(kind)
    for n in range(1, cols):
        for kind in range(2):
            col_copy(kind, n).wait_send()
    for n in range(4 + cols):
        small_copy(n).wait_send()


def scatter(prefix_len, smalls, angles, bias, sum_u, own_x, own_cot, wq, wd, first, first_t, gu, gp, branch, comb, cols, aligned,
            tok_col):
    any_spec = pl.BlockSpec(memory_space=pl.ANY)
    vmem = pl.BlockSpec(memory_space=pltpu.VMEM)
    smem = pl.BlockSpec(memory_space=pltpu.SMEM)
    dma = pltpu.SemaphoreType.DMA
    buf = pltpu.VMEM
    shape = jax.ShapeDtypeStruct
    n_q, n_u = wq.shape[1], sum_u.shape[1]
    heads = n_q // 192
    h_d, h_p = wd.shape[0] // DPS, 2 * gp.shape[3]
    pieces = pieces_of(n_q, n_u, h_d, h_p)
    n_p = len(pieces)
    part = SEQ_LEN // cols
    line = max(n_q, n_u, D)
    square = (SEQ_LEN, D)
    turned = buf((heads, HD, SEQ_LEN), BF)
    scratch = [
        buf((D, n_q), BF), buf(wd.shape, BF), buf(square, BF), buf(square, BF), buf(square, BF), buf(square, BF),
        turned, turned, turned, turned, turned, buf((n_q, SEQ_LEN), BF),
        buf((HD, SEQ_LEN), F32), buf((HD, SEQ_LEN), F32), buf((HD, SEQ_LEN), F32),
        buf((ROWS, 2, 2, 2, 32, n_q), BF), buf((2, 2, 2, h_d // 2, D), BF), buf((SEQ_LEN, heads * HD), BF), buf(square, F32), buf(square, F32),
        buf((cols - 1, part, D), F32), buf((cols - 1, part, D), F32),
        buf((8, D), F32), buf((1, n_q), F32), buf((1, D), F32), buf((4, 8, line), F32), buf((4 + cols, 8, line), F32),
        buf((8, D), F32),
    ]
    scratch += [buf((ROWS, 2, 32, n_u), BF)] * 2 + [buf((2, h_p // 2, D), BF)] * 2
    for lead, count in (((ROWS, 2), None), ((ROWS,), None), ((3,), 3), ((2,), 2)):
        for w, start, size in pieces:
            if w in (QKV, UP):
                one = lead + (32, size)
            elif count is None:
                one = ((2,) if len(lead) == 2 else ()) + (size, D)
            else:
                one = (size, 256 * count)
            scratch += [buf(one, BF)] * 2
    scratch += [
        dma((8,)), dma((n_p, 2)), dma((n_p, 2)), dma((n_p, 2)), dma((n_p, 2)), dma((n_p, 2)), dma((n_p, 2)), dma((n_p, 2)),
        dma((n_p, 2)), dma((n_p, 2)), dma((n_p, 2)), dma((n_p, 2)), dma((2, cols - 1)), dma((2, cols - 1)),
        dma((2, ROWS)), dma((2, tok_col // part)), dma((4 + cols,)), dma((4 + cols,)),
    ]
    return pl.pallas_call(
        functools.partial(scatter_kernel, cols, aligned, pieces),
        out_shape=[
            shape((tok_col, 256), BF), shape((tok_col, 256), BF), shape((2, 32, n_q), F32), shape((2, 32, n_u), F32),
            shape((2, h_d // 2, 256), F32), shape((2, h_p // 2, 256), F32), shape((8, line), F32),
        ],
        in_specs=[smem, vmem, vmem, vmem, vmem] + [any_spec] * 10,
        out_specs=[any_spec] * 2 + [vmem] * 5,
        scratch_shapes=scratch,
        compiler_params=pltpu.CompilerParams(collective_id=1, has_side_effects=True, vmem_limit_bytes=63 << 20),
    )(prefix_len, smalls, angles, bias, sum_u, own_x, own_cot, wq, wd, first, first_t, gu, gp, branch, comb)


def finish_kernel(*refs):
    whole_in, sums, whole_out, q_b, u_b, d_b, p_b, gains, rooms, sem = (
        refs[:6], refs[6], refs[7:13], *refs[13:17], refs[17:21], refs[21:27], refs[27]
    )
    arrive = [pltpu.make_async_copy(src, dst, sem.at[0, n]) for n, (src, dst) in enumerate(zip(whole_in, rooms))]
    leave = [pltpu.make_async_copy(src, dst, sem.at[1, n]) for n, (src, dst) in enumerate(zip(rooms, whole_out))]
    for copy in arrive:
        copy.start()
    dp, row = lax.axis_index("dp"), lax.axis_index("row")
    for n, gain in enumerate(gains):
        gain[...] = sums[n : n + 1, span(row * 256, 256, 256)].reshape(gain.shape)
    for n, bias in ((5, q_b), (6, u_b)):
        size = bias.shape[0]
        bias[...] = sums[n : n + 1, span(dp * size, size, 128)].reshape(bias.shape)
    me = row * DPS + dp
    pair = sums[4:5, span((me // 2) * 128, 128, 128)]
    pair = jnp.where(lax.rem(me, 2) == 0, pair, pltpu.roll(pair, 64, 1))
    for bias in (d_b, p_b):
        bias[...] = pair[:, 0:64].reshape(bias.shape)
    for first, then in zip(arrive, leave):
        first.wait()
        then.start()
    for copy in leave:
        copy.wait()


def finish(whole, sums, n_qb, n_ub):
    any_spec = pl.BlockSpec(memory_space=pl.ANY)
    vmem = pl.BlockSpec(memory_space=pltpu.VMEM)
    shape = jax.ShapeDtypeStruct
    sizes = [n_qb, n_ub, 64, 64] + [256] * 4
    out = pl.pallas_call(
        finish_kernel,
        out_shape=[shape(a.shape, a.dtype) for a in whole] + [shape((size,), F32) for size in sizes],
        in_specs=[any_spec] * 6 + [vmem],
        out_specs=[any_spec] * 6 + [vmem] * 8,
        scratch_shapes=[pltpu.VMEM(a.shape, a.dtype) for a in whole] + [pltpu.SemaphoreType.DMA((2, 6))],
    )(*whole, sums)
    lo, gt, gq, gu, gd, gp, q_b, u_b, d_b, p_b, *gains = out
    return (lo, gt, gq, q_b, gu, u_b, gd, d_b, gp, p_b, *gains)


def angles_table():
    half_rot = ROT // 2
    rates = np.exp(np.arange(half_rot, dtype=np.float32) * np.float32(-2.0 * math.log(10000.0) / ROT))
    turned = rates.astype(np.float32)[:, None] * np.arange(SEQ_LEN, dtype=np.float32)[None, :]
    return np.concatenate([np.cos(turned), np.sin(turned)], axis=0).astype(np.float32)


def shards(cols, tokens_in, prefix_len, first_gain, first_shift, second_gain, second_shift, qkv_weight, qkv_bias,
           up_weight, up_bias, dense_weight, dense_bias, down_weight, down_bias, cotangent):
    tok_col = tokens_in.shape[0]
    n_q, n_u = qkv_weight.shape[1], up_weight.shape[1]

    n_qb, n_ub = qkv_bias.shape[0], up_bias.shape[0]
    aligned = n_qb % 128 == 0 and n_ub % 128 == 0
    small = jnp.concatenate((first_gain, first_shift, second_gain, second_shift, dense_bias, down_bias, qkv_bias, up_bias))
    size = -(-small.shape[0] // 1024) * 1024
    small = jnp.pad(small, (0, size - small.shape[0])).reshape(size // 128, 128)
    if aligned:
        q_bias = u_bias = small
    else:
        q_bias = lax.all_gather(rounded(qkv_bias), "dp", axis=0, tiled=True).reshape(1, n_q)
        u_bias = lax.all_gather(rounded(up_bias), "dp", axis=0, tiled=True).reshape(1, n_u)
    own_x, own_cot, smalls, wq, wd, first, first_t, gu, gp, branch, comb, sum_u = gather(
        tokens_in, cotangent, small, u_bias, (qkv_weight, up_weight, dense_weight, down_weight), cols, aligned
    )
    layer_out, grad_tokens, out_q, out_u, out_d, out_p, sums = scatter(
        prefix_len, smalls, jnp.asarray(angles_table()), q_bias, sum_u, own_x, own_cot, wq, wd, first, first_t, gu, gp, branch,
        comb, cols, aligned, tok_col
    )
    h_d, h_p = dense_weight.shape[0], down_weight.shape[0]
    whole = (
        layer_out, grad_tokens, out_q.reshape(64, n_q), out_u.reshape(64, n_u), out_d.reshape(h_d, 256), out_p.reshape(h_p, 256)
    )
    if aligned:
        return finish(whole, sums, n_qb, n_ub)
    dp, row = lax.axis_index("dp"), lax.axis_index("row")
    gain_sums = lax.dynamic_slice(sums, (0, row * 256), (4, 256))
    out_b = lax.dynamic_slice(sums, (4, (row * DPS + dp) * 64), (1, 64))[0]
    q_b = lax.dynamic_slice(sums, (5, dp * n_qb), (1, n_qb))[0]
    u_b = lax.dynamic_slice(sums, (6, dp * n_ub), (1, n_ub))[0]
    return (
        whole[0], whole[1], whole[2], q_b, whole[3], u_b, whole[4], out_b, whole[5], out_b,
        gain_sums[0], gain_sums[1], gain_sums[2], gain_sums[3],
    )


def solution(mesh):
    in_specs = (
        P(("dp", "col"), "row"), P(("dp", "row")), P("row"), P("row"), P("row"), P("row"),
        P(("row", "dp"), "col"), P(("col", "dp")), P(("row", "dp"), "col"), P(("col", "dp")),
        P(("col", "dp"), "row"), P(("row", "dp")), P(("col", "dp"), "row"), P(("row", "dp")),
        P(("dp", "col"), "row"),
    )
    out_specs = (
        P(("dp", "col"), "row"), P(("dp", "col"), "row"), P(("row", "dp"), "col"), P(("col", "dp")),
        P(("row", "dp"), "col"), P(("col", "dp")), P(("col", "dp"), "row"), P(("row", "dp")),
        P(("col", "dp"), "row"), P(("row", "dp")), P("row"), P("row"), P("row"), P("row"),
    )
    body = functools.partial(shards, mesh.shape["col"])
    return jax.shard_map(body, mesh=mesh, in_specs=in_specs, out_specs=out_specs, check_vma=False)
```

```python
import functools
import math

import jax
import jax.numpy as jnp
import numpy as np
from jax import lax
from jax.experimental import pallas as pl
from jax.experimental.pallas import tpu as pltpu
from jax.sharding import PartitionSpec as P

D = 1024
HD = 64
ROT = 16
FF = 4096
SEQ_LEN = 1024
EPS = 1e-05
NEGATIVE = -1e30
ROWS = 4
DPS = 4
MESH = pl.DeviceIdType.MESH
BF = jnp.bfloat16
F32 = jnp.float32


def places():
    dp, row, col = lax.axis_index("dp"), lax.axis_index("row"), lax.axis_index("col")
    across = dp + 1 - 2 * lax.rem(dp, 2)
    along = lax.rem(dp + 2, 4)
    return dp, row, col, across, along


def line_order(row):
    far = row // 2
    side = row + far * (3 - 2 * row)
    at = lambda place: far * 3 + (1 - 2 * far) * place
    return side, at


def greet(targets):
    barrier = pltpu.get_barrier_semaphore()
    for target in targets:
        pl.semaphore_signal(barrier, inc=1, device_id=target, device_id_type=MESH)
    pl.semaphore_wait(barrier, len(targets))


def peers_of(dp, row, col, cols):
    group = []
    for step in range(1, ROWS * cols):
        flat = lax.rem(row * cols + col + step, ROWS * cols)
        group.append((dp, flat // cols, lax.rem(flat, cols)))
    for step in range(1, DPS):
        for other in range(ROWS):
            group.append((lax.rem(dp + step, DPS), lax.rem(row + other, ROWS), col))
    return group


def remote(src, dst, send, recv, target):
    return pltpu.make_async_remote_copy(
        src_ref=src, dst_ref=dst, send_sem=send, recv_sem=recv, device_id=target, device_id_type=MESH
    )


N_W = 4
QKV, UP, DENSE, DOWN = range(N_W)
GATHER_PLAN = (
    "b1", "z10", "b3", "s10", "s30", "z30", "b2", "z11", "p10", "z12", "b0", "z31", "p30", "m", "s12", "z20",
    "z13", "s00", "t0", "s13", "s31", "z32", "s11", "t1", "s20", "d0", "z21", "s32", "p13", "p12", "N0", "p11",
    "s21", "N1", "N2", "p20", "N3", "N4", "z33", "z00", "s33", "N5", "N6", "p31", "N7", "P0", "P1", "P2", "p32",
    "p33", "d1", "P3", "p00", "z01", "s01", "D0", "D1", "z22", "D2", "s22", "z23", "s23", "D3", "B0", "z02", "B1",
    "s02", "B2", "z03", "p21", "s03", "B3", "B4", "B5", "B6", "B7", "p03", "p02", "p01", "B8", "B9", "B10", "B11",
    "p23", "p22",
)


def run(words, loops, act):
    i = 0
    while i < len(words):
        kind = words[i][0]
        if kind not in loops:
            act(words[i])
            i += 1
            continue
        count, body = loops[kind]
        groups = [[]]
        i += 1
        while len(groups) < count:
            if words[i][0] == kind:
                groups.append([])
            else:
                groups[-1].append(words[i])
            i += 1

        def served(index, first=0, stride=1):
            for n, group in enumerate(groups[first::stride]):
                if group:

                    @pl.when(index == n)
                    def _():
                        for word in group:
                            act(word)

        body(served)


def parts_of(kind, count):
    return ["%s%d" % (kind, n) for n in range(count)]


def nt(left, right):
    return lax.dot_general(left, right, (((1,), (1,)), ((), ())), preferred_element_type=F32)


def nn(left, right):
    return jnp.dot(left, right, preferred_element_type=F32)


def span(start, size, unit):
    return pl.ds(pl.multiple_of(start, unit), size)


def slot(w, ref, row, dp, height, half=None):
    if w in (QKV, UP):
        if half is None:
            return ref.at[span((row * DPS + dp) * height, height, 64), :]
        return ref.at[span((row * DPS + dp) * height + half * (height // 2), height // 2, 32), :]
    if half is None:
        return ref.at[span(dp * height, height, 16), span(row * 256, 256, 256)]
    if w == DENSE:
        return ref.at[span(dp * height, height, 16), span(row * 256 + half * 128, 128, 128)]
    return ref.at[span(dp * height + half * (height // 2), height // 2, 16), span(row * 256, 256, 256)]


def half_of(w, ref, half):
    height = ref.shape[0]
    if w == DENSE:
        return ref.at[:, pl.ds(half * 128, 128)]
    return ref.at[pl.ds(half * (height // 2), height // 2), :]


def read_gains(smalls, gains):
    for r in range(ROWS):
        for g in range(4):
            for t in range(2):
                gains[g : g + 1, pl.ds(r * 256 + t * 128, 128)] = smalls[r * DPS, pl.ds(2 * g + t, 1), :]


def rounded(value):
    return value.astype(BF).astype(F32)


def read_bias(smalls, bias, first_row, size):
    per = size // 128
    for d in range(DPS):
        for t in range(per):
            bias[0:1, pl.ds(d * size + t * 128, 128)] = rounded(smalls[d, pl.ds(first_row + t, 1), :])


def norm_rows(x):
    center = jnp.mean(x, axis=1, keepdims=True)
    spread = jnp.mean(x * x, axis=1, keepdims=True) - center * center
    scale_inv = lax.rsqrt(spread + EPS)
    return (x - center) * scale_inv, scale_inv


def norm_stage(x_ref, gains, outs, served):
    def body(i, carry):
        rows = span(i * 128, 128, 128)
        normed, ignored = norm_rows(x_ref[rows, :].astype(F32))
        for which, plain, turned in outs:
            value = (normed * gains[which : which + 1, :] + gains[which + 1 : which + 2, :]).astype(BF)
            plain[rows, :] = value
            turned[:, rows] = value.T
        served(i)
        return carry

    lax.fori_loop(0, SEQ_LEN // 128, body, 0)


def project_stage(wq, first, bias_row, angles, q_t, k_t, v_t, heads, served):
    pair = min(heads, 2)
    width = 192 * pair

    def body(p, carry):
        cols = pl.ds(0, width) if heads == pair else span(p * width, width, 128)
        w_t = wq[:, cols].T
        bias = jnp.broadcast_to(bias_row[0:1, cols], (8, width)).T[:, 0:1]
        for j in range(SEQ_LEN // 256):
            toks = pl.ds(j * 256, 256)
            mixed = nt(w_t, first[toks, :]) + bias
            cos, sin = angles[0:8, toks], angles[8:16, toks]

            def turn(base):
                x1, x2 = mixed[base : base + 8], mixed[base + 8 : base + 16]
                return jnp.concatenate([x1 * cos - x2 * sin, x2 * cos + x1 * sin, mixed[base + 16 : base + 64]], axis=0)

            for e in range(pair):
                base, h = 192 * e, pair * p + e
                q_t[h, :, toks] = (turn(base) * HD ** (-0.5)).astype(BF)
                k_t[h, :, toks] = turn(base + 64).astype(BF)
                v_t[h, :, toks] = mixed[base + 128 : base + 192].astype(BF)
        served(p)
        return carry

    lax.fori_loop(0, heads // pair, body, 0)


def upstream_stage(wd, c_ref, up_t, heads):
    for j in range(SEQ_LEN // 256):
        toks = pl.ds(j * 256, 256)
        grad = nt(wd[...], c_ref[toks, :]).astype(BF)
        for h in range(heads):
            up_t[h, :, toks] = grad[HD * h : HD * (h + 1)]


def attend_head(h, prefix, angles, q_t, k_t, v_t, up_t, att_t, gm_t, grad_q, grad_k, grad_v, served):
    keys_plain, values_plain = k_t[h].T, v_t[h].T
    done = 0
    for i in range(SEQ_LEN // 256):
        low = 256 * i
        seen = max(512, low + 256)
        spot = pl.ds(low, 256)
        q, up = q_t[h, :, spot], up_t[h, :, spot]
        scores = nn(keys_plain[0:seen], q)
        plain = min(low, seen)
        keys = lax.broadcasted_iota(jnp.int32, (seen - plain, 256), 0) + plain
        queries = lax.broadcasted_iota(jnp.int32, (seen - plain, 256), 1) + low
        masked = jnp.where((keys <= queries) | (keys < prefix), scores[plain:], NEGATIVE)
        scores = jnp.concatenate([scores[:plain], masked], axis=0) if plain else masked
        exponent = jnp.exp(scores - jnp.max(scores, axis=0, keepdims=True))
        probs = exponent * (1.0 / jnp.sum(exponent, axis=0, keepdims=True))
        weights = probs.astype(BF)
        outputs = nn(v_t[h, :, 0:seen], weights)
        att_t[h, :, spot] = outputs.astype(BF)
        inner = jnp.sum(outputs * up.astype(F32), axis=0, keepdims=True)
        grad_probs = nn(values_plain[0:seen], up)
        grad_scores = (probs * (grad_probs - inner)).astype(BF)
        grad_q[:, spot] = nn(k_t[h, :, 0:seen], grad_scores)
        for total, part in ((grad_v, nt(up, weights)), (grad_k, nt(q, grad_scores))):
            if done:
                total[:, 0:done] += part[:, :done]
            if seen > done:
                total[:, done:seen] = part[:, done:]
        done = seen
        served(h, i, SEQ_LEN // 256)
    cos, sin = angles[0:8, :], angles[8:16, :]

    def turn_back(grad):
        g1, g2 = grad[0:8], grad[8:16]
        return jnp.concatenate([g1 * cos + g2 * sin, g2 * cos - g1 * sin, grad[16:]], axis=0)

    base = h * 192
    gm_t[span(base, HD, HD), :] = (turn_back(grad_q[...]) * HD ** (-0.5)).astype(BF)
    gm_t[span(base + HD, HD, HD), :] = turn_back(grad_k[...]).astype(BF)
    gm_t[span(base + 2 * HD, HD, HD), :] = grad_v[...].astype(BF)


def gelu_parts(x):
    below = 0.5 * (1.0 + lax.erf(x * (0.5**0.5)))
    density = jnp.exp(-0.5 * x * x) * (1.0 / math.sqrt(2.0 * math.pi))
    return x * below, below + x * density


def gather_kernel(cols, aligned, *refs):
    (tok_ref, cot_ref, small_ref, bias_in) = refs[:4]
    masters = refs[4:8]
    (x_out, c_out, smalls_out, gq_ref, gd_ref, first_out, first_t_out, gu_out, gp_out, branch_out, comb_out, sum_out) = refs[8:20]
    own = refs[20:24]
    stage = refs[24:28]
    (x_ref, c_ref, smalls, wu, wp, gains, bias_row, second, second_t) = refs[28:37]
    (hidden, slope, ghp, gu, gp, branch, comb) = refs[37:44]
    (z_send, z_recv, s1_send, s1_recv, s2_send, s2_recv, t_send, t_recv, a_send, a_recv, m_send, m_recv, l_sem) = refs[44:]
    full = (gq_ref, wu, gd_ref, wp)
    n_q, n_u = gq_ref.shape[1], wu.shape[1]
    width = ghp.shape[1]
    blocks = n_u // width
    dp, row, col, across, along = places()
    side, at = line_order(row)
    order = [row, at(1 - side), at(2), at(3)]
    middle = side == 1
    tok_col = tok_ref.shape[0]
    part = SEQ_LEN // cols
    chunk = min(tok_col, SEQ_LEN)
    n_seq = tok_col // chunk
    n_part = chunk // part

    loads = [pltpu.make_async_copy(masters[w], stage[w], l_sem.at[w]) for w in range(N_W)]
    for load in loads:
        load.start()
    greet(peers_of(dp, row, col, cols))

    def token_copy(kind, j, i):
        src_ref, dst_ref = ((tok_ref, x_ref), (cot_ref, c_ref))[kind]
        n = j * n_part + i
        if n_seq > 1:
            j = lax.rem(j + (n_seq - 1) * (1 - col), n_seq)
        start = col * tok_col + j * chunk
        to_row = start // SEQ_LEN
        piece = lax.rem(start, SEQ_LEN) // part + i
        src = src_ref.at[span(j * chunk + i * part, part, part), :]
        dst = dst_ref.at[span(piece * part, part, part), span(row * 256, 256, 256)]
        sends, recvs = t_send.at[kind, n], t_recv.at[kind, row]
        is_here = jnp.logical_and(to_row == row, piece == col)
        far = remote(src, dst, sends, recvs, (dp, to_row, piece))
        near = pltpu.make_async_copy(src, dst, recvs)
        return is_here, far, near

    def token_start(kind):
        for j in range(n_seq):
            for i in range(n_part):
                is_here, far, near = token_copy(kind, j, i)
                pl.when(jnp.logical_not(is_here))(far.start)
                pl.when(is_here)(near.start)

    def part_rows(piece):
        return span(piece * part, part, part)

    def spread_copy(kind, step):
        mine = (x_ref, c_ref)[kind].at[part_rows(col), :]
        to_col = lax.rem(col + step, cols)
        return remote(mine, mine, a_send.at[kind, step - 1], a_recv.at[kind, step - 1], (dp, row, to_col))

    def token_spread(kind):
        dst_ref = (x_ref, c_ref)[kind]
        for other in range(ROWS):
            block = dst_ref.at[part_rows(col), pl.ds(other * 256, 256)]
            pltpu.make_async_copy(block, block, t_recv.at[kind, other]).wait()
        for step in range(1, cols):
            spread_copy(kind, step).start()

    def token_finish(kind):
        dst_ref = (x_ref, c_ref)[kind]
        for step in range(1, cols):
            from_col = lax.rem(col + cols - step, cols)
            theirs = dst_ref.at[part_rows(from_col), :]
            pltpu.make_async_copy(theirs, theirs, a_recv.at[kind, step - 1]).wait()

    def token_drain(kind):
        for j in range(n_seq):
            for i in range(n_part):
                is_here, far, near = token_copy(kind, j, i)
                pl.when(jnp.logical_not(is_here))(far.wait_send)
        for step in range(1, cols):
            spread_copy(kind, step).wait_send()

    me = row * DPS + dp

    def small_copy(step):
        flat = lax.rem(me + step, ROWS * DPS)
        return remote(
            small_ref, smalls.at[me], m_send.at[step - 1], m_recv.at[step - 1], (lax.rem(flat, DPS), flat // DPS, col)
        )

    def place(w, r, d, half=None):
        return slot(w, full[w], r, d, own[w].shape[0], half)

    def source(w, k, half=None):
        if k == 0:
            return own[w] if half is None else half_of(w, own[w], half)
        return place(w, order[k], dp, half)

    def line_copies(w, k):
        src = source(w, k)
        dst = place(w, order[k], dp)
        recv = z_recv.at[w, order[k]]
        if k == 0:
            return [
                (None, remote(src, dst, z_send.at[w, 0], recv, (dp, at(1 - side), col))),
                (middle, remote(src, dst, z_send.at[w, 1], recv, (dp, at(2), col))),
            ]
        onward = at(2) if k == 1 else at(0)
        return [(middle, remote(src, dst, z_send.at[w, k + 1], recv, (dp, onward, col)))]

    def first_copies(w, k):
        out = []
        for half, target in ((0, across), (1, along)):
            out.append(
                remote(source(w, k, half), place(w, order[k], dp, half), s1_send.at[w, k, half],
                       s1_recv.at[w, k, half], (target, row, col))
            )
        return out

    def second_copies(w, k, which):
        out = []
        for half, target, other in ((0, along, across), (1, across, along)):
            if which == 0:
                src, owner = source(w, k, half), dp
            else:
                src, owner = place(w, order[k], other, half), other
            out.append(
                remote(src, place(w, order[k], owner, half), s2_send.at[w, k, which, half],
                       s2_recv.at[w, k, which, half], (target, row, col))
            )
        return out

    def onward(w, k):
        if k > 0:
            block = place(w, order[k], dp)
            pltpu.make_async_copy(block, block, z_recv.at[w, order[k]]).wait()
        for cond, copy in line_copies(w, k):
            if cond is None:
                copy.start()
            else:
                pl.when(cond)(copy.start)

    def sideways(w, k):
        for copy in first_copies(w, k) + second_copies(w, k, 0):
            copy.start()

    def arrived(w, k):
        onward(w, k)
        sideways(w, k)

    def passed(w, k):
        for copy in first_copies(w, k):
            copy.wait_recv()
        for copy in second_copies(w, k, 1):
            copy.start()

    def finished(w):
        for k in range(ROWS):
            for which in range(2):
                for copy in second_copies(w, k, which):
                    copy.wait_recv()

    def drained(w, k):
        for cond, copy in line_copies(w, k):
            if cond is None:
                copy.wait_send()
            else:
                pl.when(cond)(copy.wait_send)
        for copy in first_copies(w, k) + second_copies(w, k, 0) + second_copies(w, k, 1):
            copy.wait_send()

    def home(w):
        return pltpu.make_async_copy(own[w], place(w, row, dp), l_sem.at[w])

    def begin(w):
        loads[w].wait()
        own[w][...] = stage[w][...].astype(BF)
        home(w).start()

    small_home = pltpu.make_async_copy(small_ref, smalls.at[me], l_sem.at[N_W])
    kept = []

    def keep(src, dst):
        copy = pltpu.make_async_copy(src, dst, l_sem.at[N_W + 1 + len(kept)])
        copy.start()
        kept.append(copy)

    def smalls_start():
        small_home.start()
        for step in range(1, ROWS * DPS):
            small_copy(step).start()

    def norm(served):
        small_home.wait()
        for step in range(1, ROWS * DPS):
            small_copy(step).wait()
        read_gains(smalls, gains)
        if aligned:
            read_bias(smalls, bias_row, 9 + n_q // (DPS * 128), n_u // DPS)
        else:
            bias_row[...] = bias_in[...]
        branch[...] = jnp.zeros(branch.shape, F32)
        comb[...] = jnp.zeros(comb.shape, F32)
        token_finish(0)
        first, first_t = hidden.at[:, pl.ds(0, D)], hidden.at[:, pl.ds(D, D)]
        norm_stage(x_ref, gains, ((0, first, first_t), (2, second, second_t)), served)
        keep(x_ref, x_out)
        keep(smalls, smalls_out)
        keep(first, first_out)
        keep(first_t, first_t_out)

    def act(word):
        kind, rest = word[0], [int(d) for d in word[1:]]
        {
            "b": begin, "z": onward, "s": sideways, "p": passed, "t": token_start, "d": token_spread, "m": smalls_start,
        }[kind](*rest)

    def forward(served):
        home(UP).wait()
        finished(UP)
        for copy in kept[2:4]:
            copy.wait()

        def block(n, carry):
            cut = span(n * width, width, width)

            def body(j, carry):
                rows = span(j * 256, 256, 256)
                value, slant = gelu_parts(nn(second[rows, :], wu[:, cut]) + bias_row[0:1, cut])
                hidden[rows, cut] = value.astype(BF)
                slope[rows, cut] = slant
                return carry

            lax.fori_loop(0, SEQ_LEN // 256, body, 0)
            served(n)
            return carry

        lax.fori_loop(0, blocks, block, 0)

    def down_grads(served):
        token_finish(1)
        keep(c_ref, c_out)
        h = gp.shape[3]

        def block(n, carry):
            turned = hidden[:, span(n * width, width, width)].T
            if blocks == DPS:
                for half in range(2):
                    gp[n // 2, lax.rem(n, 2), half] = nn(turned[half * h : (half + 1) * h, :], c_ref[...]).astype(BF)
            else:
                gp[...] = nn(turned, c_ref[...]).astype(BF).reshape(2, 2, 2, h, D)
            served(n)
            return carry

        lax.fori_loop(0, blocks, block, 0)
        keep(gp, gp_out)

    def backward(served):
        home(DOWN).wait()
        finished(DOWN)
        sum_out[...] = jnp.zeros(sum_out.shape, F32)

        def block(n, carry):
            cut = span(n * width, width, width)

            def body(j, carry):
                rows = span(j * 256, 256, 256)
                grad = (nt(c_ref[rows, :], wp[cut, :]) * slope[rows, cut]).astype(BF)
                ghp[rows, :] = grad
                branch[rows, :] += nn(hidden[rows, cut], wp[cut, :])
                comb[rows, :] += nt(grad, wu[:, cut])
                sum_out[0:1, cut] += jnp.sum(grad.astype(F32), axis=0, keepdims=True)
                return carry

            for part_of in range(2):
                lax.fori_loop(2 * part_of, 2 * part_of + 2, body, 0)
                served(n, part_of, 3)

            def up_body(r, carry):
                value = nn(second_t[span(r * 256, 256, 256), :], ghp[...]).astype(BF)
                gu[r, :, :, :, :, cut] = value.reshape(2, 2, 2, 32, width)
                return carry

            lax.fori_loop(0, ROWS, up_body, 0)
            served(n, 2, 3)
            return carry

        lax.fori_loop(0, blocks, block, 0)

    loops = {"N": (8, norm), "P": (blocks, forward), "D": (blocks, down_grads), "B": (3 * blocks, backward)}
    plan = GATHER_PLAN
    if blocks != DPS:
        plan = [word for word in plan if word[0] not in loops]
        for kind in "NPDB":
            plan = plan + parts_of(kind, loops[kind][0])
    run(plan, loops, act)
    for src, dst in ((gu, gu_out), (branch, branch_out), (comb, comb_out)):
        keep(src, dst)
    for w in (QKV, DENSE):
        home(w).wait()
        finished(w)
    for w in range(N_W):
        for k in range(ROWS):
            drained(w, k)
    for kind in range(2):
        token_drain(kind)
    for copy in kept[:2] + kept[4:]:
        copy.wait()


def gather(tokens_in, cotangent, small, bias, weights, cols, aligned):
    wq, wu, wd, wp = weights
    n_q, n_u = wq.shape[1], wu.shape[1]
    att_width, h_p = wd.shape[0] * DPS, wp.shape[0]
    width = 512 if n_u == DPS * 512 else n_u
    any_spec = pl.BlockSpec(memory_space=pl.ANY)
    vmem = pl.BlockSpec(memory_space=pltpu.VMEM)
    shape = jax.ShapeDtypeStruct
    smalls = (ROWS * DPS,) + small.shape
    square = (SEQ_LEN, D)
    up_shape, down_shape = (ROWS, 2, 2, 2, 32, n_u), (2, 2, 2, h_p // 2, D)
    out_shape = [
        shape(square, BF), shape(square, BF), shape(smalls, F32), shape((D, n_q), BF), shape((att_width, D), BF),
        shape(square, BF), shape(square, BF), shape(up_shape, BF), shape(down_shape, BF), shape(square, F32),
        shape(square, F32), shape((1, n_u), F32),
    ]
    tok_col = tokens_in.shape[0]
    pieces = tok_col // (SEQ_LEN // cols)
    dma = pltpu.SemaphoreType.DMA
    buf = pltpu.VMEM
    scratch = [buf(w.shape, BF) for w in weights] + [buf(w.shape, F32) for w in weights]
    scratch += [
        buf(square, BF), buf(square, BF), buf(smalls, F32), buf((D, n_u), BF), buf((n_u, D), BF),
        buf((8, D), F32), buf((1, n_u), F32), buf(square, BF), buf(square, BF),
        buf((SEQ_LEN, max(n_u, 2 * D)), BF), buf((SEQ_LEN, n_u), F32), buf((SEQ_LEN, width), BF), buf(up_shape, BF), buf(down_shape, BF), buf(square, F32),
        buf(square, F32),
        dma((N_W, 5)), dma((N_W, 4)), dma((N_W, 4, 2)), dma((N_W, 4, 2)), dma((N_W, 4, 2, 2)), dma((N_W, 4, 2, 2)),
        dma((2, pieces)), dma((2, 4)), dma((2, cols - 1)), dma((2, cols - 1)),
        dma((ROWS * DPS - 1,)), dma((ROWS * DPS - 1,)), dma((N_W + 10,)),
    ]
    return pl.pallas_call(
        functools.partial(gather_kernel, cols, aligned),
        out_shape=out_shape,
        in_specs=[any_spec] * 3 + [vmem] + [any_spec] * 4,
        out_specs=[any_spec] * 11 + [vmem],
        scratch_shapes=scratch,
        compiler_params=pltpu.CompilerParams(collective_id=0, has_side_effects=True, vmem_limit_bytes=60 << 20),
    )(tokens_in, cotangent, small, bias, wq, wu, wd, wp)


SCATTER_PLAN = (
    "f0", "f1", "J0", "J1", "J2", "f2", "J3", "U", "H0", "H1", "H2", "H3", "H4", "H5", "g0", "H6", "H7", "H8",
    "H9", "H10", "g1", "f3", "H11", "H12", "H13", "H14", "H15", "h0", "H16", "H17", "g2", "h1", "H18", "H19", "f4",
    "H20", "g3", "H21", "q0", "H22", "H23", "H24", "h2", "H25", "H26", "H27", "g4", "H28", "f5", "q1", "r0", "H29",
    "h3", "H30", "H31", "h4", "q2", "T", "f6", "q3", "W0", "q4", "X", "f7", "G0", "G1", "G2", "g5", "W1", "G3",
    "f8", "h5", "g6", "g7", "r1", "h6", "f9", "W2", "u0", "q5", "u1", "g8", "r2", "h7", "Y", "W3", "h8", "g9",
    "q6", "f10", "r3", "u2", "f11", "v0", "h9", "r4", "g10", "q7", "u3", "q8", "v1", "h10", "r5", "g11", "v2",
    "h11", "q9", "r6", "u4", "q10", "u5", "r7", "r8", "v3", "r9", "q11", "v4", "r10", "u6", "u7", "u8", "u9",
    "u10", "r11", "u11",
)
PIECES = 12


def add_into(dst, src):
    shape = dst.shape
    outer, height = shape[:-2], shape[-2]
    step = min(32, height)
    per = height // step
    total = math.prod(outer) * per

    def body(i, carry):
        index, rest = [], i // per
        for size in reversed(outer):
            index.append(lax.rem(rest, size))
            rest = rest // size
        where = tuple(reversed(index)) + (span(lax.rem(i, per) * step, step, step),)
        dst[where] = (dst[where].astype(F32) + src[where].astype(F32)).astype(BF)
        return carry

    lax.fori_loop(0, total, body, 0)


def pieces_of(n_q, n_u, h_d, h_p):
    out = []

    def columns(w, n):
        size = 512 if n % 512 == 0 else n
        out.extend((w, start, size) for start in range(0, n, size))

    columns(UP, n_u)
    half = h_p // 2
    size = 64 if half % 64 == 0 else half
    out.extend((DOWN, start, size) for start in range(0, half, size))
    out.append((DENSE, 0, h_d // 2))
    columns(QKV, n_q)
    return out


def scatter_kernel(cols, aligned, pieces, *refs):
    n_p = len(pieces)
    (prefix_ref, smalls, angles, bias_in, sum_u, x_in, c_in, wq_in, wd_in, first_in, first_t_in, gu_in, gp_in, branch_in,
     comb_in) = refs[:15]
    (lo_out, gt_out, oq, ou, od, op, sm_out) = refs[15:22]
    (wq, wd, x_ref, c_ref, first, first_t, q_t, k_t, v_t, up_t, att_t, gm_t, grad_q, grad_k, grad_v) = refs[22:37]
    (gq, gd, att, branch, comb, branch_got, comb_got, gains, bias_row, out_bias, sm, sm_got, gain_sum) = refs[37:50]
    mine_u, mine_p = refs[50:52], refs[52:54]
    base = 54

    def buffers(start):
        return [refs[start + 2 * i : start + 2 * i + 2] for i in range(n_p)]

    got1, got2, got_end, got_mid = [buffers(base + 2 * n_p * n) for n in range(4)]
    (l_sem, f_sem, s1_send, s1_recv, s2_send, s2_recv, e_send, e_recv, m_send, m_recv, b_send, b_recv, d_send, d_recv,
     t_send, t_recv, v_send, v_recv) = refs[base + 8 * n_p :]
    dp, row, col, across, along = places()
    x, y = lax.rem(dp, 2), dp // 2
    side, at = line_order(row)
    far_end = row // 2
    middle, end = side == 1, side == 0
    n_q, n_u = wq_in.shape[1], sum_u.shape[1]
    heads = q_t.shape[0]
    tok_col = lo_out.shape[0]
    part = SEQ_LEN // cols

    def load(src, dst, n):
        return pltpu.make_async_copy(src, dst, l_sem.at[n])

    loads = [load(first_in, first, 0), load(wq_in, wq, 1), load(wd_in, wd, 2), load(c_in, c_ref, 3), load(first_t_in, first_t, 4),
             load(branch_in, branch, 5), load(comb_in, comb, 6), load(x_in, x_ref, 7)]
    for one in loads:
        one.start()
    group = [(dp, lax.rem(row + step, ROWS), lax.rem(col + other, cols)) for step in range(ROWS) for other in range(cols)]
    greet([(across, row, col), (along, row, col)] + group[1:])

    def view(i, half, other):
        w, start, size = pieces[i]
        if half == 0:
            place_y, place_x = (1 - y if other else y), slice(None)
        else:
            place_y, place_x = slice(None), (1 - x if other else x)
        cut = pl.ds(start, size)
        if w in (QKV, UP):
            if w == UP and not other:
                return mine_u[half].at[:, :, :, cut]
            return (gu_in if w == UP else gq).at[:, place_y, place_x, half, :, cut]
        if w == DOWN and not other:
            return mine_p[half].at[:, cut, :]
        return (gp_in if w == DOWN else gd).at[place_y, place_x, half, cut, :]

    def fetch(i, half):
        w, start, size = pieces[i]
        place_y, place_x = (y, slice(None)) if half == 0 else (slice(None), x)
        cut = pl.ds(start, size)
        src = gu_in.at[:, place_y, place_x, half, :, cut] if w == UP else gp_in.at[place_y, place_x, half, cut, :]
        return pltpu.make_async_copy(src, view(i, half, False), f_sem.at[i, half])

    def first_copy(i, half):
        target = along if half == 0 else across
        return remote(view(i, half, True), got1[i][half], s1_send.at[i, half], s1_recv.at[i, half], (target, row, col))

    def keep(i, half, other):
        which = x if half == 0 else y
        which = 1 - which if other else which
        kept = view(i, half, False)
        return kept.at[:, which] if pieces[i][0] in (QKV, UP) else kept.at[which]

    def second_copy(i, half):
        target = across if half == 0 else along
        return remote(keep(i, half, True), got2[i][half], s2_send.at[i, half], s2_recv.at[i, half], (target, row, col))

    def lines(i, ref, start, count):
        if pieces[i][0] in (QKV, UP):
            return ref.at[pl.ds(start, count)]
        return ref.at[:, span(start * 256, count * 256, 256)]

    def end_copy(i, half):
        src = lines(i, keep(i, half, False), 1 - far_end, 3)
        return remote(src, got_end[i][half], e_send.at[i, half], e_recv.at[i, half], (dp, at(1), col))

    def mid_copy(i, half):
        src = lines(i, keep(i, half, False), 2 * (1 - far_end), 2)
        return remote(src, got_mid[i][half], m_send.at[i, half], m_recv.at[i, half], (dp, at(2), col))

    def back_copy(i, half):
        src = lines(i, keep(i, half, False), at(0), 1)
        return remote(src, lines(i, got_mid[i][half], 0, 1), b_send.at[i, half], b_recv.at[i, half], (dp, at(0), col))

    def begin(i):
        for half in range(2):
            first_copy(i, half).start()
            if pieces[i][0] in (UP, DOWN):
                fetch(i, half).start()

    def stage_two(i):
        for half in range(2):
            if pieces[i][0] in (UP, DOWN):
                fetch(i, half).wait()
            first_copy(i, half).wait_recv()
            add_into(view(i, half, False), got1[i][half])
            second_copy(i, half).start()

    def stage_three(i):
        for half in range(2):
            second_copy(i, half).wait_recv()
            add_into(keep(i, half, False), got2[i][half])

            @pl.when(end)
            def _():
                end_copy(i, half).start()

    def stage_four(i):
        @pl.when(middle)
        def _():
            for half in range(2):
                end_copy(i, half).wait_recv()
                add_into(lines(i, keep(i, half, False), 2 * (1 - far_end), 2), lines(i, got_end[i][half], 1 - far_end, 2))
                mid_copy(i, half).start()

    def stage_five(i):
        @pl.when(middle)
        def _():
            for half in range(2):
                mid_copy(i, half).wait_recv()
                add_into(lines(i, keep(i, half, False), at(0), 1), lines(i, got_mid[i][half], far_end, 1))
                back_copy(i, half).start()

    def stage_six(i):
        w, start, size = pieces[i]
        out = (oq, ou, od, op)[w]
        for half in range(2):
            mine = lines(i, keep(i, half, False), row, 1)

            def total(others):
                if w in (QKV, UP):
                    value = mine[0].astype(F32)
                    for other in others:
                        value = value + other[0].astype(F32)
                    out[half, :, pl.ds(start, size)] = value
                else:
                    value = mine[...].astype(F32)
                    for other in others:
                        value = value + other[...].astype(F32)
                    out[half, pl.ds(start, size), :] = value

            @pl.when(end)
            def _():
                back_copy(i, half).wait_recv()
                total([lines(i, got_mid[i][half], 0, 1)])

            @pl.when(middle)
            def _():
                total([lines(i, got_end[i][half], 2 * far_end, 1), lines(i, got_mid[i][half], 1 - far_end, 1)])

    def drain(i):
        for half in range(2):
            first_copy(i, half).wait_send()
            second_copy(i, half).wait_send()

            @pl.when(end)
            def _():
                end_copy(i, half).wait_send()

            @pl.when(middle)
            def _():
                mid_copy(i, half).wait_send()
                back_copy(i, half).wait_send()

    def part_rows(piece):
        return span(piece * part, part, part)

    def col_copy(kind, n):
        other = lax.rem(col + n, cols)
        src = (branch, comb)[kind].at[part_rows(other), :]
        dst = (branch_got, comb_got)[kind].at[n - 1]
        return remote(src, dst, d_send.at[kind, n - 1], d_recv.at[kind, n - 1], (dp, row, other))

    start = row * SEQ_LEN + col * part
    owner, offset = start // tok_col, lax.rem(start, tok_col)

    def out_copy(kind, r):
        src = first.at[pl.ds(kind * part, part), span(r * 256, 256, 256)]
        dst = (lo_out, gt_out)[kind].at[span(offset, part, part), :]
        recv = t_recv.at[kind, offset // part]
        here = jnp.logical_and(row == r, owner == col)
        far = remote(src, dst, t_send.at[kind, r], recv, (dp, r, owner))
        return here, far, pltpu.make_async_copy(src, dst, recv)

    def out_start(kind):
        for r in (at(1 - side), at(2), at(3), row):
            here, far, near = out_copy(kind, r)
            pl.when(jnp.logical_not(here))(far.start)
            pl.when(here)(near.start)

    def out_finish(kind):
        for r in range(ROWS):
            here, far, near = out_copy(kind, r)
            pl.when(jnp.logical_not(here))(far.wait_send)
        out = (lo_out, gt_out)[kind]
        for n in range(tok_col // part):
            block = out.at[pl.ds(n * part, part), :]
            pltpu.make_async_copy(block, block, t_recv.at[kind, n]).wait()

    height = min(128, part)

    def finish_rows(kind):
        for n in range(1, cols):
            col_copy(kind, n).wait_recv()

        def body(i, carry):
            here = span(i * height, height, height)
            rows = span(col * part + i * height, height, height)
            value = (branch, comb)[kind][rows, :]
            for n in range(1, cols):
                value = value + (branch_got, comb_got)[kind][n - 1, here, :]
            wide = x_ref[rows, :].astype(F32)
            if kind == 0:
                value = wide + value + out_bias[0:1, :]
            else:
                normed, scale_inv = norm_rows(wide)
                mean = jnp.mean(value, axis=1, keepdims=True)
                cross = jnp.mean(value * normed, axis=1, keepdims=True)
                value = c_ref[rows, :].astype(F32) + scale_inv * (value - mean - normed * cross)
            first[span(kind * part + i * height, height, height), :] = value.astype(BF)
            return carry

        lax.fori_loop(0, part // height, body, 0)

    def small_copy(n):
        if n < 2:
            return remote(sm.at[n], sm_got.at[n], v_send.at[n], v_recv.at[n], ((across, along)[n], row, col))
        if n < 5:
            target = (dp, lax.rem(row + n - 1, ROWS), col)
            return remote(sm.at[2], sm_got.at[n], v_send.at[n], v_recv.at[n], target)
        target = (dp, row, lax.rem(col + n - 4, cols))
        return remote(sm.at[3], sm_got.at[n], v_send.at[n], v_recv.at[n], target)

    def small_step(n):
        if n > 0:
            waits = ((0,), (1,), (2, 3, 4), tuple(range(5, 4 + cols)))[n - 1]
            for m in waits:
                small_copy(m).wait_recv()
            value = sm[n - 1]
            if n < 4:
                for m in waits:
                    value = value + sm_got[m]
                sm[n] = value
            else:
                sm_out[...] = value
                value = value[0:4]
                for m in waits:
                    value = value + sm_got[m, 0:4, :]
                sm_out[0:4, :] = value
        for m in ((0,), (1,), (2, 3, 4), tuple(range(5, 4 + cols)), ())[n]:
            small_copy(m).start()

    def project(served):
        read_gains(smalls, gains)
        lanes = lax.broadcasted_iota(jnp.int32, (1, 128), 1)
        for r in range(ROWS):
            for d in range(0, DPS, 2):
                both = [rounded(smalls[r * DPS + d + n, 8:9, :]) for n in range(2)]
                both = [value + pltpu.roll(value, 64, 1) for value in both]
                out_bias[0:1, pl.ds(r * 256 + d * 64, 128)] = jnp.where(lanes < 64, both[0], both[1])
        if aligned:
            read_bias(smalls, bias_row, 9, n_q // DPS)
        else:
            bias_row[...] = bias_in[...]
        sm[0] = jnp.zeros(sm.shape[1:], F32)
        sm[0, 6:7, 0:n_u] = sum_u[...]
        loads[0].wait()
        loads[1].wait()
        project_stage(wq, first, bias_row, angles, q_t, k_t, v_t, heads, served)

    def upstream():
        loads[2].wait()
        loads[3].wait()
        upstream_stage(wd, c_ref, up_t, heads)

    def attended():
        group_h = min(heads, 4)

        def turn_body(i, carry):
            block = att_t[pl.ds(i * group_h, group_h)].reshape(group_h * HD, SEQ_LEN)
            spot = pl.ds(0, group_h * HD) if heads == group_h else span(i * group_h * HD, group_h * HD, 128)
            att[:, spot] = block.T
            return carry

        lax.fori_loop(0, heads // group_h, turn_body, 0)
        loads[5].wait()

        def out_body(j, carry):
            rows = span(j * 256, 256, 256)
            branch[rows, :] += nn(att[rows, :], wd[...])
            return carry

        lax.fori_loop(0, SEQ_LEN // 256, out_body, 0)
        for n in range(1, cols):
            col_copy(0, n).start()

    def weight_grads(n):
        if n == 0:
            all_heads = att_t[...].reshape(heads * HD, SEQ_LEN)
            gd[...] = nn(all_heads, c_ref[...]).astype(BF).reshape(gd.shape)
            return
        if n == 1:
            loads[4].wait()
        wide = min(512, n_q)
        cut = pl.ds((n - 1) * wide, wide)

        def qkv_body(r, carry):
            rows = span(r * 256, 256, 256)
            gq[r, :, :, :, :, cut] = nt(first_t[rows, :], gm_t[cut, :]).astype(BF).reshape(2, 2, 2, 32, wide)
            return carry

        lax.fori_loop(0, ROWS, qkv_body, 0)

    need_x = [loads[7]]

    def output_home():
        if len(need_x):
            need_x.pop().wait()
        finish_rows(0)
        out_start(0)

    def features(served):
        loads[6].wait()
        if len(need_x):
            need_x.pop().wait()
        for n in range(8):
            gain_sum[n : n + 1, :] = jnp.zeros((1, D), F32)

        def body(j, carry):
            rows = span(j * 256, 256, 256)
            grad = gm_t[:, rows].T
            grad_first = nt(grad, wq[...])
            grad_second = comb[rows, :]
            normed, ignored = norm_rows(x_ref[rows, :].astype(F32))
            for n, value in enumerate((normed * grad_first, grad_first, normed * grad_second, grad_second,
                                       c_ref[rows, :].astype(F32))):
                gain_sum[n : n + 1, :] += jnp.sum(value, axis=0, keepdims=True)
            sm[0, 5:6, 0:n_q] += jnp.sum(grad.astype(F32), axis=0, keepdims=True)
            comb[rows, :] = gains[0:1, :] * grad_first + gains[2:3, :] * grad_second
            served(j)
            return carry

        lax.fori_loop(0, SEQ_LEN // 256, body, 0)
        for n in range(1, cols):
            col_copy(1, n).start()
        sm[0, 0:5, 0:D] = gain_sum[0:5, :]

    def gradient_home():
        finish_rows(1)
        out_start(1)

    stages = {"f": begin, "g": stage_two, "h": stage_three, "q": stage_four, "r": stage_five, "u": stage_six}
    others = {"U": upstream, "T": attended, "X": output_home, "Y": gradient_home}

    def act(word):
        kind, rest = word[0], word[1:]
        if kind in others:
            others[kind]()
        elif kind == "W":
            weight_grads(int(rest))
        elif kind == "v":
            small_step(int(rest))
        else:
            stages[kind](int(rest))

    def attention(served):
        prefix = prefix_ref[0]

        def head_body(h, carry):
            attend_head(h, prefix, angles, q_t, k_t, v_t, up_t, att_t, gm_t, grad_q, grad_k, grad_v, served)
            return carry

        lax.fori_loop(0, heads, head_body, 0)

    loops = {
        "J": (heads // min(heads, 2), project), "H": (heads * (SEQ_LEN // 256), attention), "G": (SEQ_LEN // 256, features),
    }
    plan = SCATTER_PLAN
    if n_p != PIECES:
        late = [i for i in range(n_p) if pieces[i][0] in (QKV, DENSE)]
        plan = ["f%d" % i for i in range(n_p) if i not in late] + parts_of("J", loops["J"][0]) + ["U"]
        plan = plan + parts_of("H", loops["H"][0]) + ["T", "W0", "W1", "X"] + parts_of("G", loops["G"][0]) + ["Y"]
        plan = plan + ["f%d" % i for i in late] + [s + str(i) for s in "ghqru" for i in range(n_p)] + parts_of("v", 5)
    run(plan, loops, act)
    for i in range(n_p):
        drain(i)
    for kind in range(2):
        out_finish(kind)
    for n in range(1, cols):
        for kind in range(2):
            col_copy(kind, n).wait_send()
    for n in range(4 + cols):
        small_copy(n).wait_send()


def scatter(prefix_len, smalls, angles, bias, sum_u, own_x, own_cot, wq, wd, first, first_t, gu, gp, branch, comb, cols, aligned,
            tok_col):
    any_spec = pl.BlockSpec(memory_space=pl.ANY)
    vmem = pl.BlockSpec(memory_space=pltpu.VMEM)
    smem = pl.BlockSpec(memory_space=pltpu.SMEM)
    dma = pltpu.SemaphoreType.DMA
    buf = pltpu.VMEM
    shape = jax.ShapeDtypeStruct
    n_q, n_u = wq.shape[1], sum_u.shape[1]
    heads = n_q // 192
    h_d, h_p = wd.shape[0] // DPS, 2 * gp.shape[3]
    pieces = pieces_of(n_q, n_u, h_d, h_p)
    n_p = len(pieces)
    part = SEQ_LEN // cols
    line = max(n_q, n_u, D)
    square = (SEQ_LEN, D)
    turned = buf((heads, HD, SEQ_LEN), BF)
    scratch = [
        buf((D, n_q), BF), buf(wd.shape, BF), buf(square, BF), buf(square, BF), buf(square, BF), buf(square, BF),
        turned, turned, turned, turned, turned, buf((n_q, SEQ_LEN), BF),
        buf((HD, SEQ_LEN), F32), buf((HD, SEQ_LEN), F32), buf((HD, SEQ_LEN), F32),
        buf((ROWS, 2, 2, 2, 32, n_q), BF), buf((2, 2, 2, h_d // 2, D), BF), buf((SEQ_LEN, heads * HD), BF), buf(square, F32), buf(square, F32),
        buf((cols - 1, part, D), F32), buf((cols - 1, part, D), F32),
        buf((8, D), F32), buf((1, n_q), F32), buf((1, D), F32), buf((4, 8, line), F32), buf((4 + cols, 8, line), F32),
        buf((8, D), F32),
    ]
    scratch += [buf((ROWS, 2, 32, n_u), BF)] * 2 + [buf((2, h_p // 2, D), BF)] * 2
    for lead, count in (((ROWS, 2), None), ((ROWS,), None), ((3,), 3), ((2,), 2)):
        for w, start, size in pieces:
            if w in (QKV, UP):
                one = lead + (32, size)
            elif count is None:
                one = ((2,) if len(lead) == 2 else ()) + (size, D)
            else:
                one = (size, 256 * count)
            scratch += [buf(one, BF)] * 2
    scratch += [
        dma((8,)), dma((n_p, 2)), dma((n_p, 2)), dma((n_p, 2)), dma((n_p, 2)), dma((n_p, 2)), dma((n_p, 2)), dma((n_p, 2)),
        dma((n_p, 2)), dma((n_p, 2)), dma((n_p, 2)), dma((n_p, 2)), dma((2, cols - 1)), dma((2, cols - 1)),
        dma((2, ROWS)), dma((2, tok_col // part)), dma((4 + cols,)), dma((4 + cols,)),
    ]
    return pl.pallas_call(
        functools.partial(scatter_kernel, cols, aligned, pieces),
        out_shape=[
            shape((tok_col, 256), BF), shape((tok_col, 256), BF), shape((2, 32, n_q), F32), shape((2, 32, n_u), F32),
            shape((2, h_d // 2, 256), F32), shape((2, h_p // 2, 256), F32), shape((8, line), F32),
        ],
        in_specs=[smem, vmem, vmem, vmem, vmem] + [any_spec] * 10,
        out_specs=[any_spec] * 2 + [vmem] * 5,
        scratch_shapes=scratch,
        compiler_params=pltpu.CompilerParams(collective_id=1, has_side_effects=True, vmem_limit_bytes=63 << 20),
    )(prefix_len, smalls, angles, bias, sum_u, own_x, own_cot, wq, wd, first, first_t, gu, gp, branch, comb)


def finish_kernel(*refs):
    whole_in, sums, whole_out, q_b, u_b, d_b, p_b, gains, rooms, sem = (
        refs[:6], refs[6], refs[7:13], *refs[13:17], refs[17:21], refs[21:27], refs[27]
    )
    arrive = [pltpu.make_async_copy(src, dst, sem.at[0, n]) for n, (src, dst) in enumerate(zip(whole_in, rooms))]
    leave = [pltpu.make_async_copy(src, dst, sem.at[1, n]) for n, (src, dst) in enumerate(zip(rooms, whole_out))]
    for copy in arrive:
        copy.start()
    dp, row = lax.axis_index("dp"), lax.axis_index("row")
    for n, gain in enumerate(gains):
        gain[...] = sums[n : n + 1, span(row * 256, 256, 256)].reshape(gain.shape)
    for n, bias in ((5, q_b), (6, u_b)):
        size = bias.shape[0]
        bias[...] = sums[n : n + 1, span(dp * size, size, 128)].reshape(bias.shape)
    me = row * DPS + dp
    pair = sums[4:5, span((me // 2) * 128, 128, 128)]
    pair = jnp.where(lax.rem(me, 2) == 0, pair, pltpu.roll(pair, 64, 1))
    for bias in (d_b, p_b):
        bias[...] = pair[:, 0:64].reshape(bias.shape)
    for first, then in zip(arrive, leave):
        first.wait()
        then.start()
    for copy in leave:
        copy.wait()


def finish(whole, sums, n_qb, n_ub):
    any_spec = pl.BlockSpec(memory_space=pl.ANY)
    vmem = pl.BlockSpec(memory_space=pltpu.VMEM)
    shape = jax.ShapeDtypeStruct
    sizes = [n_qb, n_ub, 64, 64] + [256] * 4
    out = pl.pallas_call(
        finish_kernel,
        out_shape=[shape(a.shape, a.dtype) for a in whole] + [shape((size,), F32) for size in sizes],
        in_specs=[any_spec] * 6 + [vmem],
        out_specs=[any_spec] * 6 + [vmem] * 8,
        scratch_shapes=[pltpu.VMEM(a.shape, a.dtype) for a in whole] + [pltpu.SemaphoreType.DMA((2, 6))],
    )(*whole, sums)
    lo, gt, gq, gu, gd, gp, q_b, u_b, d_b, p_b, *gains = out
    return (lo, gt, gq, q_b, gu, u_b, gd, d_b, gp, p_b, *gains)


def angles_table():
    half_rot = ROT // 2
    rates = np.exp(np.arange(half_rot, dtype=np.float32) * np.float32(-2.0 * math.log(10000.0) / ROT))
    turned = rates.astype(np.float32)[:, None] * np.arange(SEQ_LEN, dtype=np.float32)[None, :]
    return np.concatenate([np.cos(turned), np.sin(turned)], axis=0).astype(np.float32)


def shards(cols, tokens_in, prefix_len, first_gain, first_shift, second_gain, second_shift, qkv_weight, qkv_bias,
           up_weight, up_bias, dense_weight, dense_bias, down_weight, down_bias, cotangent):
    tok_col = tokens_in.shape[0]
    n_q, n_u = qkv_weight.shape[1], up_weight.shape[1]

    n_qb, n_ub = qkv_bias.shape[0], up_bias.shape[0]
    aligned = n_qb % 128 == 0 and n_ub % 128 == 0
    small = jnp.concatenate((first_gain, first_shift, second_gain, second_shift, dense_bias, down_bias, qkv_bias, up_bias))
    size = -(-small.shape[0] // 1024) * 1024
    small = jnp.pad(small, (0, size - small.shape[0])).reshape(size // 128, 128)
    if aligned:
        q_bias = u_bias = small
    else:
        q_bias = lax.all_gather(rounded(qkv_bias), "dp", axis=0, tiled=True).reshape(1, n_q)
        u_bias = lax.all_gather(rounded(up_bias), "dp", axis=0, tiled=True).reshape(1, n_u)
    own_x, own_cot, smalls, wq, wd, first, first_t, gu, gp, branch, comb, sum_u = gather(
        tokens_in, cotangent, small, u_bias, (qkv_weight, up_weight, dense_weight, down_weight), cols, aligned
    )
    layer_out, grad_tokens, out_q, out_u, out_d, out_p, sums = scatter(
        prefix_len, smalls, jnp.asarray(angles_table()), q_bias, sum_u, own_x, own_cot, wq, wd, first, first_t, gu, gp, branch,
        comb, cols, aligned, tok_col
    )
    h_d, h_p = dense_weight.shape[0], down_weight.shape[0]
    whole = (
        layer_out, grad_tokens, out_q.reshape(64, n_q), out_u.reshape(64, n_u), out_d.reshape(h_d, 256), out_p.reshape(h_p, 256)
    )
    if aligned:
        return finish(whole, sums, n_qb, n_ub)
    dp, row = lax.axis_index("dp"), lax.axis_index("row")
    gain_sums = lax.dynamic_slice(sums, (0, row * 256), (4, 256))
    out_b = lax.dynamic_slice(sums, (4, (row * DPS + dp) * 64), (1, 64))[0]
    q_b = lax.dynamic_slice(sums, (5, dp * n_qb), (1, n_qb))[0]
    u_b = lax.dynamic_slice(sums, (6, dp * n_ub), (1, n_ub))[0]
    return (
        whole[0], whole[1], whole[2], q_b, whole[3], u_b, whole[4], out_b, whole[5], out_b,
        gain_sums[0], gain_sums[1], gain_sums[2], gain_sums[3],
    )


def solution(mesh):
    in_specs = (
        P(("dp", "col"), "row"), P(("dp", "row")), P("row"), P("row"), P("row"), P("row"),
        P(("row", "dp"), "col"), P(("col", "dp")), P(("row", "dp"), "col"), P(("col", "dp")),
        P(("col", "dp"), "row"), P(("row", "dp")), P(("col", "dp"), "row"), P(("row", "dp")),
        P(("dp", "col"), "row"),
    )
    out_specs = (
        P(("dp", "col"), "row"), P(("dp", "col"), "row"), P(("row", "dp"), "col"), P(("col", "dp")),
        P(("row", "dp"), "col"), P(("col", "dp")), P(("col", "dp"), "row"), P(("row", "dp")),
        P(("col", "dp"), "row"), P(("row", "dp")), P("row"), P("row"), P("row"), P("row"),
    )
    body = functools.partial(shards, mesh.shape["col"])
    return jax.shard_map(body, mesh=mesh, in_specs=in_specs, out_specs=out_specs, check_vma=False)
```

```python
import functools
import math

import jax
import jax.numpy as jnp
import numpy as np
from jax import lax
from jax.experimental import pallas as pl
from jax.experimental.pallas import tpu as pltpu
from jax.sharding import PartitionSpec as P

D = 1024
HD = 64
ROT = 16
FF = 4096
SEQ_LEN = 1024
EPS = 1e-05
NEGATIVE = -1e30
ROWS = 4
DPS = 4
MESH = pl.DeviceIdType.MESH
BF = jnp.bfloat16
F32 = jnp.float32


def places():
    dp, row, col = lax.axis_index("dp"), lax.axis_index("row"), lax.axis_index("col")
    across = dp + 1 - 2 * lax.rem(dp, 2)
    along = lax.rem(dp + 2, 4)
    return dp, row, col, across, along


def line_order(row):
    far = row // 2
    side = row + far * (3 - 2 * row)
    at = lambda place: far * 3 + (1 - 2 * far) * place
    return side, at


def greet(targets):
    barrier = pltpu.get_barrier_semaphore()
    for target in targets:
        pl.semaphore_signal(barrier, inc=1, device_id=target, device_id_type=MESH)
    pl.semaphore_wait(barrier, len(targets))


def peers_of(dp, row, col, cols):
    group = []
    for step in range(1, ROWS * cols):
        flat = lax.rem(row * cols + col + step, ROWS * cols)
        group.append((dp, flat // cols, lax.rem(flat, cols)))
    for step in range(1, DPS):
        for other in range(ROWS):
            group.append((lax.rem(dp + step, DPS), lax.rem(row + other, ROWS), col))
    return group


def remote(src, dst, send, recv, target):
    return pltpu.make_async_remote_copy(
        src_ref=src, dst_ref=dst, send_sem=send, recv_sem=recv, device_id=target, device_id_type=MESH
    )


N_W = 4
QKV, UP, DENSE, DOWN = range(N_W)
GATHER_PLAN = (
    "b1", "z10", "b3", "s30", "b2", "z30", "s10", "z11", "z12", "s11", "m", "z31", "z20", "s12", "p11", "z13",
    "p30", "s13", "t0", "s20", "z32", "p10", "b0", "p13", "t1", "s32", "d0", "s31", "N0", "p12", "N1", "N2", "N3",
    "N4", "s00", "z33", "s33", "N5", "N6", "z00", "N7", "p32", "P0", "P1", "z21", "p31", "P2", "P3", "d1", "p33",
    "s21", "z01", "s01", "D0", "D1", "D2", "D3", "z22", "s22", "z02", "B0", "B1", "s02", "p21", "B2", "B3", "B4",
    "z23", "p02", "z03", "B5", "p00", "p20", "s03", "B6", "B7", "s23", "p22", "B8", "p03", "B9", "B10", "B11",
    "p23", "p01",
)


def run(words, loops, act):
    i = 0
    while i < len(words):
        kind = words[i][0]
        if kind not in loops:
            act(words[i])
            i += 1
            continue
        count, body = loops[kind]
        groups = [[]]
        i += 1
        while len(groups) < count:
            if words[i][0] == kind:
                groups.append([])
            else:
                groups[-1].append(words[i])
            i += 1

        def served(index, first=0, stride=1):
            for n, group in enumerate(groups[first::stride]):
                if group:

                    @pl.when(index == n)
                    def _():
                        for word in group:
                            act(word)

        body(served)


def parts_of(kind, count):
    return ["%s%d" % (kind, n) for n in range(count)]


def nt(left, right):
    return lax.dot_general(left, right, (((1,), (1,)), ((), ())), preferred_element_type=F32)


def nn(left, right):
    return jnp.dot(left, right, preferred_element_type=F32)


def span(start, size, unit):
    return pl.ds(pl.multiple_of(start, unit), size)


def slot(w, ref, row, dp, height, half=None):
    if w in (QKV, UP):
        if half is None:
            return ref.at[span((row * DPS + dp) * height, height, 64), :]
        return ref.at[span((row * DPS + dp) * height + half * (height // 2), height // 2, 32), :]
    if half is None:
        return ref.at[span(dp * height, height, 16), span(row * 256, 256, 256)]
    if w == DENSE:
        return ref.at[span(dp * height, height, 16), span(row * 256 + half * 128, 128, 128)]
    return ref.at[span(dp * height + half * (height // 2), height // 2, 16), span(row * 256, 256, 256)]


def half_of(w, ref, half):
    height = ref.shape[0]
    if w == DENSE:
        return ref.at[:, pl.ds(half * 128, 128)]
    return ref.at[pl.ds(half * (height // 2), height // 2), :]


def read_gains(smalls, gains):
    for r in range(ROWS):
        for g in range(4):
            for t in range(2):
                gains[g : g + 1, pl.ds(r * 256 + t * 128, 128)] = smalls[r * DPS, pl.ds(2 * g + t, 1), :]


def rounded(value):
    return value.astype(BF).astype(F32)


def read_bias(smalls, bias, first_row, size):
    per = size // 128
    for d in range(DPS):
        for t in range(per):
            bias[0:1, pl.ds(d * size + t * 128, 128)] = rounded(smalls[d, pl.ds(first_row + t, 1), :])


def norm_rows(x):
    center = jnp.mean(x, axis=1, keepdims=True)
    spread = jnp.mean(x * x, axis=1, keepdims=True) - center * center
    scale_inv = lax.rsqrt(spread + EPS)
    return (x - center) * scale_inv, scale_inv


def norm_stage(x_ref, gains, outs, served):
    def body(i, carry):
        rows = span(i * 128, 128, 128)
        normed, ignored = norm_rows(x_ref[rows, :].astype(F32))
        for which, plain, turned in outs:
            value = (normed * gains[which : which + 1, :] + gains[which + 1 : which + 2, :]).astype(BF)
            plain[rows, :] = value
            turned[:, rows] = value.T
        served(i)
        return carry

    lax.fori_loop(0, SEQ_LEN // 128, body, 0)


def project_stage(wq, first, bias_row, angles, q_t, k_t, v_t, heads, served):
    pair = min(heads, 2)
    width = 192 * pair

    def body(p, carry):
        cols = pl.ds(0, width) if heads == pair else span(p * width, width, 128)
        w_t = wq[:, cols].T
        bias = jnp.broadcast_to(bias_row[0:1, cols], (8, width)).T[:, 0:1]
        for j in range(SEQ_LEN // 256):
            toks = pl.ds(j * 256, 256)
            mixed = nt(w_t, first[toks, :]) + bias
            cos, sin = angles[0:8, toks], angles[8:16, toks]

            def turn(base):
                x1, x2 = mixed[base : base + 8], mixed[base + 8 : base + 16]
                return jnp.concatenate([x1 * cos - x2 * sin, x2 * cos + x1 * sin, mixed[base + 16 : base + 64]], axis=0)

            for e in range(pair):
                base, h = 192 * e, pair * p + e
                q_t[h, :, toks] = (turn(base) * HD ** (-0.5)).astype(BF)
                k_t[h, :, toks] = turn(base + 64).astype(BF)
                v_t[h, :, toks] = mixed[base + 128 : base + 192].astype(BF)
        served(p)
        return carry

    lax.fori_loop(0, heads // pair, body, 0)


def upstream_stage(wd, c_ref, up_t, heads):
    for j in range(SEQ_LEN // 256):
        toks = pl.ds(j * 256, 256)
        grad = nt(wd[...], c_ref[toks, :]).astype(BF)
        for h in range(heads):
            up_t[h, :, toks] = grad[HD * h : HD * (h + 1)]


def hide_stage(prefix, hidden_keys):
    for i in range(SEQ_LEN // 256):
        low = 256 * i
        seen = max(512, low + 256)
        place, size = (0, 512) if i == 0 else (256 * (i + 1), 256)
        keys = lax.broadcasted_iota(jnp.int32, (size, 256), 0) + seen - size
        queries = lax.broadcasted_iota(jnp.int32, (size, 256), 1) + low
        hidden_keys[place : place + size, :] = jnp.where((keys <= queries) | (keys < prefix), 0.0, NEGATIVE)


def attend_head(h, hidden_keys, angles, q_t, k_t, v_t, up_t, att_t, gm_t, grad_q, grad_k, grad_v, served):
    keys_plain, values_plain = k_t[h].T, v_t[h].T
    done = 0
    for i in range(SEQ_LEN // 256):
        low = 256 * i
        seen = max(512, low + 256)
        spot = pl.ds(low, 256)
        q, up = q_t[h, :, spot], up_t[h, :, spot]
        scores = nn(keys_plain[0:seen], q)
        place, size = (0, 512) if i == 0 else (256 * (i + 1), 256)
        masked = scores[seen - size :] + hidden_keys[place : place + size, :]
        scores = jnp.concatenate([scores[: seen - size], masked], axis=0) if seen > size else masked
        exponent = jnp.exp(scores - jnp.max(scores, axis=0, keepdims=True))
        probs = exponent * (1.0 / jnp.sum(exponent, axis=0, keepdims=True))
        weights = probs.astype(BF)
        outputs = nn(v_t[h, :, 0:seen], weights)
        att_t[h, :, spot] = outputs.astype(BF)
        inner = jnp.sum(outputs * up.astype(F32), axis=0, keepdims=True)
        grad_probs = nn(values_plain[0:seen], up)
        grad_scores = (probs * (grad_probs - inner)).astype(BF)
        grad_q[:, spot] = nn(k_t[h, :, 0:seen], grad_scores)
        for total, part in ((grad_v, nt(up, weights)), (grad_k, nt(q, grad_scores))):
            if done:
                total[:, 0:done] += part[:, :done]
            if seen > done:
                total[:, done:seen] = part[:, done:]
        done = seen
        served(h, i, SEQ_LEN // 256)
    cos, sin = angles[0:8, :], angles[8:16, :]

    def turn_back(grad):
        g1, g2 = grad[0:8], grad[8:16]
        return jnp.concatenate([g1 * cos + g2 * sin, g2 * cos - g1 * sin, grad[16:]], axis=0)

    base = h * 192
    gm_t[span(base, HD, HD), :] = (turn_back(grad_q[...]) * HD ** (-0.5)).astype(BF)
    gm_t[span(base + HD, HD, HD), :] = turn_back(grad_k[...]).astype(BF)
    gm_t[span(base + 2 * HD, HD, HD), :] = grad_v[...].astype(BF)


def gelu_parts(x):
    below = 0.5 * (1.0 + lax.erf(x * (0.5**0.5)))
    density = jnp.exp(-0.5 * x * x) * (1.0 / math.sqrt(2.0 * math.pi))
    return x * below, below + x * density


def gather_kernel(cols, aligned, *refs):
    (tok_ref, cot_ref, small_ref, bias_in) = refs[:4]
    masters = refs[4:8]
    (x_out, c_out, smalls_out, gq_ref, gd_ref, first_out, first_t_out, gu_out, gp_out, branch_out, comb_out, sum_out) = refs[8:20]
    own = refs[20:24]
    stage = refs[24:28]
    (x_ref, c_ref, smalls, wu, wp, gains, bias_row, second, second_t) = refs[28:37]
    (hidden, slope, ghp, gu, gp, branch, comb) = refs[37:44]
    (z_send, z_recv, s1_send, s1_recv, s2_send, s2_recv, t_send, t_recv, a_send, a_recv, m_send, m_recv, l_sem) = refs[44:]
    full = (gq_ref, wu, gd_ref, wp)
    n_q, n_u = gq_ref.shape[1], wu.shape[1]
    width = ghp.shape[1]
    blocks = n_u // width
    dp, row, col, across, along = places()
    side, at = line_order(row)
    order = [row, at(1 - side), at(2), at(3)]
    middle = side == 1
    tok_col = tok_ref.shape[0]
    part = SEQ_LEN // cols
    chunk = min(tok_col, SEQ_LEN)
    n_seq = tok_col // chunk
    n_part = chunk // part

    loads = [pltpu.make_async_copy(masters[w], stage[w], l_sem.at[w]) for w in range(N_W)]
    for load in loads:
        load.start()
    greet(peers_of(dp, row, col, cols))

    def token_copy(kind, j, i):
        src_ref, dst_ref = ((tok_ref, x_ref), (cot_ref, c_ref))[kind]
        n = j * n_part + i
        if n_seq > 1:
            j = lax.rem(j + (n_seq - 1) * (1 - col), n_seq)
        start = col * tok_col + j * chunk
        to_row = start // SEQ_LEN
        piece = lax.rem(start, SEQ_LEN) // part + i
        src = src_ref.at[span(j * chunk + i * part, part, part), :]
        dst = dst_ref.at[span(piece * part, part, part), span(row * 256, 256, 256)]
        sends, recvs = t_send.at[kind, n], t_recv.at[kind, row]
        is_here = jnp.logical_and(to_row == row, piece == col)
        far = remote(src, dst, sends, recvs, (dp, to_row, piece))
        near = pltpu.make_async_copy(src, dst, recvs)
        return is_here, far, near

    def token_start(kind):
        for j in range(n_seq):
            for i in range(n_part):
                is_here, far, near = token_copy(kind, j, i)
                pl.when(jnp.logical_not(is_here))(far.start)
                pl.when(is_here)(near.start)

    def part_rows(piece):
        return span(piece * part, part, part)

    def spread_copy(kind, step):
        mine = (x_ref, c_ref)[kind].at[part_rows(col), :]
        to_col = lax.rem(col + step, cols)
        return remote(mine, mine, a_send.at[kind, step - 1], a_recv.at[kind, step - 1], (dp, row, to_col))

    def token_spread(kind):
        dst_ref = (x_ref, c_ref)[kind]
        for other in range(ROWS):
            block = dst_ref.at[part_rows(col), pl.ds(other * 256, 256)]
            pltpu.make_async_copy(block, block, t_recv.at[kind, other]).wait()
        for step in range(1, cols):
            spread_copy(kind, step).start()

    def token_finish(kind):
        dst_ref = (x_ref, c_ref)[kind]
        for step in range(1, cols):
            from_col = lax.rem(col + cols - step, cols)
            theirs = dst_ref.at[part_rows(from_col), :]
            pltpu.make_async_copy(theirs, theirs, a_recv.at[kind, step - 1]).wait()

    def token_drain(kind):
        for j in range(n_seq):
            for i in range(n_part):
                is_here, far, near = token_copy(kind, j, i)
                pl.when(jnp.logical_not(is_here))(far.wait_send)
        for step in range(1, cols):
            spread_copy(kind, step).wait_send()

    me = row * DPS + dp

    def small_copy(step):
        flat = lax.rem(me + step, ROWS * DPS)
        return remote(
            small_ref, smalls.at[me], m_send.at[step - 1], m_recv.at[step - 1], (lax.rem(flat, DPS), flat // DPS, col)
        )

    def place(w, r, d, half=None):
        return slot(w, full[w], r, d, own[w].shape[0], half)

    def source(w, k, half=None):
        if k == 0:
            return own[w] if half is None else half_of(w, own[w], half)
        return place(w, order[k], dp, half)

    def line_copies(w, k):
        src = source(w, k)
        dst = place(w, order[k], dp)
        recv = z_recv.at[w, order[k]]
        if k == 0:
            return [
                (None, remote(src, dst, z_send.at[w, 0], recv, (dp, at(1 - side), col))),
                (middle, remote(src, dst, z_send.at[w, 1], recv, (dp, at(2), col))),
            ]
        onward = at(2) if k == 1 else at(0)
        return [(middle, remote(src, dst, z_send.at[w, k + 1], recv, (dp, onward, col)))]

    def first_copies(w, k):
        out = []
        for half, target in ((0, across), (1, along)):
            out.append(
                remote(source(w, k, half), place(w, order[k], dp, half), s1_send.at[w, k, half],
                       s1_recv.at[w, k, half], (target, row, col))
            )
        return out

    def second_copies(w, k, which):
        out = []
        for half, target, other in ((0, along, across), (1, across, along)):
            if which == 0:
                src, owner = source(w, k, half), dp
            else:
                src, owner = place(w, order[k], other, half), other
            out.append(
                remote(src, place(w, order[k], owner, half), s2_send.at[w, k, which, half],
                       s2_recv.at[w, k, which, half], (target, row, col))
            )
        return out

    def onward(w, k):
        if k > 0:
            block = place(w, order[k], dp)
            pltpu.make_async_copy(block, block, z_recv.at[w, order[k]]).wait()
        for cond, copy in line_copies(w, k):
            if cond is None:
                copy.start()
            else:
                pl.when(cond)(copy.start)

    def sideways(w, k):
        for copy in first_copies(w, k) + second_copies(w, k, 0):
            copy.start()

    def arrived(w, k):
        onward(w, k)
        sideways(w, k)

    def passed(w, k):
        for copy in first_copies(w, k):
            copy.wait_recv()
        for copy in second_copies(w, k, 1):
            copy.start()

    def finished(w):
        for k in range(ROWS):
            for which in range(2):
                for copy in second_copies(w, k, which):
                    copy.wait_recv()

    def drained(w, k):
        for cond, copy in line_copies(w, k):
            if cond is None:
                copy.wait_send()
            else:
                pl.when(cond)(copy.wait_send)
        for copy in first_copies(w, k) + second_copies(w, k, 0) + second_copies(w, k, 1):
            copy.wait_send()

    def home(w):
        return pltpu.make_async_copy(own[w], place(w, row, dp), l_sem.at[w])

    def begin(w):
        loads[w].wait()
        own[w][...] = stage[w][...].astype(BF)
        home(w).start()

    small_home = pltpu.make_async_copy(small_ref, smalls.at[me], l_sem.at[N_W])
    kept = []

    def keep(src, dst):
        copy = pltpu.make_async_copy(src, dst, l_sem.at[N_W + 1 + len(kept)])
        copy.start()
        kept.append(copy)

    def smalls_start():
        small_home.start()
        for step in range(1, ROWS * DPS):
            small_copy(step).start()

    def norm(served):
        small_home.wait()
        for step in range(1, ROWS * DPS):
            small_copy(step).wait()
        read_gains(smalls, gains)
        if aligned:
            read_bias(smalls, bias_row, 9 + n_q // (DPS * 128), n_u // DPS)
        else:
            bias_row[...] = bias_in[...]
        branch[...] = jnp.zeros(branch.shape, F32)
        comb[...] = jnp.zeros(comb.shape, F32)
        token_finish(0)
        first, first_t = hidden.at[:, pl.ds(0, D)], hidden.at[:, pl.ds(D, D)]
        norm_stage(x_ref, gains, ((0, first, first_t), (2, second, second_t)), served)
        keep(x_ref, x_out)
        keep(smalls, smalls_out)
        keep(first, first_out)
        keep(first_t, first_t_out)

    def act(word):
        kind, rest = word[0], [int(d) for d in word[1:]]
        {
            "b": begin, "z": onward, "s": sideways, "p": passed, "t": token_start, "d": token_spread, "m": smalls_start,
        }[kind](*rest)

    def forward(served):
        home(UP).wait()
        finished(UP)
        for copy in kept[2:4]:
            copy.wait()

        def block(n, carry):
            cut = span(n * width, width, width)

            def body(j, carry):
                rows = span(j * 256, 256, 256)
                value, slant = gelu_parts(nn(second[rows, :], wu[:, cut]) + bias_row[0:1, cut])
                hidden[rows, cut] = value.astype(BF)
                slope[rows, cut] = slant
                return carry

            lax.fori_loop(0, SEQ_LEN // 256, body, 0)
            served(n)
            return carry

        lax.fori_loop(0, blocks, block, 0)

    def down_grads(served):
        token_finish(1)
        keep(c_ref, c_out)
        h = gp.shape[3]

        def block(n, carry):
            turned = hidden[:, span(n * width, width, width)].T
            if blocks == DPS:
                for half in range(2):
                    gp[n // 2, lax.rem(n, 2), half] = nn(turned[half * h : (half + 1) * h, :], c_ref[...]).astype(BF)
            else:
                gp[...] = nn(turned, c_ref[...]).astype(BF).reshape(2, 2, 2, h, D)
            served(n)
            return carry

        lax.fori_loop(0, blocks, block, 0)
        keep(gp, gp_out)

    def backward(served):
        home(DOWN).wait()
        finished(DOWN)
        sum_out[...] = jnp.zeros(sum_out.shape, F32)

        def block(n, carry):
            cut = span(n * width, width, width)

            def body(j, carry):
                rows = span(j * 256, 256, 256)
                grad = (nt(c_ref[rows, :], wp[cut, :]) * slope[rows, cut]).astype(BF)
                ghp[rows, :] = grad
                branch[rows, :] += nn(hidden[rows, cut], wp[cut, :])
                comb[rows, :] += nt(grad, wu[:, cut])
                sum_out[0:1, cut] += jnp.sum(grad.astype(F32), axis=0, keepdims=True)
                return carry

            for part_of in range(2):
                lax.fori_loop(2 * part_of, 2 * part_of + 2, body, 0)
                served(n, part_of, 3)

            def up_body(r, carry):
                value = nn(second_t[span(r * 256, 256, 256), :], ghp[...]).astype(BF)
                gu[r, :, :, :, :, cut] = value.reshape(2, 2, 2, 32, width)
                return carry

            lax.fori_loop(0, ROWS, up_body, 0)
            served(n, 2, 3)
            return carry

        lax.fori_loop(0, blocks, block, 0)

    loops = {"N": (8, norm), "P": (blocks, forward), "D": (blocks, down_grads), "B": (3 * blocks, backward)}
    plan = GATHER_PLAN
    if blocks != DPS:
        plan = [word for word in plan if word[0] not in loops]
        for kind in "NPDB":
            plan = plan + parts_of(kind, loops[kind][0])
    run(plan, loops, act)
    for src, dst in ((gu, gu_out), (branch, branch_out), (comb, comb_out)):
        keep(src, dst)
    for w in (QKV, DENSE):
        home(w).wait()
        finished(w)
    for w in range(N_W):
        for k in range(ROWS):
            drained(w, k)
    for kind in range(2):
        token_drain(kind)
    for copy in kept[:2] + kept[4:]:
        copy.wait()


def gather(tokens_in, cotangent, small, bias, weights, cols, aligned):
    wq, wu, wd, wp = weights
    n_q, n_u = wq.shape[1], wu.shape[1]
    att_width, h_p = wd.shape[0] * DPS, wp.shape[0]
    width = 512 if n_u == DPS * 512 else n_u
    any_spec = pl.BlockSpec(memory_space=pl.ANY)
    vmem = pl.BlockSpec(memory_space=pltpu.VMEM)
    shape = jax.ShapeDtypeStruct
    smalls = (ROWS * DPS,) + small.shape
    square = (SEQ_LEN, D)
    up_shape, down_shape = (ROWS, 2, 2, 2, 32, n_u), (2, 2, 2, h_p // 2, D)
    out_shape = [
        shape(square, BF), shape(square, BF), shape(smalls, F32), shape((D, n_q), BF), shape((att_width, D), BF),
        shape(square, BF), shape(square, BF), shape(up_shape, BF), shape(down_shape, BF), shape(square, F32),
        shape(square, F32), shape((1, n_u), F32),
    ]
    tok_col = tokens_in.shape[0]
    pieces = tok_col // (SEQ_LEN // cols)
    dma = pltpu.SemaphoreType.DMA
    buf = pltpu.VMEM
    scratch = [buf(w.shape, BF) for w in weights] + [buf(w.shape, F32) for w in weights]
    scratch += [
        buf(square, BF), buf(square, BF), buf(smalls, F32), buf((D, n_u), BF), buf((n_u, D), BF),
        buf((8, D), F32), buf((1, n_u), F32), buf(square, BF), buf(square, BF),
        buf((SEQ_LEN, max(n_u, 2 * D)), BF), buf((SEQ_LEN, n_u), F32), buf((SEQ_LEN, width), BF), buf(up_shape, BF), buf(down_shape, BF), buf(square, F32),
        buf(square, F32),
        dma((N_W, 5)), dma((N_W, 4)), dma((N_W, 4, 2)), dma((N_W, 4, 2)), dma((N_W, 4, 2, 2)), dma((N_W, 4, 2, 2)),
        dma((2, pieces)), dma((2, 4)), dma((2, cols - 1)), dma((2, cols - 1)),
        dma((ROWS * DPS - 1,)), dma((ROWS * DPS - 1,)), dma((N_W + 10,)),
    ]
    return pl.pallas_call(
        functools.partial(gather_kernel, cols, aligned),
        out_shape=out_shape,
        in_specs=[any_spec] * 3 + [vmem] + [any_spec] * 4,
        out_specs=[any_spec] * 11 + [vmem],
        scratch_shapes=scratch,
        compiler_params=pltpu.CompilerParams(collective_id=0, has_side_effects=True, vmem_limit_bytes=60 << 20),
    )(tokens_in, cotangent, small, bias, wq, wu, wd, wp)


SCATTER_PLAN = (
    "f0", "f1", "J0", "J1", "J2", "f2", "J3", "U", "H0", "H1", "H2", "H3", "H4", "H5", "g0", "H6", "H7", "H8",
    "H9", "H10", "g1", "f3", "H11", "H12", "H13", "H14", "H15", "h0", "H16", "H17", "g2", "h1", "H18", "H19", "f4",
    "H20", "g3", "H21", "q0", "H22", "H23", "H24", "h2", "H25", "H26", "H27", "g4", "H28", "f5", "q1", "r0", "H29",
    "h3", "H30", "H31", "h4", "q2", "T", "f6", "q3", "W0", "q4", "X", "f7", "G0", "G1", "G2", "g5", "W1", "G3",
    "f8", "h5", "g6", "g7", "r1", "h6", "f9", "W2", "u0", "q5", "u1", "g8", "r2", "h7", "Y", "W3", "h8", "g9",
    "q6", "f10", "r3", "u2", "f11", "v0", "h9", "r4", "g10", "q7", "u3", "q8", "v1", "h10", "r5", "g11", "v2",
    "h11", "q9", "r6", "u4", "q10", "u5", "r7", "r8", "v3", "r9", "q11", "v4", "r10", "u6", "u7", "u8", "u9",
    "u10", "r11", "u11",
)
PIECES = 12


def add_into(dst, src):
    shape = dst.shape
    outer, height = shape[:-2], shape[-2]
    step = min(32, height)
    per = height // step
    total = math.prod(outer) * per

    def body(i, carry):
        index, rest = [], i // per
        for size in reversed(outer):
            index.append(lax.rem(rest, size))
            rest = rest // size
        where = tuple(reversed(index)) + (span(lax.rem(i, per) * step, step, step),)
        dst[where] = (dst[where].astype(F32) + src[where].astype(F32)).astype(BF)
        return carry

    lax.fori_loop(0, total, body, 0)


def pieces_of(n_q, n_u, h_d, h_p):
    out = []

    def columns(w, n):
        size = 512 if n % 512 == 0 else n
        out.extend((w, start, size) for start in range(0, n, size))

    columns(UP, n_u)
    half = h_p // 2
    size = 64 if half % 64 == 0 else half
    out.extend((DOWN, start, size) for start in range(0, half, size))
    out.append((DENSE, 0, h_d // 2))
    columns(QKV, n_q)
    return out


def scatter_kernel(cols, aligned, pieces, *refs):
    n_p = len(pieces)
    (prefix_ref, smalls, angles, bias_in, sum_u, x_in, c_in, wq_in, wd_in, first_in, first_t_in, gu_in, gp_in, branch_in,
     comb_in) = refs[:15]
    (lo_out, gt_out, oq, ou, od, op, sm_out) = refs[15:22]
    (wq, wd, x_ref, c_ref, first, first_t, q_t, k_t, v_t, up_t, att_t, gm_t, grad_q, grad_k, grad_v) = refs[22:37]
    (gq, gd, att, branch, comb, branch_got, comb_got, gains, bias_row, out_bias, sm, sm_got, gain_sum, hidden_keys) = refs[37:51]
    mine_u, mine_p = refs[51:53], refs[53:55]
    base = 55

    def buffers(start):
        return [refs[start + 2 * i : start + 2 * i + 2] for i in range(n_p)]

    got1, got2, got_end, got_mid = [buffers(base + 2 * n_p * n) for n in range(4)]
    (l_sem, f_sem, s1_send, s1_recv, s2_send, s2_recv, e_send, e_recv, m_send, m_recv, b_send, b_recv, d_send, d_recv,
     t_send, t_recv, v_send, v_recv) = refs[base + 8 * n_p :]
    dp, row, col, across, along = places()
    x, y = lax.rem(dp, 2), dp // 2
    side, at = line_order(row)
    far_end = row // 2
    middle, end = side == 1, side == 0
    n_q, n_u = wq_in.shape[1], sum_u.shape[1]
    heads = q_t.shape[0]
    folded = small_room(n_q, n_u)[0]
    tok_col = lo_out.shape[0]
    part = SEQ_LEN // cols

    def load(src, dst, n):
        return pltpu.make_async_copy(src, dst, l_sem.at[n])

    loads = [load(first_in, first, 0), load(wq_in, wq, 1), load(wd_in, wd, 2), load(c_in, c_ref, 3), load(first_t_in, first_t, 4),
             load(branch_in, branch, 5), load(comb_in, comb, 6), load(x_in, x_ref, 7)]
    for one in loads:
        one.start()
    group = [(dp, lax.rem(row + step, ROWS), lax.rem(col + other, cols)) for step in range(ROWS) for other in range(cols)]
    greet([(across, row, col), (along, row, col)] + group[1:])

    def view(i, half, other):
        w, start, size = pieces[i]
        if half == 0:
            place_y, place_x = (1 - y if other else y), slice(None)
        else:
            place_y, place_x = slice(None), (1 - x if other else x)
        cut = pl.ds(start, size)
        if w in (QKV, UP):
            if w == UP and not other:
                return mine_u[half].at[:, :, :, cut]
            return (gu_in if w == UP else gq).at[:, place_y, place_x, half, :, cut]
        if w == DOWN and not other:
            return mine_p[half].at[:, cut, :]
        return (gp_in if w == DOWN else gd).at[place_y, place_x, half, cut, :]

    def fetch(i, half):
        w, start, size = pieces[i]
        place_y, place_x = (y, slice(None)) if half == 0 else (slice(None), x)
        cut = pl.ds(start, size)
        src = gu_in.at[:, place_y, place_x, half, :, cut] if w == UP else gp_in.at[place_y, place_x, half, cut, :]
        return pltpu.make_async_copy(src, view(i, half, False), f_sem.at[i, half])

    def first_copy(i, half):
        target = along if half == 0 else across
        return remote(view(i, half, True), got1[i][half], s1_send.at[i, half], s1_recv.at[i, half], (target, row, col))

    def keep(i, half, other):
        which = x if half == 0 else y
        which = 1 - which if other else which
        kept = view(i, half, False)
        return kept.at[:, which] if pieces[i][0] in (QKV, UP) else kept.at[which]

    def second_copy(i, half):
        target = across if half == 0 else along
        return remote(keep(i, half, True), got2[i][half], s2_send.at[i, half], s2_recv.at[i, half], (target, row, col))

    def lines(i, ref, start, count):
        if pieces[i][0] in (QKV, UP):
            return ref.at[pl.ds(start, count)]
        return ref.at[:, span(start * 256, count * 256, 256)]

    def end_copy(i, half):
        src = lines(i, keep(i, half, False), 1 - far_end, 3)
        return remote(src, got_end[i][half], e_send.at[i, half], e_recv.at[i, half], (dp, at(1), col))

    def mid_copy(i, half):
        src = lines(i, keep(i, half, False), 2 * (1 - far_end), 2)
        return remote(src, got_mid[i][half], m_send.at[i, half], m_recv.at[i, half], (dp, at(2), col))

    def back_copy(i, half):
        src = lines(i, keep(i, half, False), at(0), 1)
        return remote(src, lines(i, got_mid[i][half], 0, 1), b_send.at[i, half], b_recv.at[i, half], (dp, at(0), col))

    def begin(i):
        for half in range(2):
            first_copy(i, half).start()
            if pieces[i][0] in (UP, DOWN):
                fetch(i, half).start()

    def stage_two(i):
        for half in range(2):
            if pieces[i][0] in (UP, DOWN):
                fetch(i, half).wait()
            first_copy(i, half).wait_recv()
            add_into(view(i, half, False), got1[i][half])
            second_copy(i, half).start()

    def stage_three(i):
        for half in range(2):
            second_copy(i, half).wait_recv()
            add_into(keep(i, half, False), got2[i][half])

            @pl.when(end)
            def _():
                end_copy(i, half).start()

    def stage_four(i):
        @pl.when(middle)
        def _():
            for half in range(2):
                end_copy(i, half).wait_recv()
                add_into(lines(i, keep(i, half, False), 2 * (1 - far_end), 2), lines(i, got_end[i][half], 1 - far_end, 2))
                mid_copy(i, half).start()

    def stage_five(i):
        @pl.when(middle)
        def _():
            for half in range(2):
                mid_copy(i, half).wait_recv()
                add_into(lines(i, keep(i, half, False), at(0), 1), lines(i, got_mid[i][half], far_end, 1))
                back_copy(i, half).start()

    def stage_six(i):
        w, start, size = pieces[i]
        out = (oq, ou, od, op)[w]
        for half in range(2):
            mine = lines(i, keep(i, half, False), row, 1)

            def total(others):
                if w in (QKV, UP):
                    value = mine[0].astype(F32)
                    for other in others:
                        value = value + other[0].astype(F32)
                    out[half, :, pl.ds(start, size)] = value
                else:
                    value = mine[...].astype(F32)
                    for other in others:
                        value = value + other[...].astype(F32)
                    out[half, pl.ds(start, size), :] = value

            @pl.when(end)
            def _():
                back_copy(i, half).wait_recv()
                total([lines(i, got_mid[i][half], 0, 1)])

            @pl.when(middle)
            def _():
                total([lines(i, got_end[i][half], 2 * far_end, 1), lines(i, got_mid[i][half], 1 - far_end, 1)])

    def drain(i):
        for half in range(2):
            first_copy(i, half).wait_send()
            second_copy(i, half).wait_send()

            @pl.when(end)
            def _():
                end_copy(i, half).wait_send()

            @pl.when(middle)
            def _():
                mid_copy(i, half).wait_send()
                back_copy(i, half).wait_send()

    def part_rows(piece):
        return span(piece * part, part, part)

    def col_copy(kind, n):
        other = lax.rem(col + n, cols)
        src = (branch, comb)[kind].at[part_rows(other), :]
        dst = (branch_got, comb_got)[kind].at[n - 1]
        return remote(src, dst, d_send.at[kind, n - 1], d_recv.at[kind, n - 1], (dp, row, other))

    start = row * SEQ_LEN + col * part
    owner, offset = start // tok_col, lax.rem(start, tok_col)

    def out_copy(kind, r):
        src = first.at[pl.ds(kind * part, part), span(r * 256, 256, 256)]
        dst = (lo_out, gt_out)[kind].at[span(offset, part, part), :]
        recv = t_recv.at[kind, offset // part]
        here = jnp.logical_and(row == r, owner == col)
        far = remote(src, dst, t_send.at[kind, r], recv, (dp, r, owner))
        return here, far, pltpu.make_async_copy(src, dst, recv)

    def out_start(kind):
        for r in (at(1 - side), at(2), at(3), row):
            here, far, near = out_copy(kind, r)
            pl.when(jnp.logical_not(here))(far.start)
            pl.when(here)(near.start)

    def out_finish(kind):
        for r in range(ROWS):
            here, far, near = out_copy(kind, r)
            pl.when(jnp.logical_not(here))(far.wait_send)
        out = (lo_out, gt_out)[kind]
        for n in range(tok_col // part):
            block = out.at[pl.ds(n * part, part), :]
            pltpu.make_async_copy(block, block, t_recv.at[kind, n]).wait()

    height = min(128, part)

    def finish_rows(kind):
        for n in range(1, cols):
            col_copy(kind, n).wait_recv()

        def body(i, carry):
            here = span(i * height, height, height)
            rows = span(col * part + i * height, height, height)
            value = (branch, comb)[kind][rows, :]
            for n in range(1, cols):
                value = value + (branch_got, comb_got)[kind][n - 1, here, :]
            wide = x_ref[rows, :].astype(F32)
            if kind == 0:
                value = wide + value + out_bias[0:1, :]
            else:
                normed, scale_inv = norm_rows(wide)
                mean = jnp.mean(value, axis=1, keepdims=True)
                cross = jnp.mean(value * normed, axis=1, keepdims=True)
                value = c_ref[rows, :].astype(F32) + scale_inv * (value - mean - normed * cross)
            first[span(kind * part + i * height, height, height), :] = value.astype(BF)
            return carry

        lax.fori_loop(0, part // height, body, 0)

    def small_copy(n):
        if n < 2:
            return remote(sm.at[n], sm_got.at[n], v_send.at[n], v_recv.at[n], ((across, along)[n], row, col))
        if n < 5:
            target = (dp, lax.rem(row + n - 1, ROWS), col)
            return remote(sm.at[2], sm_got.at[n], v_send.at[n], v_recv.at[n], target)
        target = (dp, row, lax.rem(col + n - 4, cols))
        return remote(sm.at[3], sm_got.at[n], v_send.at[n], v_recv.at[n], target)

    def small_step(n):
        if n > 0:
            waits = ((0,), (1,), (2, 3, 4), tuple(range(5, 4 + cols)))[n - 1]
            for m in waits:
                small_copy(m).wait_recv()
            value = sm[n - 1]
            if n < 4:
                for m in waits:
                    value = value + sm_got[m]
                sm[n] = value
            else:
                sm_out[...] = value
                value = value[0:4, 0:D]
                for m in waits:
                    value = value + sm_got[m, 0:4, 0:D]
                sm_out[0:4, 0:D] = value
        for m in ((0,), (1,), (2, 3, 4), tuple(range(5, 4 + cols)), ())[n]:
            small_copy(m).start()

    def project(served):
        read_gains(smalls, gains)
        lanes = lax.broadcasted_iota(jnp.int32, (1, 128), 1)
        for r in range(ROWS):
            for d in range(0, DPS, 2):
                both = [rounded(smalls[r * DPS + d + n, 8:9, :]) for n in range(2)]
                both = [value + pltpu.roll(value, 64, 1) for value in both]
                out_bias[0:1, pl.ds(r * 256 + d * 64, 128)] = jnp.where(lanes < 64, both[0], both[1])
        if aligned:
            read_bias(smalls, bias_row, 9, n_q // DPS)
        else:
            bias_row[...] = bias_in[...]
        sm[0] = jnp.zeros(sm.shape[1:], F32)
        put_up(sm.at[0], sum_u[...], folded)
        loads[0].wait()
        loads[1].wait()
        project_stage(wq, first, bias_row, angles, q_t, k_t, v_t, heads, served)

    def upstream():
        loads[2].wait()
        loads[3].wait()
        upstream_stage(wd, c_ref, up_t, heads)

    def attended():
        group_h = min(heads, 4)

        def turn_body(i, carry):
            block = att_t[pl.ds(i * group_h, group_h)].reshape(group_h * HD, SEQ_LEN)
            spot = pl.ds(0, group_h * HD) if heads == group_h else span(i * group_h * HD, group_h * HD, 128)
            att[:, spot] = block.T
            return carry

        lax.fori_loop(0, heads // group_h, turn_body, 0)
        loads[5].wait()

        def out_body(j, carry):
            rows = span(j * 256, 256, 256)
            branch[rows, :] += nn(att[rows, :], wd[...])
            return carry

        lax.fori_loop(0, SEQ_LEN // 256, out_body, 0)
        for n in range(1, cols):
            col_copy(0, n).start()

    def weight_grads(n):
        if n == 0:
            all_heads = att_t[...].reshape(heads * HD, SEQ_LEN)
            gd[...] = nn(all_heads, c_ref[...]).astype(BF).reshape(gd.shape)
            return
        if n == 1:
            loads[4].wait()
        wide = min(512, n_q)
        cut = pl.ds((n - 1) * wide, wide)

        def qkv_body(r, carry):
            rows = span(r * 256, 256, 256)
            gq[r, :, :, :, :, cut] = nt(first_t[rows, :], gm_t[cut, :]).astype(BF).reshape(2, 2, 2, 32, wide)
            return carry

        lax.fori_loop(0, ROWS, qkv_body, 0)

    need_x = [loads[7]]

    def output_home():
        if len(need_x):
            need_x.pop().wait()
        finish_rows(0)
        out_start(0)

    def features(served):
        loads[6].wait()
        if len(need_x):
            need_x.pop().wait()
        for n in range(8):
            gain_sum[n : n + 1, :] = jnp.zeros((1, D), F32)

        def body(j, carry):
            rows = span(j * 256, 256, 256)
            grad = gm_t[:, rows].T
            grad_first = nt(grad, wq[...])
            grad_second = comb[rows, :]
            normed, ignored = norm_rows(x_ref[rows, :].astype(F32))
            for n, value in enumerate((normed * grad_first, grad_first, normed * grad_second, grad_second,
                                       c_ref[rows, :].astype(F32))):
                gain_sum[n : n + 1, :] += jnp.sum(value, axis=0, keepdims=True)
            add_qkv(sm.at[0], jnp.sum(grad.astype(F32), axis=0, keepdims=True), folded)
            comb[rows, :] = gains[0:1, :] * grad_first + gains[2:3, :] * grad_second
            served(j)
            return carry

        lax.fori_loop(0, SEQ_LEN // 256, body, 0)
        for n in range(1, cols):
            col_copy(1, n).start()
        sm[0, 0:5, 0:D] = gain_sum[0:5, :]

    def gradient_home():
        finish_rows(1)
        out_start(1)

    stages = {"f": begin, "g": stage_two, "h": stage_three, "q": stage_four, "r": stage_five, "u": stage_six}
    others = {"U": upstream, "T": attended, "X": output_home, "Y": gradient_home}

    def act(word):
        kind, rest = word[0], word[1:]
        if kind in others:
            others[kind]()
        elif kind == "W":
            weight_grads(int(rest))
        elif kind == "v":
            small_step(int(rest))
        else:
            stages[kind](int(rest))

    def attention(served):
        hide_stage(prefix_ref[0], hidden_keys)

        def head_body(h, carry):
            attend_head(h, hidden_keys, angles, q_t, k_t, v_t, up_t, att_t, gm_t, grad_q, grad_k, grad_v, served)
            return carry

        lax.fori_loop(0, heads, head_body, 0)

    loops = {
        "J": (heads // min(heads, 2), project), "H": (heads * (SEQ_LEN // 256), attention), "G": (SEQ_LEN // 256, features),
    }
    plan = SCATTER_PLAN
    if n_p != PIECES:
        late = [i for i in range(n_p) if pieces[i][0] in (QKV, DENSE)]
        plan = ["f%d" % i for i in range(n_p) if i not in late] + parts_of("J", loops["J"][0]) + ["U"]
        plan = plan + parts_of("H", loops["H"][0]) + ["T", "W0", "W1", "X"] + parts_of("G", loops["G"][0]) + ["Y"]
        plan = plan + ["f%d" % i for i in late] + [s + str(i) for s in "ghqru" for i in range(n_p)] + parts_of("v", 5)
    run(plan, loops, act)
    for i in range(n_p):
        drain(i)
    for kind in range(2):
        out_finish(kind)
    for n in range(1, cols):
        for kind in range(2):
            col_copy(kind, n).wait_send()
    for n in range(4 + cols):
        small_copy(n).wait_send()


def scatter(prefix_len, smalls, angles, bias, sum_u, own_x, own_cot, wq, wd, first, first_t, gu, gp, branch, comb, cols, aligned,
            tok_col):
    any_spec = pl.BlockSpec(memory_space=pl.ANY)
    vmem = pl.BlockSpec(memory_space=pltpu.VMEM)
    smem = pl.BlockSpec(memory_space=pltpu.SMEM)
    dma = pltpu.SemaphoreType.DMA
    buf = pltpu.VMEM
    shape = jax.ShapeDtypeStruct
    n_q, n_u = wq.shape[1], sum_u.shape[1]
    heads = n_q // 192
    h_d, h_p = wd.shape[0] // DPS, 2 * gp.shape[3]
    pieces = pieces_of(n_q, n_u, h_d, h_p)
    n_p = len(pieces)
    part = SEQ_LEN // cols
    line = small_room(n_q, n_u)[1]
    square = (SEQ_LEN, D)
    turned = buf((heads, HD, SEQ_LEN), BF)
    scratch = [
        buf((D, n_q), BF), buf(wd.shape, BF), buf(square, BF), buf(square, BF), buf(square, BF), buf(square, BF),
        turned, turned, turned, turned, turned, buf((n_q, SEQ_LEN), BF),
        buf((HD, SEQ_LEN), F32), buf((HD, SEQ_LEN), F32), buf((HD, SEQ_LEN), F32),
        buf((ROWS, 2, 2, 2, 32, n_q), BF), buf((2, 2, 2, h_d // 2, D), BF), buf((SEQ_LEN, heads * HD), BF), buf(square, F32), buf(square, F32),
        buf((cols - 1, part, D), F32), buf((cols - 1, part, D), F32),
        buf((8, D), F32), buf((1, n_q), F32), buf((1, D), F32), buf((4, 8, line), F32), buf((4 + cols, 8, line), F32),
        buf((8, D), F32), buf((1280, 256), F32),
    ]
    scratch += [buf((ROWS, 2, 32, n_u), BF)] * 2 + [buf((2, h_p // 2, D), BF)] * 2
    for lead, count in (((ROWS, 2), None), ((ROWS,), None), ((3,), 3), ((2,), 2)):
        for w, start, size in pieces:
            if w in (QKV, UP):
                one = lead + (32, size)
            elif count is None:
                one = ((2,) if len(lead) == 2 else ()) + (size, D)
            else:
                one = (size, 256 * count)
            scratch += [buf(one, BF)] * 2
    scratch += [
        dma((8,)), dma((n_p, 2)), dma((n_p, 2)), dma((n_p, 2)), dma((n_p, 2)), dma((n_p, 2)), dma((n_p, 2)), dma((n_p, 2)),
        dma((n_p, 2)), dma((n_p, 2)), dma((n_p, 2)), dma((n_p, 2)), dma((2, cols - 1)), dma((2, cols - 1)),
        dma((2, ROWS)), dma((2, tok_col // part)), dma((4 + cols,)), dma((4 + cols,)),
    ]
    return pl.pallas_call(
        functools.partial(scatter_kernel, cols, aligned, pieces),
        out_shape=[
            shape((tok_col, 256), BF), shape((tok_col, 256), BF), shape((2, 32, n_q), F32), shape((2, 32, n_u), F32),
            shape((2, h_d // 2, 256), F32), shape((2, h_p // 2, 256), F32), shape((8, line), F32),
        ],
        in_specs=[smem, vmem, vmem, vmem, vmem] + [any_spec] * 10,
        out_specs=[any_spec] * 2 + [vmem] * 5,
        scratch_shapes=scratch,
        compiler_params=pltpu.CompilerParams(collective_id=1, has_side_effects=True, vmem_limit_bytes=63 << 20),
    )(prefix_len, smalls, angles, bias, sum_u, own_x, own_cot, wq, wd, first, first_t, gu, gp, branch, comb)


def small_room(n_q, n_u):
    folded = n_q == D + 512 and n_u == 2 * D
    return folded, (D + 128 if folded else max(n_q, n_u, D))


def put_up(rows, value, folded):
    if not folded:
        rows[6:7, 0 : value.shape[1]] = value
        return
    rows[6:7, 0:D] = value[:, 0:D]
    rows[7:8, 0:D] = value[:, D:]


def add_qkv(rows, value, folded):
    if not folded:
        rows[5:6, 0 : value.shape[1]] += value
        return
    rows[5:6, 0:D] += value[:, 0:D]
    for n in range(4):
        rows[n : n + 1, D : D + 128] += value[:, D + 128 * n : D + 128 * (n + 1)]


def finish_kernel(*refs):
    whole_in, sums, whole_out, q_b, u_b, d_b, p_b, gains, rooms, sem = (
        refs[:6], refs[6], refs[7:13], *refs[13:17], refs[17:21], refs[21:27], refs[27]
    )
    q_row, u_row = refs[28], refs[29]
    arrive = [pltpu.make_async_copy(src, dst, sem.at[0, n]) for n, (src, dst) in enumerate(zip(whole_in, rooms))]
    leave = [pltpu.make_async_copy(src, dst, sem.at[1, n]) for n, (src, dst) in enumerate(zip(rooms, whole_out))]
    for copy in arrive:
        copy.start()
    dp, row = lax.axis_index("dp"), lax.axis_index("row")
    for n, gain in enumerate(gains):
        gain[...] = sums[n : n + 1, span(row * 256, 256, 256)].reshape(gain.shape)
    if sums.shape[1] == D + 128:
        q_row[:, 0:D] = sums[5:6, 0:D]
        for n in range(4):
            q_row[:, D + 128 * n : D + 128 * (n + 1)] = sums[n : n + 1, D : D + 128]
        u_row[:, 0:D] = sums[6:7, 0:D]
        u_row[:, D:] = sums[7:8, 0:D]
    else:
        q_row[...] = sums[5:6, 0 : q_row.shape[1]]
        u_row[...] = sums[6:7, 0 : u_row.shape[1]]
    for row_of, bias in ((q_row, q_b), (u_row, u_b)):
        size = bias.shape[0]
        bias[...] = row_of[0:1, span(dp * size, size, 128)].reshape(bias.shape)
    me = row * DPS + dp
    pair = sums[4:5, span((me // 2) * 128, 128, 128)]
    pair = jnp.where(lax.rem(me, 2) == 0, pair, pltpu.roll(pair, 64, 1))
    for bias in (d_b, p_b):
        bias[...] = pair[:, 0:64].reshape(bias.shape)
    for first, then in zip(arrive, leave):
        first.wait()
        then.start()
    for copy in leave:
        copy.wait()


def finish(whole, sums, n_qb, n_ub):
    any_spec = pl.BlockSpec(memory_space=pl.ANY)
    vmem = pl.BlockSpec(memory_space=pltpu.VMEM)
    shape = jax.ShapeDtypeStruct
    sizes = [n_qb, n_ub, 64, 64] + [256] * 4
    out = pl.pallas_call(
        finish_kernel,
        out_shape=[shape(a.shape, a.dtype) for a in whole] + [shape((size,), F32) for size in sizes],
        in_specs=[any_spec] * 6 + [vmem],
        out_specs=[any_spec] * 6 + [vmem] * 8,
        scratch_shapes=[pltpu.VMEM(a.shape, a.dtype) for a in whole] + [
            pltpu.SemaphoreType.DMA((2, 6)), pltpu.VMEM((1, n_qb * DPS), F32), pltpu.VMEM((1, n_ub * DPS), F32),
        ],
    )(*whole, sums)
    lo, gt, gq, gu, gd, gp, q_b, u_b, d_b, p_b, *gains = out
    return (lo, gt, gq, q_b, gu, u_b, gd, d_b, gp, p_b, *gains)


def angles_table():
    half_rot = ROT // 2
    rates = np.exp(np.arange(half_rot, dtype=np.float32) * np.float32(-2.0 * math.log(10000.0) / ROT))
    turned = rates.astype(np.float32)[:, None] * np.arange(SEQ_LEN, dtype=np.float32)[None, :]
    return np.concatenate([np.cos(turned), np.sin(turned)], axis=0).astype(np.float32)


def shards(cols, tokens_in, prefix_len, first_gain, first_shift, second_gain, second_shift, qkv_weight, qkv_bias,
           up_weight, up_bias, dense_weight, dense_bias, down_weight, down_bias, cotangent):
    tok_col = tokens_in.shape[0]
    n_q, n_u = qkv_weight.shape[1], up_weight.shape[1]

    n_qb, n_ub = qkv_bias.shape[0], up_bias.shape[0]
    aligned = n_qb % 128 == 0 and n_ub % 128 == 0
    small = jnp.concatenate((first_gain, first_shift, second_gain, second_shift, dense_bias, down_bias, qkv_bias, up_bias))
    size = -(-small.shape[0] // 1024) * 1024
    small = jnp.pad(small, (0, size - small.shape[0])).reshape(size // 128, 128)
    if aligned:
        q_bias = u_bias = small
    else:
        q_bias = lax.all_gather(rounded(qkv_bias), "dp", axis=0, tiled=True).reshape(1, n_q)
        u_bias = lax.all_gather(rounded(up_bias), "dp", axis=0, tiled=True).reshape(1, n_u)
    own_x, own_cot, smalls, wq, wd, first, first_t, gu, gp, branch, comb, sum_u = gather(
        tokens_in, cotangent, small, u_bias, (qkv_weight, up_weight, dense_weight, down_weight), cols, aligned
    )
    layer_out, grad_tokens, out_q, out_u, out_d, out_p, sums = scatter(
        prefix_len, smalls, jnp.asarray(angles_table()), q_bias, sum_u, own_x, own_cot, wq, wd, first, first_t, gu, gp, branch,
        comb, cols, aligned, tok_col
    )
    h_d, h_p = dense_weight.shape[0], down_weight.shape[0]
    whole = (
        layer_out, grad_tokens, out_q.reshape(64, n_q), out_u.reshape(64, n_u), out_d.reshape(h_d, 256), out_p.reshape(h_p, 256)
    )
    if aligned:
        return finish(whole, sums, n_qb, n_ub)
    dp, row = lax.axis_index("dp"), lax.axis_index("row")
    gain_sums = lax.dynamic_slice(sums, (0, row * 256), (4, 256))
    out_b = lax.dynamic_slice(sums, (4, (row * DPS + dp) * 64), (1, 64))[0]
    q_b = lax.dynamic_slice(sums, (5, dp * n_qb), (1, n_qb))[0]
    u_b = lax.dynamic_slice(sums, (6, dp * n_ub), (1, n_ub))[0]
    return (
        whole[0], whole[1], whole[2], q_b, whole[3], u_b, whole[4], out_b, whole[5], out_b,
        gain_sums[0], gain_sums[1], gain_sums[2], gain_sums[3],
    )


def solution(mesh):
    in_specs = (
        P(("dp", "col"), "row"), P(("dp", "row")), P("row"), P("row"), P("row"), P("row"),
        P(("row", "dp"), "col"), P(("col", "dp")), P(("row", "dp"), "col"), P(("col", "dp")),
        P(("col", "dp"), "row"), P(("row", "dp")), P(("col", "dp"), "row"), P(("row", "dp")),
        P(("dp", "col"), "row"),
    )
    out_specs = (
        P(("dp", "col"), "row"), P(("dp", "col"), "row"), P(("row", "dp"), "col"), P(("col", "dp")),
        P(("row", "dp"), "col"), P(("col", "dp")), P(("col", "dp"), "row"), P(("row", "dp")),
        P(("col", "dp"), "row"), P(("row", "dp")), P("row"), P("row"), P("row"), P("row"),
    )
    body = functools.partial(shards, mesh.shape["col"])
    return jax.shard_map(body, mesh=mesh, in_specs=in_specs, out_specs=out_specs, check_vma=False)
```

```python
import functools
import math

import jax
import jax.numpy as jnp
import numpy as np
from jax import lax
from jax.experimental import pallas as pl
from jax.experimental.pallas import tpu as pltpu
from jax.sharding import PartitionSpec as P

D = 1024
HD = 64
ROT = 16
FF = 4096
SEQ_LEN = 1024
EPS = 1e-05
NEGATIVE = -1e30
ROWS = 4
DPS = 4
MESH = pl.DeviceIdType.MESH
BF = jnp.bfloat16
F32 = jnp.float32


def places():
    dp, row, col = lax.axis_index("dp"), lax.axis_index("row"), lax.axis_index("col")
    across = dp + 1 - 2 * lax.rem(dp, 2)
    along = lax.rem(dp + 2, 4)
    return dp, row, col, across, along


def line_order(row):
    far = row // 2
    side = row + far * (3 - 2 * row)
    at = lambda place: far * 3 + (1 - 2 * far) * place
    return side, at


def greet(targets):
    barrier = pltpu.get_barrier_semaphore()
    for target in targets:
        pl.semaphore_signal(barrier, inc=1, device_id=target, device_id_type=MESH)
    pl.semaphore_wait(barrier, len(targets))


def peers_of(dp, row, col, cols):
    group = []
    for step in range(1, ROWS * cols):
        flat = lax.rem(row * cols + col + step, ROWS * cols)
        group.append((dp, flat // cols, lax.rem(flat, cols)))
    for step in range(1, DPS):
        for other in range(ROWS):
            group.append((lax.rem(dp + step, DPS), lax.rem(row + other, ROWS), col))
    return group


def remote(src, dst, send, recv, target):
    return pltpu.make_async_remote_copy(
        src_ref=src, dst_ref=dst, send_sem=send, recv_sem=recv, device_id=target, device_id_type=MESH
    )


N_W = 4
QKV, UP, DENSE, DOWN = range(N_W)
GATHER_PLAN = (
    "b1", "z10", "b3", "s30", "b2", "z30", "s10", "z11", "z12", "s11", "m", "z31", "z20", "s12", "p11", "z13",
    "p30", "s13", "t0", "s20", "z32", "p10", "b0", "p13", "t1", "s32", "d0", "s31", "N0", "p12", "N1", "N2", "N3",
    "N4", "s00", "z33", "s33", "N5", "N6", "z00", "N7", "p32", "P0", "P1", "z21", "p31", "P2", "P3", "d1", "p33",
    "s21", "z01", "s01", "D0", "D1", "D2", "D3", "z22", "s22", "z02", "B0", "B1", "s02", "p21", "B2", "B3", "B4",
    "z23", "p02", "z03", "B5", "p00", "p20", "s03", "B6", "B7", "s23", "p22", "B8", "p03", "B9", "B10", "B11",
    "p23", "p01",
)


def run(words, loops, act):
    i = 0
    while i < len(words):
        kind = words[i][0]
        if kind not in loops:
            act(words[i])
            i += 1
            continue
        count, body = loops[kind]
        groups = [[]]
        i += 1
        while len(groups) < count:
            if words[i][0] == kind:
                groups.append([])
            else:
                groups[-1].append(words[i])
            i += 1

        def served(index, first=0, stride=1):
            for n, group in enumerate(groups[first::stride]):
                if group:

                    @pl.when(index == n)
                    def _():
                        for word in group:
                            act(word)

        body(served)


def parts_of(kind, count):
    return ["%s%d" % (kind, n) for n in range(count)]


def nt(left, right):
    return lax.dot_general(left, right, (((1,), (1,)), ((), ())), preferred_element_type=F32)


def nn(left, right):
    return jnp.dot(left, right, preferred_element_type=F32)


def span(start, size, unit):
    return pl.ds(pl.multiple_of(start, unit), size)


def slot(w, ref, row, dp, height, half=None):
    if w in (QKV, UP):
        if half is None:
            return ref.at[span((row * DPS + dp) * height, height, 64), :]
        return ref.at[span((row * DPS + dp) * height + half * (height // 2), height // 2, 32), :]
    if half is None:
        return ref.at[span(dp * height, height, 16), span(row * 256, 256, 256)]
    if w == DENSE:
        return ref.at[span(dp * height, height, 16), span(row * 256 + half * 128, 128, 128)]
    return ref.at[span(dp * height + half * (height // 2), height // 2, 16), span(row * 256, 256, 256)]


def half_of(w, ref, half):
    height = ref.shape[0]
    if w == DENSE:
        return ref.at[:, pl.ds(half * 128, 128)]
    return ref.at[pl.ds(half * (height // 2), height // 2), :]


def read_gains(smalls, gains):
    for r in range(ROWS):
        for g in range(4):
            for t in range(2):
                gains[g : g + 1, pl.ds(r * 256 + t * 128, 128)] = smalls[r * DPS, pl.ds(2 * g + t, 1), :]


def rounded(value):
    return value.astype(BF).astype(F32)


def read_bias(smalls, bias, first_row, size):
    per = size // 128
    for d in range(DPS):
        for t in range(per):
            bias[0:1, pl.ds(d * size + t * 128, 128)] = rounded(smalls[d, pl.ds(first_row + t, 1), :])


def norm_rows(x):
    center = jnp.mean(x, axis=1, keepdims=True)
    spread = jnp.mean(x * x, axis=1, keepdims=True) - center * center
    scale_inv = lax.rsqrt(spread + EPS)
    return (x - center) * scale_inv, scale_inv


def norm_stage(x_ref, gains, outs, served):
    def body(i, carry):
        rows = span(i * 128, 128, 128)
        normed, ignored = norm_rows(x_ref[rows, :].astype(F32))
        for which, plain, turned in outs:
            value = (normed * gains[which : which + 1, :] + gains[which + 1 : which + 2, :]).astype(BF)
            plain[rows, :] = value
            turned[:, rows] = value.T
        served(i)
        return carry

    lax.fori_loop(0, SEQ_LEN // 128, body, 0)


def project_stage(wq, first, bias_row, angles, q_t, k_t, v_t, heads, served):
    pair = min(heads, 2)
    width = 192 * pair

    def body(p, carry):
        cols = pl.ds(0, width) if heads == pair else span(p * width, width, 128)
        w_t = wq[:, cols].T
        bias = jnp.broadcast_to(bias_row[0:1, cols], (8, width)).T[:, 0:1]
        for j in range(SEQ_LEN // 256):
            toks = pl.ds(j * 256, 256)
            mixed = nt(w_t, first[toks, :]) + bias
            cos, sin = angles[0:8, toks], angles[8:16, toks]

            def turn(base):
                x1, x2 = mixed[base : base + 8], mixed[base + 8 : base + 16]
                return jnp.concatenate([x1 * cos - x2 * sin, x2 * cos + x1 * sin, mixed[base + 16 : base + 64]], axis=0)

            for e in range(pair):
                base, h = 192 * e, pair * p + e
                q_t[h, :, toks] = (turn(base) * HD ** (-0.5)).astype(BF)
                k_t[h, :, toks] = turn(base + 64).astype(BF)
                v_t[h, :, toks] = mixed[base + 128 : base + 192].astype(BF)
        served(p)
        return carry

    lax.fori_loop(0, heads // pair, body, 0)


def upstream_stage(wd, c_ref, up_t, heads):
    for j in range(SEQ_LEN // 256):
        toks = pl.ds(j * 256, 256)
        grad = nt(wd[...], c_ref[toks, :]).astype(BF)
        for h in range(heads):
            up_t[h, :, toks] = grad[HD * h : HD * (h + 1)]


def hide_stage(prefix, hidden_keys):
    for i in range(SEQ_LEN // 256):
        low = 256 * i
        seen = max(512, low + 256)
        place, size = (0, 512) if i == 0 else (256 * (i + 1), 256)
        keys = lax.broadcasted_iota(jnp.int32, (size, 256), 0) + seen - size
        queries = lax.broadcasted_iota(jnp.int32, (size, 256), 1) + low
        hidden_keys[place : place + size, :] = jnp.where((keys <= queries) | (keys < prefix), 0.0, NEGATIVE)


def attend_head(h, hidden_keys, angles, q_t, k_t, v_t, up_t, att_t, gm_t, grad_q, grad_k, grad_v, served):
    keys_plain, values_plain = k_t[h].T, v_t[h].T
    done = 0
    for i in range(SEQ_LEN // 256):
        low = 256 * i
        seen = max(512, low + 256)
        spot = pl.ds(low, 256)
        q, up = q_t[h, :, spot], up_t[h, :, spot]
        scores = nn(keys_plain[0:seen], q)
        place, size = (0, 512) if i == 0 else (256 * (i + 1), 256)
        masked = scores[seen - size :] + hidden_keys[place : place + size, :]
        scores = jnp.concatenate([scores[: seen - size], masked], axis=0) if seen > size else masked
        exponent = jnp.exp(scores - jnp.max(scores, axis=0, keepdims=True))
        probs = exponent * (1.0 / jnp.sum(exponent, axis=0, keepdims=True))
        weights = probs.astype(BF)
        outputs = nn(v_t[h, :, 0:seen], weights)
        att_t[h, :, spot] = outputs.astype(BF)
        inner = jnp.sum(outputs * up.astype(F32), axis=0, keepdims=True)
        grad_probs = nn(values_plain[0:seen], up)
        grad_scores = (probs * (grad_probs - inner)).astype(BF)
        grad_q[:, spot] = nn(k_t[h, :, 0:seen], grad_scores)
        for total, part in ((grad_v, nt(up, weights)), (grad_k, nt(q, grad_scores))):
            if done:
                total[:, 0:done] += part[:, :done]
            if seen > done:
                total[:, done:seen] = part[:, done:]
        done = seen
        served(h, i, SEQ_LEN // 256)
    cos, sin = angles[0:8, :], angles[8:16, :]

    def turn_back(grad):
        g1, g2 = grad[0:8], grad[8:16]
        return jnp.concatenate([g1 * cos + g2 * sin, g2 * cos - g1 * sin, grad[16:]], axis=0)

    base = h * 192
    gm_t[span(base, HD, HD), :] = (turn_back(grad_q[...]) * HD ** (-0.5)).astype(BF)
    gm_t[span(base + HD, HD, HD), :] = turn_back(grad_k[...]).astype(BF)
    gm_t[span(base + 2 * HD, HD, HD), :] = grad_v[...].astype(BF)


def gelu_parts(x):
    below = 0.5 * (1.0 + lax.erf(x * (0.5**0.5)))
    density = jnp.exp(-0.5 * x * x) * (1.0 / math.sqrt(2.0 * math.pi))
    return x * below, below + x * density


def gather_kernel(cols, aligned, *refs):
    (tok_ref, cot_ref, small_ref, bias_in) = refs[:4]
    masters = refs[4:8]
    (x_out, c_out, smalls_out, gq_ref, gd_ref, first_out, first_t_out, gu_out, gp_out, branch_out, comb_out, sum_out) = refs[8:20]
    own = refs[20:24]
    stage = refs[24:28]
    (x_ref, c_ref, smalls, wu, wp, gains, bias_row, second, second_t) = refs[28:37]
    (hidden, slope, ghp, gu, gp, branch, comb) = refs[37:44]
    (z_send, z_recv, s1_send, s1_recv, s2_send, s2_recv, t_send, t_recv, a_send, a_recv, m_send, m_recv, l_sem) = refs[44:]
    full = (gq_ref, wu, gd_ref, wp)
    n_q, n_u = gq_ref.shape[1], wu.shape[1]
    width = ghp.shape[1]
    blocks = n_u // width
    dp, row, col, across, along = places()
    side, at = line_order(row)
    order = [row, at(1 - side), at(2), at(3)]
    middle = side == 1
    tok_col = tok_ref.shape[0]
    part = SEQ_LEN // cols
    chunk = min(tok_col, SEQ_LEN)
    n_seq = tok_col // chunk
    n_part = chunk // part

    loads = [pltpu.make_async_copy(masters[w], stage[w], l_sem.at[w]) for w in range(N_W)]
    for load in loads:
        load.start()
    greet(peers_of(dp, row, col, cols))

    def token_copy(kind, j, i):
        src_ref, dst_ref = ((tok_ref, x_ref), (cot_ref, c_ref))[kind]
        n = j * n_part + i
        if n_seq > 1:
            j = lax.rem(j + (n_seq - 1) * (1 - col), n_seq)
        start = col * tok_col + j * chunk
        to_row = start // SEQ_LEN
        piece = lax.rem(start, SEQ_LEN) // part + i
        src = src_ref.at[span(j * chunk + i * part, part, part), :]
        dst = dst_ref.at[span(piece * part, part, part), span(row * 256, 256, 256)]
        sends, recvs = t_send.at[kind, n], t_recv.at[kind, row]
        is_here = jnp.logical_and(to_row == row, piece == col)
        far = remote(src, dst, sends, recvs, (dp, to_row, piece))
        near = pltpu.make_async_copy(src, dst, recvs)
        return is_here, far, near

    def token_start(kind):
        for j in range(n_seq):
            for i in range(n_part):
                is_here, far, near = token_copy(kind, j, i)
                pl.when(jnp.logical_not(is_here))(far.start)
                pl.when(is_here)(near.start)

    def part_rows(piece):
        return span(piece * part, part, part)

    def spread_copy(kind, step):
        mine = (x_ref, c_ref)[kind].at[part_rows(col), :]
        to_col = lax.rem(col + step, cols)
        return remote(mine, mine, a_send.at[kind, step - 1], a_recv.at[kind, step - 1], (dp, row, to_col))

    def token_spread(kind):
        dst_ref = (x_ref, c_ref)[kind]
        for other in range(ROWS):
            block = dst_ref.at[part_rows(col), pl.ds(other * 256, 256)]
            pltpu.make_async_copy(block, block, t_recv.at[kind, other]).wait()
        for step in range(1, cols):
            spread_copy(kind, step).start()

    def token_finish(kind):
        dst_ref = (x_ref, c_ref)[kind]
        for step in range(1, cols):
            from_col = lax.rem(col + cols - step, cols)
            theirs = dst_ref.at[part_rows(from_col), :]
            pltpu.make_async_copy(theirs, theirs, a_recv.at[kind, step - 1]).wait()

    def token_drain(kind):
        for j in range(n_seq):
            for i in range(n_part):
                is_here, far, near = token_copy(kind, j, i)
                pl.when(jnp.logical_not(is_here))(far.wait_send)
        for step in range(1, cols):
            spread_copy(kind, step).wait_send()

    me = row * DPS + dp

    def small_copy(step):
        flat = lax.rem(me + step, ROWS * DPS)
        return remote(
            small_ref, smalls.at[me], m_send.at[step - 1], m_recv.at[step - 1], (lax.rem(flat, DPS), flat // DPS, col)
        )

    def place(w, r, d, half=None):
        return slot(w, full[w], r, d, own[w].shape[0], half)

    def source(w, k, half=None):
        if k == 0:
            return own[w] if half is None else half_of(w, own[w], half)
        return place(w, order[k], dp, half)

    def line_copies(w, k):
        src = source(w, k)
        dst = place(w, order[k], dp)
        recv = z_recv.at[w, order[k]]
        if k == 0:
            return [
                (None, remote(src, dst, z_send.at[w, 0], recv, (dp, at(1 - side), col))),
                (middle, remote(src, dst, z_send.at[w, 1], recv, (dp, at(2), col))),
            ]
        onward = at(2) if k == 1 else at(0)
        return [(middle, remote(src, dst, z_send.at[w, k + 1], recv, (dp, onward, col)))]

    def first_copies(w, k):
        out = []
        for half, target in ((0, across), (1, along)):
            out.append(
                remote(source(w, k, half), place(w, order[k], dp, half), s1_send.at[w, k, half],
                       s1_recv.at[w, k, half], (target, row, col))
            )
        return out

    def second_copies(w, k, which):
        out = []
        for half, target, other in ((0, along, across), (1, across, along)):
            if which == 0:
                src, owner = source(w, k, half), dp
            else:
                src, owner = place(w, order[k], other, half), other
            out.append(
                remote(src, place(w, order[k], owner, half), s2_send.at[w, k, which, half],
                       s2_recv.at[w, k, which, half], (target, row, col))
            )
        return out

    def onward(w, k):
        if k > 0:
            block = place(w, order[k], dp)
            pltpu.make_async_copy(block, block, z_recv.at[w, order[k]]).wait()
        for cond, copy in line_copies(w, k):
            if cond is None:
                copy.start()
            else:
                pl.when(cond)(copy.start)

    def sideways(w, k):
        for copy in first_copies(w, k) + second_copies(w, k, 0):
            copy.start()

    def arrived(w, k):
        onward(w, k)
        sideways(w, k)

    def passed(w, k):
        for copy in first_copies(w, k):
            copy.wait_recv()
        for copy in second_copies(w, k, 1):
            copy.start()

    def finished(w):
        for k in range(ROWS):
            for which in range(2):
                for copy in second_copies(w, k, which):
                    copy.wait_recv()

    def drained(w, k):
        for cond, copy in line_copies(w, k):
            if cond is None:
                copy.wait_send()
            else:
                pl.when(cond)(copy.wait_send)
        for copy in first_copies(w, k) + second_copies(w, k, 0) + second_copies(w, k, 1):
            copy.wait_send()

    def home(w):
        return pltpu.make_async_copy(own[w], place(w, row, dp), l_sem.at[w])

    def begin(w):
        loads[w].wait()
        own[w][...] = stage[w][...].astype(BF)
        home(w).start()

    small_home = pltpu.make_async_copy(small_ref, smalls.at[me], l_sem.at[N_W])
    kept = []

    def keep(src, dst):
        copy = pltpu.make_async_copy(src, dst, l_sem.at[N_W + 1 + len(kept)])
        copy.start()
        kept.append(copy)

    def smalls_start():
        small_home.start()
        for step in range(1, ROWS * DPS):
            small_copy(step).start()

    def norm(served):
        small_home.wait()
        for step in range(1, ROWS * DPS):
            small_copy(step).wait()
        read_gains(smalls, gains)
        if aligned:
            read_bias(smalls, bias_row, 9 + n_q // (DPS * 128), n_u // DPS)
        else:
            bias_row[...] = bias_in[...]
        branch[...] = jnp.zeros(branch.shape, F32)
        comb[...] = jnp.zeros(comb.shape, F32)
        token_finish(0)
        first, first_t = hidden.at[:, pl.ds(0, D)], hidden.at[:, pl.ds(D, D)]
        norm_stage(x_ref, gains, ((0, first, first_t), (2, second, second_t)), served)
        keep(x_ref, x_out)
        keep(smalls, smalls_out)
        keep(first, first_out)
        keep(first_t, first_t_out)

    def act(word):
        kind, rest = word[0], [int(d) for d in word[1:]]
        {
            "b": begin, "z": onward, "s": sideways, "p": passed, "t": token_start, "d": token_spread, "m": smalls_start,
        }[kind](*rest)

    def forward(served):
        home(UP).wait()
        finished(UP)
        for copy in kept[2:4]:
            copy.wait()

        def block(n, carry):
            cut = span(n * width, width, width)

            def body(j, carry):
                rows = span(j * 256, 256, 256)
                value, slant = gelu_parts(nn(second[rows, :], wu[:, cut]) + bias_row[0:1, cut])
                hidden[rows, cut] = value.astype(BF)
                slope[rows, cut] = slant
                return carry

            lax.fori_loop(0, SEQ_LEN // 256, body, 0)
            served(n)
            return carry

        lax.fori_loop(0, blocks, block, 0)

    def down_grads(served):
        token_finish(1)
        keep(c_ref, c_out)
        h = gp.shape[3]

        def block(n, carry):
            turned = hidden[:, span(n * width, width, width)].T
            if blocks == DPS:
                for half in range(2):
                    gp[n // 2, lax.rem(n, 2), half] = nn(turned[half * h : (half + 1) * h, :], c_ref[...]).astype(BF)
            else:
                gp[...] = nn(turned, c_ref[...]).astype(BF).reshape(2, 2, 2, h, D)
            served(n)
            return carry

        lax.fori_loop(0, blocks, block, 0)
        keep(gp, gp_out)

    def backward(served):
        home(DOWN).wait()
        finished(DOWN)
        sum_out[...] = jnp.zeros(sum_out.shape, F32)

        def block(n, carry):
            cut = span(n * width, width, width)

            def body(j, carry):
                rows = span(j * 256, 256, 256)
                grad = (nt(c_ref[rows, :], wp[cut, :]) * slope[rows, cut]).astype(BF)
                ghp[rows, :] = grad
                branch[rows, :] += nn(hidden[rows, cut], wp[cut, :])
                comb[rows, :] += nt(grad, wu[:, cut])
                sum_out[0:1, cut] += jnp.sum(grad.astype(F32), axis=0, keepdims=True)
                return carry

            for part_of in range(2):
                lax.fori_loop(2 * part_of, 2 * part_of + 2, body, 0)
                served(n, part_of, 3)

            def up_body(r, carry):
                value = nn(second_t[span(r * 256, 256, 256), :], ghp[...]).astype(BF)
                gu[r, :, :, :, :, cut] = value.reshape(2, 2, 2, 32, width)
                return carry

            lax.fori_loop(0, ROWS, up_body, 0)
            served(n, 2, 3)
            return carry

        lax.fori_loop(0, blocks, block, 0)

    loops = {"N": (8, norm), "P": (blocks, forward), "D": (blocks, down_grads), "B": (3 * blocks, backward)}
    plan = GATHER_PLAN
    if blocks != DPS:
        plan = [word for word in plan if word[0] not in loops]
        for kind in "NPDB":
            plan = plan + parts_of(kind, loops[kind][0])
    run(plan, loops, act)
    for src, dst in ((gu, gu_out), (branch, branch_out), (comb, comb_out)):
        keep(src, dst)
    for w in (QKV, DENSE):
        home(w).wait()
        finished(w)
    for w in range(N_W):
        for k in range(ROWS):
            drained(w, k)
    for kind in range(2):
        token_drain(kind)
    for copy in kept[:2] + kept[4:]:
        copy.wait()


def gather(tokens_in, cotangent, small, bias, weights, cols, aligned):
    wq, wu, wd, wp = weights
    n_q, n_u = wq.shape[1], wu.shape[1]
    att_width, h_p = wd.shape[0] * DPS, wp.shape[0]
    width = 512 if n_u == DPS * 512 else n_u
    any_spec = pl.BlockSpec(memory_space=pl.ANY)
    vmem = pl.BlockSpec(memory_space=pltpu.VMEM)
    shape = jax.ShapeDtypeStruct
    smalls = (ROWS * DPS,) + small.shape
    square = (SEQ_LEN, D)
    up_shape, down_shape = (ROWS, 2, 2, 2, 32, n_u), (2, 2, 2, h_p // 2, D)
    out_shape = [
        shape(square, BF), shape(square, BF), shape(smalls, F32), shape((D, n_q), BF), shape((att_width, D), BF),
        shape(square, BF), shape(square, BF), shape(up_shape, BF), shape(down_shape, BF), shape(square, F32),
        shape(square, F32), shape((1, n_u), F32),
    ]
    tok_col = tokens_in.shape[0]
    pieces = tok_col // (SEQ_LEN // cols)
    dma = pltpu.SemaphoreType.DMA
    buf = pltpu.VMEM
    scratch = [buf(w.shape, BF) for w in weights] + [buf(w.shape, F32) for w in weights]
    scratch += [
        buf(square, BF), buf(square, BF), buf(smalls, F32), buf((D, n_u), BF), buf((n_u, D), BF),
        buf((8, D), F32), buf((1, n_u), F32), buf(square, BF), buf(square, BF),
        buf((SEQ_LEN, max(n_u, 2 * D)), BF), buf((SEQ_LEN, n_u), F32), buf((SEQ_LEN, width), BF), buf(up_shape, BF), buf(down_shape, BF), buf(square, F32),
        buf(square, F32),
        dma((N_W, 5)), dma((N_W, 4)), dma((N_W, 4, 2)), dma((N_W, 4, 2)), dma((N_W, 4, 2, 2)), dma((N_W, 4, 2, 2)),
        dma((2, pieces)), dma((2, 4)), dma((2, cols - 1)), dma((2, cols - 1)),
        dma((ROWS * DPS - 1,)), dma((ROWS * DPS - 1,)), dma((N_W + 10,)),
    ]
    return pl.pallas_call(
        functools.partial(gather_kernel, cols, aligned),
        out_shape=out_shape,
        in_specs=[any_spec] * 3 + [vmem] + [any_spec] * 4,
        out_specs=[any_spec] * 11 + [vmem],
        scratch_shapes=scratch,
        compiler_params=pltpu.CompilerParams(collective_id=0, has_side_effects=True, vmem_limit_bytes=60 << 20),
    )(tokens_in, cotangent, small, bias, wq, wu, wd, wp)


SCATTER_PLAN = (
    "f0", "f1", "J0", "J1", "J2", "f2", "J3", "U", "H0", "H1", "H2", "H3", "H4", "H5", "g0", "H6", "H7", "H8",
    "H9", "H10", "g1", "f3", "H11", "H12", "H13", "H14", "H15", "h0", "H16", "H17", "g2", "h1", "H18", "H19", "f4",
    "H20", "g3", "H21", "q0", "H22", "H23", "H24", "h2", "H25", "H26", "H27", "g4", "H28", "f5", "q1", "r0", "H29",
    "h3", "H30", "H31", "h4", "q2", "T", "f6", "q3", "W0", "q4", "X", "f7", "G0", "G1", "G2", "g5", "W1", "G3",
    "f8", "h5", "g6", "g7", "r1", "h6", "f9", "W2", "u0", "q5", "u1", "g8", "r2", "h7", "Y", "W3", "h8", "g9",
    "q6", "f10", "r3", "u2", "f11", "v0", "h9", "r4", "g10", "q7", "u3", "q8", "v1", "h10", "r5", "g11", "v2",
    "h11", "q9", "r6", "u4", "q10", "u5", "r7", "r8", "v3", "r9", "q11", "v4", "r10", "u6", "u7", "u8", "u9",
    "u10", "r11", "u11",
)
PIECES = 12


def add_into(dst, src):
    shape = dst.shape
    outer, height = shape[:-2], shape[-2]
    step = min(32, height)
    per = height // step
    total = math.prod(outer) * per

    def body(i, carry):
        index, rest = [], i // per
        for size in reversed(outer):
            index.append(lax.rem(rest, size))
            rest = rest // size
        where = tuple(reversed(index)) + (span(lax.rem(i, per) * step, step, step),)
        dst[where] = (dst[where].astype(F32) + src[where].astype(F32)).astype(BF)
        return carry

    lax.fori_loop(0, total, body, 0, unroll=min(4, total))


def pieces_of(n_q, n_u, h_d, h_p):
    out = []

    def columns(w, n):
        size = 512 if n % 512 == 0 else n
        out.extend((w, start, size) for start in range(0, n, size))

    columns(UP, n_u)
    half = h_p // 2
    size = 64 if half % 64 == 0 else half
    out.extend((DOWN, start, size) for start in range(0, half, size))
    out.append((DENSE, 0, h_d // 2))
    columns(QKV, n_q)
    return out


def scatter_kernel(cols, aligned, pieces, *refs):
    n_p = len(pieces)
    (prefix_ref, smalls, angles, bias_in, sum_u, x_in, c_in, wq_in, wd_in, first_in, first_t_in, gu_in, gp_in, branch_in,
     comb_in) = refs[:15]
    (lo_out, gt_out, oq, ou, od, op, sm_out) = refs[15:22]
    (wq, wd, x_ref, c_ref, first, first_t, q_t, k_t, v_t, up_t, att_t, gm_t, grad_q, grad_k, grad_v) = refs[22:37]
    (gq, gd, att, branch, comb, branch_got, comb_got, gains, bias_row, out_bias, sm, sm_got, gain_sum, hidden_keys) = refs[37:51]
    mine_u, mine_p = refs[51:53], refs[53:55]
    base = 55

    def buffers(start):
        return [refs[start + 2 * i : start + 2 * i + 2] for i in range(n_p)]

    got1, got2, got_end, got_mid = [buffers(base + 2 * n_p * n) for n in range(4)]
    (l_sem, f_sem, s1_send, s1_recv, s2_send, s2_recv, e_send, e_recv, m_send, m_recv, b_send, b_recv, d_send, d_recv,
     t_send, t_recv, v_send, v_recv) = refs[base + 8 * n_p :]
    dp, row, col, across, along = places()
    x, y = lax.rem(dp, 2), dp // 2
    side, at = line_order(row)
    far_end = row // 2
    middle, end = side == 1, side == 0
    n_q, n_u = wq_in.shape[1], sum_u.shape[1]
    heads = q_t.shape[0]
    folded = small_room(n_q, n_u)[0]
    tok_col = lo_out.shape[0]
    part = SEQ_LEN // cols

    def load(src, dst, n):
        return pltpu.make_async_copy(src, dst, l_sem.at[n])

    loads = [load(first_in, first, 0), load(wq_in, wq, 1), load(wd_in, wd, 2), load(c_in, c_ref, 3), load(first_t_in, first_t, 4),
             load(branch_in, branch, 5), load(comb_in, comb, 6), load(x_in, x_ref, 7)]
    for one in loads:
        one.start()
    group = [(dp, lax.rem(row + step, ROWS), lax.rem(col + other, cols)) for step in range(ROWS) for other in range(cols)]
    greet([(across, row, col), (along, row, col)] + group[1:])

    def view(i, half, other):
        w, start, size = pieces[i]
        if half == 0:
            place_y, place_x = (1 - y if other else y), slice(None)
        else:
            place_y, place_x = slice(None), (1 - x if other else x)
        cut = pl.ds(start, size)
        if w in (QKV, UP):
            if w == UP and not other:
                return mine_u[half].at[:, :, :, cut]
            return (gu_in if w == UP else gq).at[:, place_y, place_x, half, :, cut]
        if w == DOWN and not other:
            return mine_p[half].at[:, cut, :]
        return (gp_in if w == DOWN else gd).at[place_y, place_x, half, cut, :]

    def fetch(i, half):
        w, start, size = pieces[i]
        place_y, place_x = (y, slice(None)) if half == 0 else (slice(None), x)
        cut = pl.ds(start, size)
        src = gu_in.at[:, place_y, place_x, half, :, cut] if w == UP else gp_in.at[place_y, place_x, half, cut, :]
        return pltpu.make_async_copy(src, view(i, half, False), f_sem.at[i, half])

    def first_copy(i, half):
        target = along if half == 0 else across
        return remote(view(i, half, True), got1[i][half], s1_send.at[i, half], s1_recv.at[i, half], (target, row, col))

    def keep(i, half, other):
        which = x if half == 0 else y
        which = 1 - which if other else which
        kept = view(i, half, False)
        return kept.at[:, which] if pieces[i][0] in (QKV, UP) else kept.at[which]

    def second_copy(i, half):
        target = across if half == 0 else along
        return remote(keep(i, half, True), got2[i][half], s2_send.at[i, half], s2_recv.at[i, half], (target, row, col))

    def lines(i, ref, start, count):
        if pieces[i][0] in (QKV, UP):
            return ref.at[pl.ds(start, count)]
        return ref.at[:, span(start * 256, count * 256, 256)]

    def end_copy(i, half):
        src = lines(i, keep(i, half, False), 1 - far_end, 3)
        return remote(src, got_end[i][half], e_send.at[i, half], e_recv.at[i, half], (dp, at(1), col))

    def mid_copy(i, half):
        src = lines(i, keep(i, half, False), 2 * (1 - far_end), 2)
        return remote(src, got_mid[i][half], m_send.at[i, half], m_recv.at[i, half], (dp, at(2), col))

    def back_copy(i, half):
        src = lines(i, keep(i, half, False), at(0), 1)
        return remote(src, lines(i, got_mid[i][half], 0, 1), b_send.at[i, half], b_recv.at[i, half], (dp, at(0), col))

    def begin(i):
        for half in range(2):
            first_copy(i, half).start()
            if pieces[i][0] in (UP, DOWN):
                fetch(i, half).start()

    def stage_two(i):
        for half in range(2):
            if pieces[i][0] in (UP, DOWN):
                fetch(i, half).wait()
            first_copy(i, half).wait_recv()
            add_into(view(i, half, False), got1[i][half])
            second_copy(i, half).start()

    def stage_three(i):
        for half in range(2):
            second_copy(i, half).wait_recv()
            add_into(keep(i, half, False), got2[i][half])

            @pl.when(end)
            def _():
                end_copy(i, half).start()

    def stage_four(i):
        @pl.when(middle)
        def _():
            for half in range(2):
                end_copy(i, half).wait_recv()
                add_into(lines(i, keep(i, half, False), 2 * (1 - far_end), 2), lines(i, got_end[i][half], 1 - far_end, 2))
                mid_copy(i, half).start()

    def stage_five(i):
        @pl.when(middle)
        def _():
            for half in range(2):
                mid_copy(i, half).wait_recv()
                add_into(lines(i, keep(i, half, False), at(0), 1), lines(i, got_mid[i][half], far_end, 1))
                back_copy(i, half).start()

    def stage_six(i):
        w, start, size = pieces[i]
        out = (oq, ou, od, op)[w]
        for half in range(2):
            mine = lines(i, keep(i, half, False), row, 1)

            def total(others):
                if w in (QKV, UP):
                    value = mine[0].astype(F32)
                    for other in others:
                        value = value + other[0].astype(F32)
                    out[half, :, pl.ds(start, size)] = value
                else:
                    value = mine[...].astype(F32)
                    for other in others:
                        value = value + other[...].astype(F32)
                    out[half, pl.ds(start, size), :] = value

            @pl.when(end)
            def _():
                back_copy(i, half).wait_recv()
                total([lines(i, got_mid[i][half], 0, 1)])

            @pl.when(middle)
            def _():
                total([lines(i, got_end[i][half], 2 * far_end, 1), lines(i, got_mid[i][half], 1 - far_end, 1)])

    def drain(i):
        for half in range(2):
            first_copy(i, half).wait_send()
            second_copy(i, half).wait_send()

            @pl.when(end)
            def _():
                end_copy(i, half).wait_send()

            @pl.when(middle)
            def _():
                mid_copy(i, half).wait_send()
                back_copy(i, half).wait_send()

    def part_rows(piece):
        return span(piece * part, part, part)

    def col_copy(kind, n):
        other = lax.rem(col + n, cols)
        src = (branch, comb)[kind].at[part_rows(other), :]
        dst = (branch_got, comb_got)[kind].at[n - 1]
        return remote(src, dst, d_send.at[kind, n - 1], d_recv.at[kind, n - 1], (dp, row, other))

    start = row * SEQ_LEN + col * part
    owner, offset = start // tok_col, lax.rem(start, tok_col)

    def out_copy(kind, r):
        src = first.at[pl.ds(kind * part, part), span(r * 256, 256, 256)]
        dst = (lo_out, gt_out)[kind].at[span(offset, part, part), :]
        recv = t_recv.at[kind, offset // part]
        here = jnp.logical_and(row == r, owner == col)
        far = remote(src, dst, t_send.at[kind, r], recv, (dp, r, owner))
        return here, far, pltpu.make_async_copy(src, dst, recv)

    def out_start(kind):
        for r in (at(1 - side), at(2), at(3), row):
            here, far, near = out_copy(kind, r)
            pl.when(jnp.logical_not(here))(far.start)
            pl.when(here)(near.start)

    def out_finish(kind):
        for r in range(ROWS):
            here, far, near = out_copy(kind, r)
            pl.when(jnp.logical_not(here))(far.wait_send)
        out = (lo_out, gt_out)[kind]
        for n in range(tok_col // part):
            block = out.at[pl.ds(n * part, part), :]
            pltpu.make_async_copy(block, block, t_recv.at[kind, n]).wait()

    height = min(128, part)

    def finish_rows(kind):
        for n in range(1, cols):
            col_copy(kind, n).wait_recv()

        def body(i, carry):
            here = span(i * height, height, height)
            rows = span(col * part + i * height, height, height)
            value = (branch, comb)[kind][rows, :]
            for n in range(1, cols):
                value = value + (branch_got, comb_got)[kind][n - 1, here, :]
            wide = x_ref[rows, :].astype(F32)
            if kind == 0:
                value = wide + value + out_bias[0:1, :]
            else:
                normed, scale_inv = norm_rows(wide)
                mean = jnp.mean(value, axis=1, keepdims=True)
                cross = jnp.mean(value * normed, axis=1, keepdims=True)
                value = c_ref[rows, :].astype(F32) + scale_inv * (value - mean - normed * cross)
            first[span(kind * part + i * height, height, height), :] = value.astype(BF)
            return carry

        lax.fori_loop(0, part // height, body, 0)

    def small_copy(n):
        if n < 2:
            return remote(sm.at[n], sm_got.at[n], v_send.at[n], v_recv.at[n], ((across, along)[n], row, col))
        if n < 5:
            target = (dp, lax.rem(row + n - 1, ROWS), col)
            return remote(sm.at[2], sm_got.at[n], v_send.at[n], v_recv.at[n], target)
        target = (dp, row, lax.rem(col + n - 4, cols))
        return remote(sm.at[3], sm_got.at[n], v_send.at[n], v_recv.at[n], target)

    def small_step(n):
        if n > 0:
            waits = ((0,), (1,), (2, 3, 4), tuple(range(5, 4 + cols)))[n - 1]
            for m in waits:
                small_copy(m).wait_recv()
            value = sm[n - 1]
            if n < 4:
                for m in waits:
                    value = value + sm_got[m]
                sm[n] = value
            else:
                sm_out[...] = value
                value = value[0:4, 0:D]
                for m in waits:
                    value = value + sm_got[m, 0:4, 0:D]
                sm_out[0:4, 0:D] = value
        for m in ((0,), (1,), (2, 3, 4), tuple(range(5, 4 + cols)), ())[n]:
            small_copy(m).start()

    def project(served):
        read_gains(smalls, gains)
        lanes = lax.broadcasted_iota(jnp.int32, (1, 128), 1)
        for r in range(ROWS):
            for d in range(0, DPS, 2):
                both = [rounded(smalls[r * DPS + d + n, 8:9, :]) for n in range(2)]
                both = [value + pltpu.roll(value, 64, 1) for value in both]
                out_bias[0:1, pl.ds(r * 256 + d * 64, 128)] = jnp.where(lanes < 64, both[0], both[1])
        if aligned:
            read_bias(smalls, bias_row, 9, n_q // DPS)
        else:
            bias_row[...] = bias_in[...]
        sm[0] = jnp.zeros(sm.shape[1:], F32)
        put_up(sm.at[0], sum_u[...], folded)
        loads[0].wait()
        loads[1].wait()
        project_stage(wq, first, bias_row, angles, q_t, k_t, v_t, heads, served)

    def upstream():
        loads[2].wait()
        loads[3].wait()
        upstream_stage(wd, c_ref, up_t, heads)

    def attended():
        group_h = min(heads, 4)

        def turn_body(i, carry):
            block = att_t[pl.ds(i * group_h, group_h)].reshape(group_h * HD, SEQ_LEN)
            spot = pl.ds(0, group_h * HD) if heads == group_h else span(i * group_h * HD, group_h * HD, 128)
            att[:, spot] = block.T
            return carry

        lax.fori_loop(0, heads // group_h, turn_body, 0)
        loads[5].wait()

        def out_body(j, carry):
            rows = span(j * 256, 256, 256)
            branch[rows, :] += nn(att[rows, :], wd[...])
            return carry

        lax.fori_loop(0, SEQ_LEN // 256, out_body, 0)
        for n in range(1, cols):
            col_copy(0, n).start()

    def weight_grads(n):
        if n == 0:
            all_heads = att_t[...].reshape(heads * HD, SEQ_LEN)
            gd[...] = nn(all_heads, c_ref[...]).astype(BF).reshape(gd.shape)
            return
        if n == 1:
            loads[4].wait()
        wide = min(512, n_q)
        cut = pl.ds((n - 1) * wide, wide)

        def qkv_body(r, carry):
            rows = span(r * 256, 256, 256)
            gq[r, :, :, :, :, cut] = nt(first_t[rows, :], gm_t[cut, :]).astype(BF).reshape(2, 2, 2, 32, wide)
            return carry

        lax.fori_loop(0, ROWS, qkv_body, 0)

    need_x = [loads[7]]

    def output_home():
        if len(need_x):
            need_x.pop().wait()
        finish_rows(0)
        out_start(0)

    def features(served):
        loads[6].wait()
        if len(need_x):
            need_x.pop().wait()
        for n in range(8):
            gain_sum[n : n + 1, :] = jnp.zeros((1, D), F32)

        def body(j, carry):
            rows = span(j * 256, 256, 256)
            grad = gm_t[:, rows].T
            grad_first = nt(grad, wq[...])
            grad_second = comb[rows, :]
            normed, ignored = norm_rows(x_ref[rows, :].astype(F32))
            for n, value in enumerate((normed * grad_first, grad_first, normed * grad_second, grad_second,
                                       c_ref[rows, :].astype(F32))):
                gain_sum[n : n + 1, :] += jnp.sum(value, axis=0, keepdims=True)
            add_qkv(sm.at[0], jnp.sum(grad.astype(F32), axis=0, keepdims=True), folded)
            comb[rows, :] = gains[0:1, :] * grad_first + gains[2:3, :] * grad_second
            served(j)
            return carry

        lax.fori_loop(0, SEQ_LEN // 256, body, 0)
        for n in range(1, cols):
            col_copy(1, n).start()
        sm[0, 0:5, 0:D] = gain_sum[0:5, :]

    def gradient_home():
        finish_rows(1)
        out_start(1)

    stages = {"f": begin, "g": stage_two, "h": stage_three, "q": stage_four, "r": stage_five, "u": stage_six}
    others = {"U": upstream, "T": attended, "X": output_home, "Y": gradient_home}

    def act(word):
        kind, rest = word[0], word[1:]
        if kind in others:
            others[kind]()
        elif kind == "W":
            weight_grads(int(rest))
        elif kind == "v":
            small_step(int(rest))
        else:
            stages[kind](int(rest))

    def attention(served):
        hide_stage(prefix_ref[0], hidden_keys)

        def head_body(h, carry):
            attend_head(h, hidden_keys, angles, q_t, k_t, v_t, up_t, att_t, gm_t, grad_q, grad_k, grad_v, served)
            return carry

        lax.fori_loop(0, heads, head_body, 0)

    loops = {
        "J": (heads // min(heads, 2), project), "H": (heads * (SEQ_LEN // 256), attention), "G": (SEQ_LEN // 256, features),
    }
    plan = SCATTER_PLAN
    if n_p != PIECES:
        late = [i for i in range(n_p) if pieces[i][0] in (QKV, DENSE)]
        plan = ["f%d" % i for i in range(n_p) if i not in late] + parts_of("J", loops["J"][0]) + ["U"]
        plan = plan + parts_of("H", loops["H"][0]) + ["T", "W0", "W1", "X"] + parts_of("G", loops["G"][0]) + ["Y"]
        plan = plan + ["f%d" % i for i in late] + [s + str(i) for s in "ghqru" for i in range(n_p)] + parts_of("v", 5)
    run(plan, loops, act)
    for i in range(n_p):
        drain(i)
    for kind in range(2):
        out_finish(kind)
    for n in range(1, cols):
        for kind in range(2):
            col_copy(kind, n).wait_send()
    for n in range(4 + cols):
        small_copy(n).wait_send()


def scatter(prefix_len, smalls, angles, bias, sum_u, own_x, own_cot, wq, wd, first, first_t, gu, gp, branch, comb, cols, aligned,
            tok_col):
    any_spec = pl.BlockSpec(memory_space=pl.ANY)
    vmem = pl.BlockSpec(memory_space=pltpu.VMEM)
    smem = pl.BlockSpec(memory_space=pltpu.SMEM)
    dma = pltpu.SemaphoreType.DMA
    buf = pltpu.VMEM
    shape = jax.ShapeDtypeStruct
    n_q, n_u = wq.shape[1], sum_u.shape[1]
    heads = n_q // 192
    h_d, h_p = wd.shape[0] // DPS, 2 * gp.shape[3]
    pieces = pieces_of(n_q, n_u, h_d, h_p)
    n_p = len(pieces)
    part = SEQ_LEN // cols
    line = small_room(n_q, n_u)[1]
    square = (SEQ_LEN, D)
    turned = buf((heads, HD, SEQ_LEN), BF)
    scratch = [
        buf((D, n_q), BF), buf(wd.shape, BF), buf(square, BF), buf(square, BF), buf(square, BF), buf(square, BF),
        turned, turned, turned, turned, turned, buf((n_q, SEQ_LEN), BF),
        buf((HD, SEQ_LEN), F32), buf((HD, SEQ_LEN), F32), buf((HD, SEQ_LEN), F32),
        buf((ROWS, 2, 2, 2, 32, n_q), BF), buf((2, 2, 2, h_d // 2, D), BF), buf((SEQ_LEN, heads * HD), BF), buf(square, F32), buf(square, F32),
        buf((cols - 1, part, D), F32), buf((cols - 1, part, D), F32),
        buf((8, D), F32), buf((1, n_q), F32), buf((1, D), F32), buf((4, 8, line), F32), buf((4 + cols, 8, line), F32),
        buf((8, D), F32), buf((1280, 256), F32),
    ]
    scratch += [buf((ROWS, 2, 32, n_u), BF)] * 2 + [buf((2, h_p // 2, D), BF)] * 2
    for lead, count in (((ROWS, 2), None), ((ROWS,), None), ((3,), 3), ((2,), 2)):
        for w, start, size in pieces:
            if w in (QKV, UP):
                one = lead + (32, size)
            elif count is None:
                one = ((2,) if len(lead) == 2 else ()) + (size, D)
            else:
                one = (size, 256 * count)
            scratch += [buf(one, BF)] * 2
    scratch += [
        dma((8,)), dma((n_p, 2)), dma((n_p, 2)), dma((n_p, 2)), dma((n_p, 2)), dma((n_p, 2)), dma((n_p, 2)), dma((n_p, 2)),
        dma((n_p, 2)), dma((n_p, 2)), dma((n_p, 2)), dma((n_p, 2)), dma((2, cols - 1)), dma((2, cols - 1)),
        dma((2, ROWS)), dma((2, tok_col // part)), dma((4 + cols,)), dma((4 + cols,)),
    ]
    return pl.pallas_call(
        functools.partial(scatter_kernel, cols, aligned, pieces),
        out_shape=[
            shape((tok_col, 256), BF), shape((tok_col, 256), BF), shape((2, 32, n_q), F32), shape((2, 32, n_u), F32),
            shape((2, h_d // 2, 256), F32), shape((2, h_p // 2, 256), F32), shape((8, line), F32),
        ],
        in_specs=[smem, vmem, vmem, vmem, vmem] + [any_spec] * 10,
        out_specs=[any_spec] * 2 + [vmem] * 5,
        scratch_shapes=scratch,
        compiler_params=pltpu.CompilerParams(collective_id=1, has_side_effects=True, vmem_limit_bytes=63 << 20),
    )(prefix_len, smalls, angles, bias, sum_u, own_x, own_cot, wq, wd, first, first_t, gu, gp, branch, comb)


def small_room(n_q, n_u):
    folded = n_q == D + 512 and n_u == 2 * D
    return folded, (D + 128 if folded else max(n_q, n_u, D))


def put_up(rows, value, folded):
    if not folded:
        rows[6:7, 0 : value.shape[1]] = value
        return
    rows[6:7, 0:D] = value[:, 0:D]
    rows[7:8, 0:D] = value[:, D:]


def add_qkv(rows, value, folded):
    if not folded:
        rows[5:6, 0 : value.shape[1]] += value
        return
    rows[5:6, 0:D] += value[:, 0:D]
    for n in range(4):
        rows[n : n + 1, D : D + 128] += value[:, D + 128 * n : D + 128 * (n + 1)]


def finish_kernel(*refs):
    whole_in, sums, whole_out, q_b, u_b, d_b, p_b, gains, rooms, sem = (
        refs[:6], refs[6], refs[7:13], *refs[13:17], refs[17:21], refs[21:27], refs[27]
    )
    q_row, u_row = refs[28], refs[29]
    arrive = [pltpu.make_async_copy(src, dst, sem.at[0, n]) for n, (src, dst) in enumerate(zip(whole_in, rooms))]
    leave = [pltpu.make_async_copy(src, dst, sem.at[1, n]) for n, (src, dst) in enumerate(zip(rooms, whole_out))]
    for copy in arrive:
        copy.start()
    dp, row = lax.axis_index("dp"), lax.axis_index("row")
    for n, gain in enumerate(gains):
        gain[...] = sums[n : n + 1, span(row * 256, 256, 256)].reshape(gain.shape)
    if sums.shape[1] == D + 128:
        q_row[:, 0:D] = sums[5:6, 0:D]
        for n in range(4):
            q_row[:, D + 128 * n : D + 128 * (n + 1)] = sums[n : n + 1, D : D + 128]
        u_row[:, 0:D] = sums[6:7, 0:D]
        u_row[:, D:] = sums[7:8, 0:D]
    else:
        q_row[...] = sums[5:6, 0 : q_row.shape[1]]
        u_row[...] = sums[6:7, 0 : u_row.shape[1]]
    for row_of, bias in ((q_row, q_b), (u_row, u_b)):
        size = bias.shape[0]
        bias[...] = row_of[0:1, span(dp * size, size, 128)].reshape(bias.shape)
    me = row * DPS + dp
    pair = sums[4:5, span((me // 2) * 128, 128, 128)]
    pair = jnp.where(lax.rem(me, 2) == 0, pair, pltpu.roll(pair, 64, 1))
    for bias in (d_b, p_b):
        bias[...] = pair[:, 0:64].reshape(bias.shape)
    for first, then in zip(arrive, leave):
        first.wait()
        then.start()
    for copy in leave:
        copy.wait()


def finish(whole, sums, n_qb, n_ub):
    any_spec = pl.BlockSpec(memory_space=pl.ANY)
    vmem = pl.BlockSpec(memory_space=pltpu.VMEM)
    shape = jax.ShapeDtypeStruct
    sizes = [n_qb, n_ub, 64, 64] + [256] * 4
    out = pl.pallas_call(
        finish_kernel,
        out_shape=[shape(a.shape, a.dtype) for a in whole] + [shape((size,), F32) for size in sizes],
        in_specs=[any_spec] * 6 + [vmem],
        out_specs=[any_spec] * 6 + [vmem] * 8,
        scratch_shapes=[pltpu.VMEM(a.shape, a.dtype) for a in whole] + [
            pltpu.SemaphoreType.DMA((2, 6)), pltpu.VMEM((1, n_qb * DPS), F32), pltpu.VMEM((1, n_ub * DPS), F32),
        ],
    )(*whole, sums)
    lo, gt, gq, gu, gd, gp, q_b, u_b, d_b, p_b, *gains = out
    return (lo, gt, gq, q_b, gu, u_b, gd, d_b, gp, p_b, *gains)


def angles_table():
    half_rot = ROT // 2
    rates = np.exp(np.arange(half_rot, dtype=np.float32) * np.float32(-2.0 * math.log(10000.0) / ROT))
    turned = rates.astype(np.float32)[:, None] * np.arange(SEQ_LEN, dtype=np.float32)[None, :]
    return np.concatenate([np.cos(turned), np.sin(turned)], axis=0).astype(np.float32)


def shards(cols, tokens_in, prefix_len, first_gain, first_shift, second_gain, second_shift, qkv_weight, qkv_bias,
           up_weight, up_bias, dense_weight, dense_bias, down_weight, down_bias, cotangent):
    tok_col = tokens_in.shape[0]
    n_q, n_u = qkv_weight.shape[1], up_weight.shape[1]

    n_qb, n_ub = qkv_bias.shape[0], up_bias.shape[0]
    aligned = n_qb % 128 == 0 and n_ub % 128 == 0
    small = jnp.concatenate((first_gain, first_shift, second_gain, second_shift, dense_bias, down_bias, qkv_bias, up_bias))
    size = -(-small.shape[0] // 1024) * 1024
    small = jnp.pad(small, (0, size - small.shape[0])).reshape(size // 128, 128)
    if aligned:
        q_bias = u_bias = small
    else:
        q_bias = lax.all_gather(rounded(qkv_bias), "dp", axis=0, tiled=True).reshape(1, n_q)
        u_bias = lax.all_gather(rounded(up_bias), "dp", axis=0, tiled=True).reshape(1, n_u)
    own_x, own_cot, smalls, wq, wd, first, first_t, gu, gp, branch, comb, sum_u = gather(
        tokens_in, cotangent, small, u_bias, (qkv_weight, up_weight, dense_weight, down_weight), cols, aligned
    )
    layer_out, grad_tokens, out_q, out_u, out_d, out_p, sums = scatter(
        prefix_len, smalls, jnp.asarray(angles_table()), q_bias, sum_u, own_x, own_cot, wq, wd, first, first_t, gu, gp, branch,
        comb, cols, aligned, tok_col
    )
    h_d, h_p = dense_weight.shape[0], down_weight.shape[0]
    whole = (
        layer_out, grad_tokens, out_q.reshape(64, n_q), out_u.reshape(64, n_u), out_d.reshape(h_d, 256), out_p.reshape(h_p, 256)
    )
    if aligned:
        return finish(whole, sums, n_qb, n_ub)
    dp, row = lax.axis_index("dp"), lax.axis_index("row")
    gain_sums = lax.dynamic_slice(sums, (0, row * 256), (4, 256))
    out_b = lax.dynamic_slice(sums, (4, (row * DPS + dp) * 64), (1, 64))[0]
    q_b = lax.dynamic_slice(sums, (5, dp * n_qb), (1, n_qb))[0]
    u_b = lax.dynamic_slice(sums, (6, dp * n_ub), (1, n_ub))[0]
    return (
        whole[0], whole[1], whole[2], q_b, whole[3], u_b, whole[4], out_b, whole[5], out_b,
        gain_sums[0], gain_sums[1], gain_sums[2], gain_sums[3],
    )


def solution(mesh):
    in_specs = (
        P(("dp", "col"), "row"), P(("dp", "row")), P("row"), P("row"), P("row"), P("row"),
        P(("row", "dp"), "col"), P(("col", "dp")), P(("row", "dp"), "col"), P(("col", "dp")),
        P(("col", "dp"), "row"), P(("row", "dp")), P(("col", "dp"), "row"), P(("row", "dp")),
        P(("dp", "col"), "row"),
    )
    out_specs = (
        P(("dp", "col"), "row"), P(("dp", "col"), "row"), P(("row", "dp"), "col"), P(("col", "dp")),
        P(("row", "dp"), "col"), P(("col", "dp")), P(("col", "dp"), "row"), P(("row", "dp")),
        P(("col", "dp"), "row"), P(("row", "dp")), P("row"), P("row"), P("row"), P("row"),
    )
    body = functools.partial(shards, mesh.shape["col"])
    return jax.shard_map(body, mesh=mesh, in_specs=in_specs, out_specs=out_specs, check_vma=False)
```
